128 devices in a mesh: grp: 8 (over y, core), sub: 16 (over z, x).
Axes of the slice: x: 4, y: 4, z: 4, core: 2. Of those that a mesh axis runs over, the one named last changes fastest.
Arguments:
- charges: bfloat16 [32, 1048576], P(None, ('grp', 'sub')), may hold values from -6 to 6
- column_basis: bfloat16 [4096, 64, 256], P(('grp', 'sub')), may hold values from -0.375 to 0.375
- row_basis: bfloat16 [4096, 64, 256], P(('grp', 'sub')), may hold values from -0.75 to 0.75
- local_up: bfloat16 [8064, 64, 64], P(('grp', 'sub')), may hold values from -0.5 to 0.5
- local_down: bfloat16 [8064, 64, 64], P(('grp', 'sub')), may hold values from -0.75 to 0.75
- local_far: int32 [8064, 8], P(('grp', 'sub')), may hold values from 0 to 4095, as said below
- local_coupling: bfloat16 [8064, 8, 64, 64], P(('grp', 'sub')), may hold values from -0.25 to 0.25
- upper_up: bfloat16 [112, 64, 64], P('grp'), may hold values from -0.5 to 0.5
- upper_down: bfloat16 [112, 64, 64], P('grp'), may hold values from -0.75 to 0.75
- upper_far: int32 [120, 8], P('grp'), may hold values from 0 to 63, as said below
- upper_coupling: bfloat16 [120, 8, 64, 64], P('grp'), may hold values from -0.25 to 0.25
- near_source: int32 [4096, 3], P(('grp', 'sub')), may hold values from 0 to 4095, as said below
- near_block: bfloat16 [4096, 3, 256, 256], P(('grp', 'sub')), may hold values from -0.21875 to 0.21875
Outputs:
- potential: bfloat16 [32, 1048576], P(None, ('grp', 'sub'))
The draws below stay inside these ranges and needn't reach their ends.
Inputs may be any that keep to these rules, and one draw needn't show every extreme that they name: `near_source`: the first near partner of every leaf is the leaf itself; every near partner of a leaf of device d (leaf i lies on d = i div 32) is a leaf of device d-1, d or d+1. `local_far`: each partner is a cluster of the same level, numbered across that level as in the tree step, of device d-1, d or d+1 when the cluster lies on device d. `upper_far`: each partner is a cluster of the same level, numbered across all groups as in the tree step.
All inputs are finite; a program needn't handle non-finite values.
Results may differ from the reference program's by a relative error of at most 0.025.
Values may be sent and summed in bfloat16 or wider, within the bound.
A program may use at most 128 MiB of HBM per device.

```python
import jax
import jax.numpy as jnp
from jax import lax

LEAF = 256
RANK = 64
RHS = 32
LEAF_DEV = 32
NEAR = 3
FAR = 8
LEAVES = 4096
POINTS = 1048576
LOCAL_ROWS = 8064
UPPER_ROWS = 120
UPPER_LINKS = 112
N_GRP = 8
N_SUB = 16


def draw_near_source(key, part):
    key = jax.random.fold_in(key, 11)
    devices = N_GRP * N_SUB
    leaf_ids = jnp.arange(LEAVES, dtype=jnp.int32)
    owner = leaf_ids // LEAF_DEV
    lowest = jnp.maximum(owner - 1, 0) * LEAF_DEV
    highest = jnp.minimum(owner + 2, devices) * LEAF_DEV
    spread = jax.random.randint(key, (LEAVES, NEAR), 0, 1 << 20, dtype=jnp.int32)
    picks = lowest[:, None] + spread % (highest - lowest)[:, None]
    return picks.at[:, 0].set(leaf_ids)


def draw_local_far(key, part):
    key = jax.random.fold_in(key, 23)
    devices = N_GRP * N_SUB
    width = 2 * LEAF_DEV - 1
    rows = jnp.arange(LOCAL_ROWS, dtype=jnp.int32)
    owner = rows // width
    within = rows % width
    clusters = jnp.ones_like(rows)
    for height in range(LEAF_DEV.bit_length()):
        amount = LEAF_DEV // 2 ** height
        offset = 2 * LEAF_DEV - 2 * amount
        inside = jnp.logical_and(within >= offset, within < offset + amount)
        clusters = jnp.where(inside, amount, clusters)
    lowest = jnp.maximum(owner - 1, 0) * clusters
    highest = jnp.minimum(owner + 2, devices) * clusters
    spread = jax.random.randint(key, (LOCAL_ROWS, FAR), 0, 1 << 20, dtype=jnp.int32)
    picks = lowest[:, None] + spread % (highest - lowest)[:, None]
    picks = picks.at[0, 0].set(0)
    return picks.at[(devices - 1) * width + LEAF_DEV - 1, 0].set(LEAVES - 1)


def draw_upper_far(key, part):
    key = jax.random.fold_in(key, 37)
    width = N_SUB - 1
    rows = jnp.arange(UPPER_ROWS, dtype=jnp.int32)
    within = rows % width
    clusters = jnp.ones_like(rows)
    for height in range(1, N_SUB.bit_length()):
        amount = N_SUB // 2 ** height
        offset = N_SUB - 2 * amount
        inside = jnp.logical_and(within >= offset, within < offset + amount)
        clusters = jnp.where(inside, amount, clusters)
    spread = jax.random.randint(key, (UPPER_ROWS, FAR), 0, 1 << 20, dtype=jnp.int32)
    picks = spread % (N_GRP * clusters)[:, None]
    picks = picks.at[0, 0].set(0)
    return picks.at[0, 1].set(N_GRP * N_SUB // 2 - 1)


def level_of(stream_key, shape, cuts, smallest, largest):
    def one(axis_at, shards_of):
        steps = jax.random.uniform(jax.random.fold_in(jax.random.fold_in(stream_key, 6), axis_at), (shards_of,), jnp.float32, smallest / len(cuts), largest / len(cuts))
        return jnp.repeat(jnp.exp(steps), shape[axis_at] // shards_of).reshape((-1,) + (1,) * (len(shape) - axis_at - 1))

    gain = one(*cuts[0])
    for cut in cuts[1:]:
        gain = gain * one(*cut)
    return gain


def bell_draw(rng, shape, deviation, bound, shards=(), kind=jnp.bfloat16):
    drawn = jax.random.normal(rng, shape, jnp.float32) * deviation
    if len(shards) > 0:
        drawn = level_of(rng, shape, shards, -0.22, 0.18) * drawn
    return jnp.clip(drawn, min=-bound, max=bound).astype(kind)


def setup_inputs(seed: int = 0) -> dict:
    keys = jax.random.split(jax.random.key(seed), 14)
    return {
        "charges": bell_draw(keys[0], (RHS, POINTS), 1.0, 6.0, ((1, 128),)),
        "column_basis": bell_draw(keys[1], (LEAVES, RANK, LEAF), LEAF ** -0.5, 0.375, ((0, 128),)),
        "row_basis": bell_draw(keys[2], (LEAVES, RANK, LEAF), RANK ** -0.5, 0.75, ((0, 128),)),
        "local_up": bell_draw(keys[3], (LOCAL_ROWS, RANK, RANK), (2 * RANK) ** -0.5, 0.5, ((0, 128),)),
        "local_down": bell_draw(keys[4], (LOCAL_ROWS, RANK, RANK), RANK ** -0.5, 0.75, ((0, 128),)),
        "local_far": draw_local_far(jax.random.fold_in(keys[13], 71), 0),
        "local_coupling": bell_draw(keys[6], (LOCAL_ROWS, FAR, RANK, RANK), (RANK * FAR) ** -0.5, 0.25, ((0, 128),)),
        "upper_up": bell_draw(keys[7], (UPPER_LINKS, RANK, RANK), (2 * RANK) ** -0.5, 0.5, ((0, 8),)),
        "upper_down": bell_draw(keys[8], (UPPER_LINKS, RANK, RANK), RANK ** -0.5, 0.75, ((0, 8),)),
        "upper_far": draw_upper_far(jax.random.fold_in(keys[13], 71), 0),
        "upper_coupling": bell_draw(keys[10], (UPPER_ROWS, FAR, RANK, RANK), (RANK * FAR) ** -0.5, 0.25, ((0, 8),)),
        "near_source": draw_near_source(jax.random.fold_in(keys[13], 71), 0),
        "near_block": bell_draw(keys[12], (LEAVES, NEAR, LEAF, LEAF), (LEAF * NEAR) ** -0.5, 0.21875, ((0, 128),)),
    }


def local_slice(stacked, height):
    amount = LEAF_DEV // 2 ** height
    offset = 2 * LEAF_DEV - 2 * amount
    devices = N_GRP * N_SUB
    blocks = stacked.reshape((devices, 2 * LEAF_DEV - 1) + stacked.shape[1:])
    return blocks[:, offset:offset + amount].reshape((devices * amount,) + stacked.shape[1:])


def upper_slice(stacked, height, width):
    amount = N_SUB // 2 ** height
    offset = N_SUB - 2 * amount
    blocks = stacked.reshape((N_GRP, width) + stacked.shape[1:])
    return blocks[:, offset:offset + amount].reshape((N_GRP * amount,) + stacked.shape[1:])


def lift_pairs(transfer, children):
    terms = jnp.einsum('jab,jar->jbr', transfer.astype(jnp.float32), children.astype(jnp.float32))
    paired = terms.reshape((terms.shape[0] // 2, 2) + terms.shape[1:])
    return jnp.sum(paired, axis=1).astype(jnp.bfloat16)


def couple(coupling, partners, source):
    picked = source[partners].astype(jnp.float32)
    return jnp.einsum('tfab,tfbr->tar', coupling.astype(jnp.float32), picked)


def descend(transfer, parents, far_terms):
    spread = jnp.repeat(parents, 2, axis=0).astype(jnp.float32)
    product = jnp.einsum('jab,jbr->jar', transfer.astype(jnp.float32), spread)
    return (far_terms + product).astype(jnp.bfloat16)


def reference(charges, column_basis, row_basis, local_up, local_down, local_far, local_coupling, upper_up, upper_down, upper_far, upper_coupling, near_source, near_block):
    levels = LEAF_DEV.bit_length() - 1
    upper_levels = N_SUB.bit_length() - 1
    devices = N_GRP * N_SUB
    leaves = charges.reshape((RHS, LEAVES, LEAF))
    moments = [jnp.einsum('ika,ria->ikr', column_basis.astype(jnp.float32), leaves.astype(jnp.float32)).astype(jnp.bfloat16)]
    for height in range(1, levels + 1):
        moments.append(lift_pairs(local_slice(local_up, height - 1), moments[-1]))
    for height in range(1, upper_levels + 1):
        if height == 1:
            transfer = local_slice(local_up, levels)
        else:
            transfer = upper_slice(upper_up, height - 1, N_SUB - 2)
        moments.append(lift_pairs(transfer, moments[-1]))
    far_terms = []
    for height in range(levels + 1):
        far_terms.append(couple(local_slice(local_coupling, height), local_slice(local_far, height), moments[height]))
    for height in range(1, upper_levels + 1):
        far_terms.append(couple(upper_slice(upper_coupling, height, N_SUB - 1), upper_slice(upper_far, height, N_SUB - 1), moments[levels + height]))
    summit = levels + upper_levels
    current = far_terms[summit].astype(jnp.bfloat16)
    for height in range(summit - 1, -1, -1):
        if height > levels:
            transfer = upper_slice(upper_down, height - levels, N_SUB - 2)
        else:
            transfer = local_slice(local_down, height)
        current = descend(transfer, current, far_terms[height])

    def one_device(pieces):
        sources, blocks = pieces
        picked = leaves[:, sources].astype(jnp.float32)
        return jnp.einsum('inab,rinb->ria', blocks.astype(jnp.float32), picked)

    near_terms = lax.map(one_device, (near_source.reshape((devices, LEAF_DEV, NEAR)), near_block.reshape((devices, LEAF_DEV, NEAR, LEAF, LEAF))))
    near_terms = jnp.transpose(near_terms, (1, 0, 2, 3)).reshape((RHS, LEAVES, LEAF))
    far_out = jnp.einsum('ika,ikr->ria', row_basis.astype(jnp.float32), current.astype(jnp.float32))
    return (near_terms + far_out).astype(jnp.bfloat16).reshape((RHS, POINTS))
```

```python
import jax
import jax.numpy as jnp
from jax import lax
from jax.experimental import pallas as pl
from jax.experimental.pallas import tpu as pltpu
from jax.sharding import PartitionSpec as P

MESH = pl.DeviceIdType.MESH
BF = jnp.bfloat16
F32 = jnp.float32
RHS = 32
LEAVES = 32
LEAF = 256
RANK = 64
LEVELS = 5
COLS = LEAVES * LEAF
MROW = 64 * RANK
XCHUNKS = 16
XW = COLS // XCHUNKS
DEPTH = 3


def nt(a, b):
    return lax.dot_general(a, b, (((1,), (1,)), ((), ())), preferred_element_type=F32)


def nn(a, b):
    return lax.dot_general(a, b, (((1,), (0,)), ((), ())), preferred_element_type=F32)


def lanes(start, size):
    return pl.ds(pl.multiple_of(start, 128), size)


def loop(count, body, unroll):
    def step(i, carry):
        body(i)
        return carry

    lax.fori_loop(0, count, step, 0, unroll=min(unroll, count))


def row_of(height):
    return 64 - 2 * (LEAVES >> height)


def kernel(
    charges,
    column_basis,
    row_basis,
    local_up,
    local_down,
    local_far,
    local_coupling,
    upper_up,
    upper_down,
    upper_far,
    upper_coupling,
    near_source,
    near_block,
    out,
    cx,
    xin,
    xw,
    cbv,
    rbv,
    upv,
    dnv,
    cpv,
    uuv,
    udv,
    ucv,
    nbv,
    mw,
    lo,
    hi,
    rx,
    rz,
    rg,
    acc,
    far,
    dloc,
    gall,
    ov,
    far_at,
    ufar_at,
    near_at,
    lsem,
    osem,
    xsend,
    xrecv,
    msend,
    mrecv,
    rxsend,
    rxrecv,
    rzsend,
    rzrecv,
    rgsend,
    rgrecv,
):
    g = lax.axis_index("grp")
    s = lax.axis_index("sub")
    d = g * 16 + s
    z = s // 4
    x = s % 4

    def place(e):
        return (e // 16, e % 16)

    right = place((d + 1) % 128)
    left = place((d + 127) % 128)
    by_x = [(g, z * 4 + (x + k) % 4) for k in range(1, 4)]
    by_z = [(g, ((z + k) % 4) * 4 + x) for k in range(1, 4)]
    by_g = [((g + k) % 8, s) for k in range(1, 8)]
    peers = [right, left] + by_x + by_z + by_g

    barrier = pltpu.get_barrier_semaphore()
    for peer in peers:
        pl.semaphore_signal(barrier, inc=1, device_id=peer, device_id_type=MESH)

    loads = []

    def load(src, dst):
        copy = pltpu.make_async_copy(src, dst, lsem.at[len(loads)])
        copy.start()
        loads.append(copy)
        return copy

    get_x = load(charges, cx)
    get_cb = [load(column_basis.at[pl.ds(8 * k, 8)], cbv.at[pl.ds(8 * k, 8)]) for k in range(4)]
    get_up = load(local_up, upv)
    get_at = [load(local_far, far_at), load(upper_far, ufar_at), load(near_source, near_at)]
    get_uu = load(upper_up, uuv)

    pl.semaphore_wait(barrier, len(peers))

    def send(src, dst, ssem, rsem, peer):
        copy = pltpu.make_async_remote_copy(
            src_ref=src, dst_ref=dst, send_sem=ssem, recv_sem=rsem, device_id=peer, device_id_type=MESH
        )
        copy.start()
        return copy

    sent = []

    def advance(count):
        for _ in range(count):
            k = len(sent)
            if k >= XCHUNKS:
                return
            if k >= DEPTH:
                for copy in sent[k - DEPTH]:
                    copy.wait_send()
            src = charges.at[:, pl.ds(k * XW, XW)]
            sent.append(
                [
                    send(src, xin.at[0, :, pl.ds(k * XW, XW)], xsend.at[0, k], xrecv.at[0, k], right),
                    send(src, xin.at[1, :, pl.ds(k * XW, XW)], xsend.at[1, k], xrecv.at[1, k], left),
                ]
            )

    advance(DEPTH)

    get_nb = [load(near_block.at[pl.ds(4 * k, 4)], nbv.at[pl.ds(4 * k, 4)]) for k in range(8)]
    get_dn = load(local_down, dnv)
    get_cp = [load(local_coupling.at[pl.ds(9 * k, 9)], cpv.at[pl.ds(9 * k, 9)]) for k in range(7)]
    get_ud = [
        load(upper_down.at[16 - (32 >> k) + s // 2**k], udv.at[k - 1]) for k in range(1, 4)
    ]
    get_uc = [
        load(upper_coupling.at[16 - (32 >> k) + s // 2**k], ucv.at[k - 1]) for k in range(1, 5)
    ]
    get_rb = load(row_basis, rbv)

    low = lax.broadcasted_iota(jnp.int32, (RHS, 128), 1) < 64

    get_x.wait()
    for k in range(4):
        get_cb[k].wait()

        def leaf_moments(i):
            at = 4 * k + i
            one, two = cx[:, lanes(512 * at, 256)], cx[:, lanes(512 * at + 256, 256)]
            xw[LEAVES + 2 * at] = one
            xw[LEAVES + 2 * at + 1] = two
            pair = jnp.concatenate([one, two], axis=0)
            both = nt(pair, cbv[pl.ds(2 * at, 2)].reshape(128, LEAF))
            mw[:, lanes(MROW + 128 * at, 128)] = jnp.where(low, both[:RHS], both[RHS:]).astype(BF)

        loop(4, leaf_moments, 4)

    def send_moments(k, start, size):
        src = mw.at[:, pl.ds(MROW + start, size)]
        return [
            send(src, mw.at[:, pl.ds(start, size)], msend.at[0, k], mrecv.at[0, k], right),
            send(src, mw.at[:, pl.ds(2 * MROW + start, size)], msend.at[1, k], mrecv.at[1, k], left),
        ]

    moved = [send_moments(0, 0, 2048)]

    get_up.wait()
    zero = jnp.zeros((RHS, RANK), F32)
    for height in range(1, LEVELS + 1):
        amount = LEAVES >> height
        base, child = row_of(height), row_of(height - 1)

        def lift(j):
            pair = mw[:, lanes(MROW + child * 64 + 128 * j, 128)]
            return nn(pair, upv[pl.ds(child + 2 * j, 2)].reshape(128, RANK))

        if amount == 1:
            root = lift(0)
            mw[:, pl.ds(MROW + base * 64, 128)] = jnp.concatenate([root, zero], axis=1).astype(BF)
        else:

            def lift_two(j):
                both = jnp.concatenate([lift(2 * j), lift(2 * j + 1)], axis=1)
                mw[:, lanes(MROW + base * 64 + 128 * j, 128)] = both.astype(BF)

            loop(amount // 2, lift_two, 4)
    moved.append(send_moments(1, 2048, 2048))

    lifted = nn(root.astype(BF), upv[62])
    rx[x] = jnp.where(low == (x < 2), jnp.concatenate([lifted, lifted], axis=1), 0.0).astype(BF)
    gone_x = [send(rx.at[x], rx.at[x], rxsend.at[k], rxrecv.at[k], p) for k, p in enumerate(by_x)]

    advance(1)
    get_at[2].wait()

    def near_own(i):
        acc[:, lanes(256 * i, 256)] = nt(xw[LEAVES + i], nbv[i, 0])

    for k in range(4):
        get_nb[k].wait()
        loop(4, lambda i: near_own(4 * k + i), 4)
        if k == 1:
            advance(1)

    get_uu.wait()
    for copy in gone_x:
        copy.wait_recv()
    first = (
        (rx[0].astype(F32) + rx[1].astype(F32)) + (rx[2].astype(F32) + rx[3].astype(F32))
    ).astype(BF)
    second = nn(first, uuv[pl.ds(2 * z, 2)].reshape(128, RANK))
    rz[z, :, 0:128] = first
    rz[z, :, 128:256] = jnp.where(
        low == (z % 2 == 0), jnp.concatenate([second, second], axis=1), 0.0
    ).astype(BF)
    gone_z = [send(rz.at[z], rz.at[z], rzsend.at[k], rzrecv.at[k], p) for k, p in enumerate(by_z)]

    advance(1)
    for k in range(4, 8):
        get_nb[k].wait()
        loop(4, lambda i: near_own(4 * k + i), 4)
        if k == 5:
            advance(1)

    for copy in gone_z:
        copy.wait_recv()
    for k in range(4):
        rg[g, k] = rz[k, :, 0:128]
    thirds = []
    for k in range(2):
        pair = (
            rz[2 * k, :, 128:256].astype(F32) + rz[2 * k + 1, :, 128:256].astype(F32)
        ).astype(BF)
        rg[g, 4 + k] = pair
        thirds.append(nn(pair, uuv[8 + 2 * k : 10 + 2 * k].reshape(128, RANK)))
    third = jnp.concatenate(thirds, axis=1).astype(BF)
    rg[g, 6] = third
    top = nn(third, uuv[12:14].reshape(128, RANK))
    rg[g, 7] = jnp.concatenate([top, zero], axis=1).astype(BF)
    gone_g = [send(rg.at[g], rg.at[g], rgsend.at[k], rgrecv.at[k], p) for k, p in enumerate(by_g)]

    advance(1)

    get_dn.wait()
    gall[pl.ds(62 * 64, 64)] = dnv[62]
    for height in range(LEVELS - 1, -1, -1):
        amount = LEAVES >> height
        base, parent = row_of(height), row_of(height + 1)

        def extend(j):
            pair = dnv[pl.ds(base + 2 * j, 2)].reshape(128, RANK)
            above = gall[pl.ds(pl.multiple_of((parent + j) * 64, 64), 64)]
            gall[pl.ds(pl.multiple_of((base + 2 * j) * 64, 128), 128)] = nn(pair, above).astype(BF)

        loop(amount // 2, extend, 4)
    for copy in get_ud:
        copy.wait()
    down1 = udv[0]
    down2 = nn(down1, udv[1]).astype(BF)
    down3 = nn(down2, udv[2]).astype(BF)
    advance(1)

    get_at[0].wait()
    for copy in get_cp:
        copy.wait()
    for pair_of in moved:
        for copy in pair_of:
            copy.wait_recv()
    blank = jnp.zeros((RHS, RANK), BF)

    def spread(i):
        pair = mw[:, lanes(128 * i, 128)]
        even, odd = pair[:, :64], pair[:, 64:]
        lo[2 * i] = jnp.concatenate([even, blank], axis=1)
        hi[2 * i] = jnp.concatenate([blank, even], axis=1)
        lo[2 * i + 1] = jnp.concatenate([odd, blank], axis=1)
        hi[2 * i + 1] = jnp.concatenate([blank, odd], axis=1)

    loop(96, spread, 4)
    advance(1)

    for height in range(LEVELS, -1, -1):
        amount = LEAVES >> height
        base = row_of(height)
        bits = LEVELS - height

        def couple(t):
            def at(f):
                q = far_at[f, t] - (d - 1) * amount
                return ((q >> bits) & 3) * 64 + base + (q & (amount - 1))

            total = None
            for q in range(2):
                moments = jnp.concatenate(
                    [lo[at(4 * q + 2 * j)] + hi[at(4 * q + 2 * j + 1)] for j in range(2)], axis=1
                )
                blocks = jnp.concatenate([cpv[t, 4 * q + j] for j in range(4)], axis=1)
                term = nt(moments, blocks)
                total = term if total is None else total + term
            return total

        if amount == 1:
            far[:, pl.ds(base * 64, 128)] = jnp.concatenate([couple(base), zero], axis=1)
        else:

            def couple_two(j):
                t = base + 2 * j
                far[:, lanes(base * 64 + 128 * j, 128)] = jnp.concatenate(
                    [couple(t), couple(t + 1)], axis=1
                )

            if amount == 32:
                for k in range(4):
                    loop(4, lambda j: couple_two(4 * k + j), 4)
                    advance(1)
            else:
                loop(amount // 2, couple_two, 4)
                if amount == 8 or amount == 16:
                    advance(1)

    dloc[:, pl.ds(62 * 64, 128)] = far[:, pl.ds(62 * 64, 128)].astype(BF)
    for height in range(LEVELS - 1, -1, -1):
        amount = LEAVES >> height
        base, parent = row_of(height), row_of(height + 1)

        def descend(at, above):
            pair = dnv[pl.ds(base + 2 * at, 2)].reshape(128, RANK)
            here = lanes(base * 64 + 128 * at, 128)
            total = far[:, here] + nt(above, pair)
            if height == 0:
                far[:, here] = total
            else:
                dloc[:, here] = total.astype(BF)

        if amount == 2:
            descend(0, dloc[:, pl.ds(62 * 64, 128)][:, :64])
        else:

            def descend_two(j):
                above = dloc[:, lanes(parent * 64 + 128 * j, 128)]
                descend(2 * j, above[:, :64])
                descend(2 * j + 1, above[:, 64:])

            loop(amount // 4, descend_two, 4)
    advance(XCHUNKS)

    get_at[1].wait()
    for copy in get_uc:
        copy.wait()
    for copy in gone_g:
        copy.wait_recv()
    terms = []
    for k in range(1, 5):
        amount = 16 >> k
        base = 16 - 2 * amount
        row = base + s // 2**k

        def pick(f):
            p = ufar_at[f, row]
            r = base + (p & (amount - 1))
            pair = rg[p >> (4 - k), r >> 1].astype(F32)
            turned = jnp.concatenate([pair[:, 64:], pair[:, :64]], axis=1)
            keep = (1 - (r + f) % 2).astype(F32)
            return pair * keep + turned * (1.0 - keep)

        total = None
        for q in range(2):
            moments = jnp.concatenate(
                [jnp.where(low, pick(4 * q + 2 * j), pick(4 * q + 2 * j + 1)) for j in range(2)], axis=1
            ).astype(BF)
            blocks = jnp.concatenate([ucv[k - 1, 4 * q + j] for j in range(4)], axis=1)
            term = nt(moments, blocks)
            total = term if total is None else total + term
        terms.append(total)
    parent = (
        terms[0]
        + nt(terms[1].astype(BF), down1)
        + nt(terms[2].astype(BF), down2)
        + nt(terms[3].astype(BF), down3)
    ).astype(BF)

    get_rb.wait()

    def expand(i):
        wide = lanes(128 * i, 128)
        path = gall[pl.ds(pl.multiple_of(128 * i, 128), 128)]
        both = far[:, wide] + nt(parent, path)
        split = jnp.concatenate(
            [jnp.where(low, both, 0.0), jnp.where(low, 0.0, both)], axis=0
        ).astype(BF)
        res = nn(split, rbv[pl.ds(2 * i, 2)].reshape(128, LEAF))
        acc[:, lanes(512 * i, 256)] += res[:RHS]
        acc[:, lanes(512 * i + 256, 256)] += res[RHS:]

    loop(16, expand, 4)

    for k, pair_of in enumerate(sent):
        for copy in pair_of:
            copy.wait_recv()
        for side in range(2):
            for i in range(XW // LEAF):
                at = k * (XW // LEAF) + i
                xw[2 * LEAVES * side + at] = xin[side, :, 256 * at : 256 * (at + 1)]

    put = []
    for k in range(4):

        def near_rest(j):
            i = 8 * k + j
            here = lanes(256 * i, 256)
            total = acc[:, here]
            for n in (1, 2):
                q = (near_at[n, i] - (d - 1) * LEAVES) & 127
                total = total + nt(xw[q], nbv[i, n])
            ov[:, here] = total.astype(BF)

        loop(8, near_rest, 8)
        part = pl.ds(2048 * k, 2048)
        copy = pltpu.make_async_copy(ov.at[:, part], out.at[:, part], osem.at[k])
        copy.start()
        put.append(copy)

    for copy in put:
        copy.wait()
    for pair_of in sent[XCHUNKS - DEPTH :]:
        for copy in pair_of:
            copy.wait_send()
    for pair_of in moved:
        for copy in pair_of:
            copy.wait_send()
    for copy in gone_x + gone_z + gone_g:
        copy.wait_send()


def on_device(
    charges,
    column_basis,
    row_basis,
    local_up,
    local_down,
    local_far,
    local_coupling,
    upper_up,
    upper_down,
    upper_far,
    upper_coupling,
    near_source,
    near_block,
):
    dma = pltpu.SemaphoreType.DMA
    vmem = pltpu.VMEM
    anywhere = pl.BlockSpec(memory_space=pl.ANY)
    return pl.pallas_call(
        kernel,
        out_shape=jax.ShapeDtypeStruct((RHS, COLS), BF),
        in_specs=[anywhere] * 13,
        out_specs=anywhere,
        scratch_shapes=[
            vmem((RHS, COLS), BF),
            vmem((2, RHS, COLS), BF),
            vmem((4 * LEAVES, RHS, LEAF), BF),
            vmem((LEAVES, RANK, LEAF), BF),
            vmem((LEAVES, RANK, LEAF), BF),
            vmem((63, RANK, RANK), BF),
            vmem((63, RANK, RANK), BF),
            vmem((63, 8, RANK, RANK), BF),
            vmem((14, RANK, RANK), BF),
            vmem((3, RANK, RANK), BF),
            vmem((4, 8, RANK, RANK), BF),
            vmem((LEAVES, 3, LEAF, LEAF), BF),
            vmem((RHS, 3 * MROW), BF),
            vmem((256, RHS, 128), BF),
            vmem((256, RHS, 128), BF),
            vmem((4, RHS, 128), BF),
            vmem((4, RHS, 256), BF),
            vmem((8, 8, RHS, 128), BF),
            vmem((RHS, COLS), F32),
            vmem((RHS, MROW), F32),
            vmem((RHS, MROW), BF),
            vmem((MROW, RANK), BF),
            vmem((RHS, COLS), BF),
            pltpu.SMEM((8, 63), jnp.int32),
            pltpu.SMEM((8, 15), jnp.int32),
            pltpu.SMEM((3, LEAVES), jnp.int32),
            dma((40,)),
            dma((4,)),
            dma((2, XCHUNKS)),
            dma((2, XCHUNKS)),
            dma((2, 2)),
            dma((2, 2)),
            dma((3,)),
            dma((3,)),
            dma((3,)),
            dma((3,)),
            dma((7,)),
            dma((7,)),
        ],
        compiler_params=pltpu.CompilerParams(
            collective_id=0, has_side_effects=True, vmem_limit_bytes=60 * 2**20
        ),
        name="h2_product",
    )(
        charges,
        column_basis,
        row_basis,
        local_up,
        local_down,
        local_far.T,
        local_coupling,
        upper_up,
        upper_down,
        upper_far.T,
        upper_coupling,
        near_source.T,
        near_block,
    )


def solution(mesh):
    both = ("grp", "sub")
    in_specs = (
        P(None, both),
        P(both, None, None),
        P(both, None, None),
        P(both, None, None),
        P(both, None, None),
        P(both, None),
        P(both, None, None, None),
        P("grp", None, None),
        P("grp", None, None),
        P("grp", None),
        P("grp", None, None, None),
        P(both, None),
        P(both, None, None, None),
    )
    return jax.shard_map(
        on_device, mesh=mesh, in_specs=in_specs, out_specs=P(None, both), check_vma=False
    )
```

```python
import jax
import jax.numpy as jnp
from jax import lax
from jax.experimental import pallas as pl
from jax.experimental.pallas import tpu as pltpu
from jax.sharding import PartitionSpec as P

MESH = pl.DeviceIdType.MESH
BF = jnp.bfloat16
F32 = jnp.float32
RHS = 32
LEAVES = 32
LEAF = 256
RANK = 64
LEVELS = 5
COLS = LEAVES * LEAF
XPARTS = ((0, 1024), (1024, 1024), (2048, 2048), (4096, 2048), (6144, 2048))
XFIRST = 2
OWN, REACH, TURN, FAR, REST, FINISH = 4, 16, 96, 16, 8, 16


def nt(a, b):
    return lax.dot_general(a, b, (((1,), (1,)), ((), ())), preferred_element_type=F32)


def nn(a, b):
    return lax.dot_general(a, b, (((1,), (0,)), ((), ())), preferred_element_type=F32)


def lanes(start, size):
    return pl.ds(pl.multiple_of(start, 128), size)


def loop(count, body, unroll):
    def step(i, carry):
        body(i)
        return carry

    lax.fori_loop(0, count, step, 0, unroll=min(unroll, count))


def batched(count, width, compute, store):
    width = min(width, count)

    def body(b):
        got = [compute(width * b + j) for j in range(width)]
        for j in range(width):
            store(width * b + j, got[j])

    loop(count // width, body, 1)


def row_of(height):
    return 64 - 2 * (LEAVES >> height)


def kernel(
    charges,
    column_basis,
    row_basis,
    local_up,
    local_down,
    local_far,
    local_coupling,
    upper_up,
    upper_down,
    upper_far,
    upper_coupling,
    near_source,
    near_block,
    out,
    cx,
    xin,
    xw,
    cbv,
    rbv,
    upv,
    dnv,
    cpv,
    uuv,
    udv,
    ucv,
    nbv,
    mv,
    rx,
    rz,
    rg,
    acc,
    far,
    dloc,
    path,
    qv,
    far_raw,
    far_row,
    far_at,
    ufar_at,
    near_at,
    lsem,
    xsend,
    xrecv,
    msend,
    mrecv,
    rxsend,
    rxrecv,
    rzsend,
    rzrecv,
    rgsend,
    rgrecv,
):
    g = lax.axis_index("grp")
    s = lax.axis_index("sub")
    d = g * 16 + s
    z = s // 4
    x = s % 4

    def place(e):
        return (e // 16, e % 16)

    sides = ((d < 127, place((d + 1) % 128)), (d > 0, place((d + 127) % 128)))
    by_x = [(g, z * 4 + (x + k) % 4) for k in range(1, 4)]
    by_z = [(g, ((z + k) % 4) * 4 + x) for k in range(1, 4)]
    by_g = [((g + k) % 8, s) for k in range(1, 8)]
    peers = by_x + by_z + by_g

    barrier = pltpu.get_barrier_semaphore()
    for peer in peers:
        pl.semaphore_signal(barrier, inc=1, device_id=peer, device_id_type=MESH)
    for there, peer in sides:

        @pl.when(there)
        def _():
            pl.semaphore_signal(barrier, inc=1, device_id=peer, device_id_type=MESH)

    loads = []

    def load(src, dst):
        copy = pltpu.make_async_copy(src, dst, lsem.at[len(loads)])
        copy.start()
        loads.append(copy)
        return copy

    get_x = [load(charges.at[:, pl.ds(4096 * k, 4096)], cx.at[:, pl.ds(4096 * k, 4096)]) for k in range(2)]
    get_cb = [load(column_basis.at[pl.ds(8 * k, 8)], cbv.at[pl.ds(8 * k, 8)]) for k in range(4)]
    get_up = load(local_up, upv)
    get_uu = load(upper_up, uuv)
    get_at = [load(local_far, far_raw), load(upper_far, ufar_at), load(near_source, near_at)]

    pl.semaphore_wait(barrier, len(peers) + (d < 127).astype(jnp.int32) + (d > 0).astype(jnp.int32))

    def remote(src, dst, ssem, rsem, peer):
        return pltpu.make_async_remote_copy(
            src_ref=src, dst_ref=dst, send_sem=ssem, recv_sem=rsem, device_id=peer, device_id_type=MESH
        )

    def send(src, dst, ssem, rsem, peer):
        copy = remote(src, dst, ssem, rsem, peer)
        copy.start()
        return copy

    def beside(src, dst, ssem, rsem):
        return [remote(src, dst(2 * k), ssem.at[k], rsem.at[k], peer) for k, (_, peer) in enumerate(sides)]

    def start(batches, straight=True, turning=True):
        for k, (there, _) in enumerate(sides):
            turns = x == 3 - 3 * k
            go = there
            if not turning:
                go = there & jnp.logical_not(turns)
            elif not straight:
                go = there & turns

            @pl.when(go)
            def _():
                for copies in batches:
                    copies[k].start()

    def arrive(copies):
        for (there, _), copy in zip((sides[1], sides[0]), copies):
            pl.when(there)(copy.wait_recv)

    def leave(copies):
        for (there, _), copy in zip(sides, copies):
            pl.when(there)(copy.wait_send)

    def charges_part(k):
        start, size = XPARTS[k]
        part = pl.ds(start, size)
        return beside(
            charges.at[:, part],
            lambda side: xin.at[side // 2, :, part],
            xsend.at[k],
            xrecv.at[k],
        )

    sent = [charges_part(k) for k in range(len(XPARTS))]
    start(sent[:XFIRST])

    get_ud = [
        load(upper_down.at[16 - (32 >> k) + s // 2**k], udv.at[k - 1]) for k in range(1, 4)
    ]
    get_uc = [
        load(upper_coupling.at[16 - (32 >> k) + s // 2**k], ucv.at[k - 1]) for k in range(1, 5)
    ]

    low = lax.broadcasted_iota(jnp.int32, (RHS, 128), 1) < 64

    for k in range(4):
        if k % 2 == 0:
            get_x[k // 2].wait()
        get_cb[k].wait()

        def leaf_moments(i):
            at = 4 * k + i
            one, two = cx[:, lanes(512 * at, 256)], cx[:, lanes(512 * at + 256, 256)]
            both = nt(jnp.concatenate([one, two], axis=0), cbv[pl.ds(2 * at, 2)].reshape(128, LEAF))
            return one, two, jnp.where(low, both[:RHS], both[RHS:]).astype(BF)

        def keep_moments(i, got):
            at = 4 * k + i
            xw[LEAVES + 2 * at] = got[0]
            xw[LEAVES + 2 * at + 1] = got[1]
            mv[32 + at] = got[2]

        batched(4, 4, leaf_moments, keep_moments)

    get_up.wait()
    zero = jnp.zeros((RHS, RANK), F32)
    for height in range(1, LEVELS + 1):
        amount = LEAVES >> height
        base, child = row_of(height), row_of(height - 1)

        def lift(j):
            return nn(mv[32 + child // 2 + j], upv[pl.ds(child + 2 * j, 2)].reshape(128, RANK))

        def lift_two(j):
            return jnp.concatenate([lift(2 * j), lift(2 * j + 1)], axis=1).astype(BF)

        def keep_two(j, got):
            mv[32 + base // 2 + j] = got

        if amount == 1:
            root = lift(0)
            mv[63] = jnp.concatenate([root, zero], axis=1).astype(BF)
        else:
            batched(amount // 2, 4, lift_two, keep_two)

    get_dn = load(local_down, dnv)
    get_nb = [load(near_block.at[pl.ds(4 * k, 4)], nbv.at[pl.ds(4 * k, 4)]) for k in range(8)]
    get_cp = [load(local_coupling.at[pl.ds(9 * k, 9)], cpv.at[pl.ds(9 * k, 9)]) for k in range(7)]
    get_rb = load(row_basis, rbv)

    lifted = nn(root.astype(BF), upv[62])
    rx[x] = jnp.where(low == (x < 2), jnp.concatenate([lifted, lifted], axis=1), 0.0).astype(BF)
    gone_x = [send(rx.at[x], rx.at[x], rxsend.at[k], rxrecv.at[k], p) for k, p in enumerate(by_x)]
    moved = [
        beside(
            mv.at[pl.ds(32 + 16 * k, 16)],
            lambda side: mv.at[pl.ds(32 * side + 16 * k, 16)],
            msend.at[k],
            mrecv.at[k],
        )
        for k in range(2)
    ]
    start(moved + sent[XFIRST:], turning=False)
    start(moved[:1], straight=False)

    get_at[0].wait()
    t = lax.broadcasted_iota(jnp.int32, (8, 63), 1)
    f = lax.broadcasted_iota(jnp.int32, (8, 63), 0)
    amount = jnp.full((8, 63), LEAVES, jnp.int32)
    for height in range(1, LEVELS + 1):
        amount = jnp.where(t < row_of(height), amount, LEAVES >> height)
    q = far_raw[...] - (d - 1) * amount
    window = (q >= amount).astype(jnp.int32) + (q >= 2 * amount).astype(jnp.int32)
    row = 64 - 2 * amount + (q & (amount - 1))
    far_row[...] = jnp.zeros((8, 64), jnp.int32)
    far_row[:, 0:63] = ((row + f) & 1) * 128 + window * 32 + (row >> 1)
    get_far = pltpu.make_async_copy(far_row, far_at, lsem.at[len(loads)])
    get_far.start()

    get_dn.wait()

    def extend_level(height):
        amount = LEAVES >> height
        base, parent = row_of(height), row_of(height + 1)

        def below(above, j):
            return nt(above, dnv[pl.ds(base + 2 * j, 2)].reshape(128, RANK)).astype(BF)

        if amount == 2:
            path[base // 2] = below(dnv[62].T, 0)
        else:

            def extend(j):
                above = path[parent // 2 + j]
                return below(above[:, :64], 2 * j), below(above[:, 64:], 2 * j + 1)

            def keep(j, got):
                path[base // 2 + 2 * j] = got[0]
                path[base // 2 + 2 * j + 1] = got[1]

            batched(amount // 4, 4, extend, keep)

    for height in range(LEVELS - 1, -1, -1):
        extend_level(height)

    get_uu.wait()
    for copy in gone_x:
        copy.wait_recv()
    first = (
        (rx[0].astype(F32) + rx[1].astype(F32)) + (rx[2].astype(F32) + rx[3].astype(F32))
    ).astype(BF)
    rz[z, 0] = first
    second = nn(first, uuv[pl.ds(2 * z, 2)].reshape(128, RANK))
    rz[z, 1] = jnp.where(low == (z % 2 == 0), jnp.concatenate([second, second], axis=1), 0.0).astype(BF)
    gone_z = [send(rz.at[z], rz.at[z], rzsend.at[k], rzrecv.at[k], p) for k, p in enumerate(by_z)]
    start(moved[1:], straight=False)

    def near_own(i):
        return nt(xw[LEAVES + i], nbv[i, 0])

    def keep_own(i, got):
        acc[:, lanes(256 * i, 256)] = got

    for k in range(4):
        get_nb[k].wait()
        batched(4, OWN, lambda i: near_own(4 * k + i), lambda i, got: keep_own(4 * k + i, got))

    for copy in gone_z:
        copy.wait_recv()
    for k in range(4):
        rg[g, k] = rz[k, 0]
    thirds = []
    for k in range(2):
        pair = (rz[2 * k, 1].astype(F32) + rz[2 * k + 1, 1].astype(F32)).astype(BF)
        rg[g, 4 + k] = pair
        thirds.append(nn(pair, uuv[8 + 2 * k : 10 + 2 * k].reshape(128, RANK)))
    third = jnp.concatenate(thirds, axis=1).astype(BF)
    rg[g, 6] = third
    top = nn(third, uuv[12:14].reshape(128, RANK))
    rg[g, 7] = jnp.concatenate([top, zero], axis=1).astype(BF)
    gone_g = [send(rg.at[g], rg.at[g], rgsend.at[k], rgrecv.at[k], p) for k, p in enumerate(by_g)]
    start(sent[XFIRST:], straight=False)

    for k in range(4, 8):
        get_nb[k].wait()
        batched(4, OWN, lambda i: near_own(4 * k + i), lambda i, got: keep_own(4 * k + i, got))

    get_rb.wait()

    def reach(i):
        pair = path[i]
        return nn(pair[:, :64], rbv[2 * i]).astype(BF), nn(pair[:, 64:], rbv[2 * i + 1]).astype(BF)

    def keep_reach(i, got):
        qv[:, lanes(512 * i, 256)] = got[0]
        qv[:, lanes(512 * i + 256, 256)] = got[1]

    batched(16, REACH, reach, keep_reach)
    for copy in get_ud:
        copy.wait()
    down1 = udv[0]
    down2 = nn(down1, udv[1]).astype(BF)
    down3 = nn(down2, udv[2]).astype(BF)

    for copies in moved:
        arrive(copies)

    def turn(i):
        pair = mv[i]
        return jnp.concatenate([pair[:, 64:], pair[:, :64]], axis=1)

    def keep_turn(i, got):
        mv[128 + i] = got

    batched(96, TURN, turn, keep_turn)
    get_far.wait()
    for copy in get_cp:
        copy.wait()

    def couple(t):
        total = None
        for q in range(2):
            moments = jnp.concatenate(
                [
                    jnp.where(low, mv[far_at[4 * q + 2 * j, t]], mv[far_at[4 * q + 2 * j + 1, t]])
                    for j in range(2)
                ],
                axis=1,
            )
            blocks = jnp.concatenate([cpv[t, 4 * q + j] for j in range(4)], axis=1)
            term = nt(moments, blocks)
            total = term if total is None else total + term
        return total

    def couple_two(j):
        return jnp.concatenate([couple(2 * j), couple(2 * j + 1)], axis=1)

    def keep_couple(j, got):
        far[j] = got

    batched(32, FAR, couple_two, keep_couple)

    dloc[31] = far[31].astype(BF)
    for height in range(LEVELS - 1, -1, -1):
        amount = LEAVES >> height
        base, parent = row_of(height), row_of(height + 1)

        def below(above, j):
            pair = dnv[pl.ds(base + 2 * j, 2)].reshape(128, RANK)
            return (far[base // 2 + j] + nt(above, pair)).astype(BF)

        if amount == 2:
            dloc[base // 2] = below(dloc[31][:, :64], 0)
        else:

            def descend(j):
                above = dloc[parent // 2 + j]
                return below(above[:, :64], 2 * j), below(above[:, 64:], 2 * j + 1)

            def keep_descend(j, got):
                dloc[base // 2 + 2 * j] = got[0]
                dloc[base // 2 + 2 * j + 1] = got[1]

            batched(amount // 4, 4, descend, keep_descend)

    def local(i):
        pair = dloc[i]
        return [
            acc[:, lanes(512 * i + 256 * k, 256)] + nn(pair[:, 64 * k : 64 * (k + 1)], rbv[2 * i + k])
            for k in range(2)
        ]

    def keep_rest(i, got):
        for k in range(2):
            acc[:, lanes(512 * i + 256 * k, 256)] = got[k]

    batched(16, 8, local, keep_rest)

    get_at[2].wait()
    for copies, (start, size) in zip(sent, XPARTS):
        arrive(copies)

        def window(i):
            part = lanes(start + LEAF * i, LEAF)
            return xin[0, :, part], xin[1, :, part]

        def keep_window(i, got):
            xw[start // LEAF + i] = got[0]
            xw[2 * LEAVES + start // LEAF + i] = got[1]

        batched(size // LEAF, 4, window, keep_window)

    def rest(i):
        totals = []
        for k in range(2):
            leaf = 2 * i + k
            total = acc[:, lanes(256 * leaf, 256)]
            for n in (1, 2):
                q = (near_at[n, leaf] - (d - 1) * LEAVES) & 127
                total = total + nt(xw[q], nbv[leaf, n])
            totals.append(total)
        return totals

    batched(16, REST, rest, keep_rest)

    get_at[1].wait()
    for copy in get_uc:
        copy.wait()
    for copy in gone_g:
        copy.wait_recv()
    terms = []
    for k in range(1, 5):
        amount = 16 >> k
        row = 16 - 2 * amount + s // 2**k

        def pick(f):
            p = ufar_at[f, row]
            group, j = p >> (4 - k), p & (amount - 1)
            pair = rg[group, (0, 4, 6, 7)[k - 1] + (j >> 1)]
            pair = pair.astype(F32)
            turned = jnp.concatenate([pair[:, 64:], pair[:, :64]], axis=1)
            keep = (1 - ((j + f) & 1)).astype(F32)
            return pair * keep + turned * (1.0 - keep)

        total = None
        for q in range(2):
            moments = jnp.concatenate(
                [jnp.where(low, pick(4 * q + 2 * j), pick(4 * q + 2 * j + 1)) for j in range(2)], axis=1
            ).astype(BF)
            blocks = jnp.concatenate([ucv[k - 1, 4 * q + j] for j in range(4)], axis=1)
            term = nt(moments, blocks)
            total = term if total is None else total + term
        terms.append(total)
    parent = (
        terms[0]
        + nt(terms[1].astype(BF), down1)
        + nt(terms[2].astype(BF), down2)
        + nt(terms[3].astype(BF), down3)
    ).astype(BF)

    def finish(i):
        part = lanes(512 * i, 512)
        return (acc[:, part] + nn(parent, qv[:, part])).astype(BF)

    def keep_finish(i, got):
        out[:, lanes(512 * i, 512)] = got

    batched(16, FINISH, finish, keep_finish)

    for copies in sent:
        leave(copies)
    for copies in moved:
        leave(copies)
    for copy in gone_x + gone_z + gone_g:
        copy.wait_send()


def on_device(
    charges,
    column_basis,
    row_basis,
    local_up,
    local_down,
    local_far,
    local_coupling,
    upper_up,
    upper_down,
    upper_far,
    upper_coupling,
    near_source,
    near_block,
):
    dma = pltpu.SemaphoreType.DMA
    vmem = pltpu.VMEM
    anywhere = pl.BlockSpec(memory_space=pl.ANY)
    return pl.pallas_call(
        kernel,
        out_shape=pltpu.VMEM((RHS, COLS), BF),
        in_specs=[anywhere] * 13,
        out_specs=pl.BlockSpec(memory_space=vmem),
        scratch_shapes=[
            vmem((RHS, COLS), BF),
            vmem((2, RHS, COLS), BF),
            vmem((4 * LEAVES, RHS, LEAF), BF),
            vmem((LEAVES, RANK, LEAF), BF),
            vmem((LEAVES, RANK, LEAF), BF),
            vmem((63, RANK, RANK), BF),
            vmem((63, RANK, RANK), BF),
            vmem((64, 8, RANK, RANK), BF),
            vmem((14, RANK, RANK), BF),
            vmem((3, RANK, RANK), BF),
            vmem((4, 8, RANK, RANK), BF),
            vmem((LEAVES, 3, LEAF, LEAF), BF),
            vmem((256, RHS, 128), BF),
            vmem((4, RHS, 128), BF),
            vmem((4, 2, RHS, 128), BF),
            vmem((8, 8, RHS, 128), BF),
            vmem((RHS, COLS), F32),
            vmem((32, RHS, 128), F32),
            vmem((32, RHS, 128), BF),
            vmem((32, RANK, 128), BF),
            vmem((RANK, COLS), BF),
            vmem((8, 63), jnp.int32),
            vmem((8, 64), jnp.int32),
            pltpu.SMEM((8, 64), jnp.int32),
            pltpu.SMEM((8, 15), jnp.int32),
            pltpu.SMEM((3, LEAVES), jnp.int32),
            dma((40,)),
            dma((len(XPARTS), 2)),
            dma((len(XPARTS), 2)),
            dma((2, 2)),
            dma((2, 2)),
            dma((3,)),
            dma((3,)),
            dma((3,)),
            dma((3,)),
            dma((7,)),
            dma((7,)),
        ],
        compiler_params=pltpu.CompilerParams(
            collective_id=0, has_side_effects=True, vmem_limit_bytes=60 * 2**20
        ),
        name="h2_product",
    )(
        charges,
        column_basis,
        row_basis,
        local_up,
        local_down,
        local_far.T,
        local_coupling,
        upper_up,
        upper_down,
        upper_far.T,
        upper_coupling,
        near_source.T,
        near_block,
    )


def solution(mesh):
    both = ("grp", "sub")
    in_specs = (
        P(None, both),
        P(both, None, None),
        P(both, None, None),
        P(both, None, None),
        P(both, None, None),
        P(both, None),
        P(both, None, None, None),
        P("grp", None, None),
        P("grp", None, None),
        P("grp", None),
        P("grp", None, None, None),
        P(both, None),
        P(both, None, None, None),
    )
    return jax.shard_map(
        on_device, mesh=mesh, in_specs=in_specs, out_specs=P(None, both), check_vma=False
    )
```

```python
import functools

import jax
import jax.numpy as jnp
from jax import lax
from jax.experimental import pallas as pl
from jax.experimental.pallas import tpu as pltpu
from jax.sharding import PartitionSpec as P

MESH = pl.DeviceIdType.MESH
BF = jnp.bfloat16
F32 = jnp.float32
RHS = 32
LEAVES = 32
LEAF = 256
RANK = 64
LEVELS = 5
COLS = LEAVES * LEAF
XPARTS = ((0, 1024), (1024, 1024), (2048, 2048), (4096, 2048), (6144, 2048))
XFIRST = 2
OWN, REACH, TURN, FAR, REST, FINISH = 4, 16, 96, 16, 8, 16


def nt(a, b):
    return lax.dot_general(a, b, (((1,), (1,)), ((), ())), preferred_element_type=F32)


def nn(a, b):
    return lax.dot_general(a, b, (((1,), (0,)), ((), ())), preferred_element_type=F32)


def lanes(start, size):
    return pl.ds(pl.multiple_of(start, 128), size)


def loop(count, body, unroll):
    def step(i, carry):
        body(i)
        return carry

    lax.fori_loop(0, count, step, 0, unroll=min(unroll, count))


def batched(count, width, compute, store):
    width = min(width, count)

    def body(b):
        got = [compute(width * b + j) for j in range(width)]
        for j in range(width):
            store(width * b + j, got[j])

    loop(count // width, body, 1)


def row_of(height):
    return 64 - 2 * (LEAVES >> height)


def kernel(
    charges,
    column_basis,
    row_basis,
    local_up,
    local_down,
    local_far,
    local_coupling,
    upper_up,
    upper_down,
    upper_far,
    upper_coupling,
    near_source,
    near_block,
    out,
    cx,
    xin,
    xw,
    cbv,
    rbv,
    upv,
    dnv,
    cpv,
    uuv,
    udv,
    ucv,
    nbv,
    mv,
    rx,
    rz,
    rg,
    pv,
    acc,
    far,
    dloc,
    path,
    qv,
    far_raw,
    far_row,
    far_at,
    ufar_at,
    near_at,
    lsem,
    xsend,
    xrecv,
    msend,
    mrecv,
    rxsend,
    rxrecv,
    rzsend,
    rzrecv,
    rgsend,
    rgrecv,
    psend,
    precv,
):
    g = lax.axis_index("grp")
    s = lax.axis_index("sub")
    d = g * 16 + s
    z = s // 4
    x = s % 4

    def place(e):
        return (e // 16, e % 16)

    sides = ((d < 127, place((d + 1) % 128)), (d > 0, place((d + 127) % 128)))
    inner = (x == 1) | (x == 2)
    outer = jnp.logical_not(inner)
    y, core = g // 2, g % 2
    middle = [(g, z * 4 + 1), (g, z * 4 + 2)]
    other = (g, z * 4 + 3 - x)
    helped = (g, z * 4 + 3 * (x // 2))
    by_z = [(g, ((z + k) % 4) * 4 + x) for k in range(1, 4)]
    by_y = [(((y + k) % 4) * 2 + core, s) for k in range(1, 4)]
    twin = (2 * y + 1 - core, s)

    barrier = pltpu.get_barrier_semaphore()

    def greet(peer):
        pl.semaphore_signal(barrier, inc=1, device_id=peer, device_id_type=MESH)

    for there, peer in sides:
        pl.when(there)(functools.partial(greet, peer))

    @pl.when(inner)
    def _():
        for peer in [other, (g, z * 4), (g, z * 4 + 3)] + by_z + by_y + [twin]:
            greet(peer)

    @pl.when(outer)
    def _():
        for peer in middle:
            greet(peer)

    loads = []

    def load(src, dst):
        copy = pltpu.make_async_copy(src, dst, lsem.at[len(loads)])
        copy.start()
        loads.append(copy)
        return copy

    get_x = [load(charges.at[:, pl.ds(4096 * k, 4096)], cx.at[:, pl.ds(4096 * k, 4096)]) for k in range(2)]
    get_cb = [load(column_basis.at[pl.ds(8 * k, 8)], cbv.at[pl.ds(8 * k, 8)]) for k in range(4)]
    get_up = load(local_up, upv)
    get_uu = load(upper_up, uuv)
    get_at = [load(local_far, far_raw), load(upper_far, ufar_at), load(near_source, near_at)]

    @pl.when(outer)
    def _():
        pl.semaphore_wait(barrier, 2 + (d < 127).astype(jnp.int32) + (d > 0).astype(jnp.int32))

    def remote(src, dst, ssem, rsem, peer):
        return pltpu.make_async_remote_copy(
            src_ref=src, dst_ref=dst, send_sem=ssem, recv_sem=rsem, device_id=peer, device_id_type=MESH
        )

    def send(src, dst, ssem, rsem, peer):
        copy = remote(src, dst, ssem, rsem, peer)
        copy.start()
        return copy

    def beside(src, dst, ssem, rsem):
        return [remote(src, dst(2 * k), ssem.at[k], rsem.at[k], peer) for k, (_, peer) in enumerate(sides)]

    def start(batches):
        for k, (there, _) in enumerate(sides):

            @pl.when(there)
            def _():
                for copies in batches:
                    copies[k].start()

    def arrive(copies):
        for (there, _), copy in zip((sides[1], sides[0]), copies):
            pl.when(there)(copy.wait_recv)

    def leave(copies):
        for (there, _), copy in zip(sides, copies):
            pl.when(there)(copy.wait_send)

    def charges_part(k):
        start, size = XPARTS[k]
        part = pl.ds(start, size)
        return beside(
            charges.at[:, part],
            lambda side: xin.at[side // 2, :, part],
            xsend.at[k],
            xrecv.at[k],
        )

    sent = [charges_part(k) for k in range(len(XPARTS))]
    pl.when(outer)(lambda: start(sent[:XFIRST]))

    get_ud = [
        load(upper_down.at[16 - (32 >> k) + s // 2**k], udv.at[k - 1]) for k in range(1, 4)
    ]
    get_uc = [
        load(upper_coupling.at[16 - (32 >> k) + s // 2**k], ucv.at[k - 1]) for k in range(1, 5)
    ]

    low = lax.broadcasted_iota(jnp.int32, (RHS, 128), 1) < 64

    for k in range(4):
        if k % 2 == 0:
            get_x[k // 2].wait()
        get_cb[k].wait()

        def leaf_moments(i):
            at = 4 * k + i
            one, two = cx[:, lanes(512 * at, 256)], cx[:, lanes(512 * at + 256, 256)]
            both = nt(jnp.concatenate([one, two], axis=0), cbv[pl.ds(2 * at, 2)].reshape(128, LEAF))
            return one, two, jnp.where(low, both[:RHS], both[RHS:]).astype(BF)

        def keep_moments(i, got):
            at = 4 * k + i
            xw[LEAVES + 2 * at] = got[0]
            xw[LEAVES + 2 * at + 1] = got[1]
            mv[32 + at] = got[2]

        batched(4, 4, leaf_moments, keep_moments)

    get_up.wait()
    zero = jnp.zeros((RHS, RANK), F32)
    for height in range(1, LEVELS + 1):
        amount = LEAVES >> height
        base, child = row_of(height), row_of(height - 1)

        def lift(j):
            return nn(mv[32 + child // 2 + j], upv[pl.ds(child + 2 * j, 2)].reshape(128, RANK))

        def lift_two(j):
            return jnp.concatenate([lift(2 * j), lift(2 * j + 1)], axis=1).astype(BF)

        def keep_two(j, got):
            mv[32 + base // 2 + j] = got

        if amount == 1:
            root = lift(0)
            mv[63] = jnp.concatenate([root, zero], axis=1).astype(BF)
        else:
            batched(amount // 2, 4, lift_two, keep_two)

    get_dn = load(local_down, dnv)
    get_nb = [load(near_block.at[pl.ds(4 * k, 4)], nbv.at[pl.ds(4 * k, 4)]) for k in range(8)]
    get_cp = [load(local_coupling.at[pl.ds(9 * k, 9)], cpv.at[pl.ds(9 * k, 9)]) for k in range(7)]
    get_rb = load(row_basis, rbv)

    lifted = nn(root.astype(BF), upv[62])
    rx[x] = jnp.where(low == (x < 2), jnp.concatenate([lifted, lifted], axis=1), 0.0).astype(BF)

    @pl.when(inner)
    def _():
        pl.semaphore_wait(barrier, 12)

    gone_x = [remote(rx.at[x], rx.at[x], rxsend.at[0], rxrecv.at[0], other)] + [
        remote(rx.at[x], rx.at[x], rxsend.at[1 + k], rxrecv.at[1 + x // 3], p) for k, p in enumerate(middle)
    ]

    @pl.when(inner)
    def _():
        gone_x[0].start()

    @pl.when(outer)
    def _():
        gone_x[1].start()
        gone_x[2].start()

    moved = [
        beside(
            mv.at[pl.ds(32 + 16 * k, 16)],
            lambda side: mv.at[pl.ds(32 * side + 16 * k, 16)],
            msend.at[k],
            mrecv.at[k],
        )
        for k in range(2)
    ]
    start(moved)
    pl.when(inner)(lambda: start(sent[:XFIRST]))
    start(sent[XFIRST:])

    get_at[0].wait()
    t = lax.broadcasted_iota(jnp.int32, (8, 63), 1)
    f = lax.broadcasted_iota(jnp.int32, (8, 63), 0)
    amount = jnp.full((8, 63), LEAVES, jnp.int32)
    for height in range(1, LEVELS + 1):
        amount = jnp.where(t < row_of(height), amount, LEAVES >> height)
    q = far_raw[...] - (d - 1) * amount
    window = (q >= amount).astype(jnp.int32) + (q >= 2 * amount).astype(jnp.int32)
    row = 64 - 2 * amount + (q & (amount - 1))
    far_row[...] = jnp.zeros((8, 64), jnp.int32)
    far_row[:, 0:63] = ((row + f) & 1) * 128 + window * 32 + (row >> 1)
    get_far = pltpu.make_async_copy(far_row, far_at, lsem.at[len(loads)])
    get_far.start()

    get_dn.wait()

    def extend_level(height):
        amount = LEAVES >> height
        base, parent = row_of(height), row_of(height + 1)

        def below(above, j):
            return nt(above, dnv[pl.ds(base + 2 * j, 2)].reshape(128, RANK)).astype(BF)

        if amount == 2:
            path[base // 2] = below(dnv[62].T, 0)
        else:

            def extend(j):
                above = path[parent // 2 + j]
                return below(above[:, :64], 2 * j), below(above[:, 64:], 2 * j + 1)

            def keep(j, got):
                path[base // 2 + 2 * j] = got[0]
                path[base // 2 + 2 * j + 1] = got[1]

            batched(amount // 4, 4, extend, keep)

    for height in range(LEVELS - 1, -1, -1):
        extend_level(height)

    get_uu.wait()
    gone_z = [remote(rz.at[z], rz.at[z], rzsend.at[k], rzrecv.at[k], p) for k, p in enumerate(by_z)]

    @pl.when(inner)
    def _():
        for k in range(3):
            remote(rx.at[k], rx.at[k], rxsend.at[k], rxrecv.at[k], other).wait_recv()
        first = (
            (rx[0].astype(F32) + rx[1].astype(F32)) + (rx[2].astype(F32) + rx[3].astype(F32))
        ).astype(BF)
        rz[z, 0] = first
        second = nn(first, uuv[pl.ds(2 * z, 2)].reshape(128, RANK))
        rz[z, 1] = jnp.where(low == (z % 2 == 0), jnp.concatenate([second, second], axis=1), 0.0).astype(BF)
        for copy in gone_z:
            copy.start()

    def near_own(i):
        return nt(xw[LEAVES + i], nbv[i, 0])

    def keep_own(i, got):
        acc[:, lanes(256 * i, 256)] = got

    for k in range(4):
        get_nb[k].wait()
        batched(4, OWN, lambda i: near_own(4 * k + i), lambda i, got: keep_own(4 * k + i, got))

    gone_y = [remote(rg.at[g], rg.at[g], rgsend.at[k], rgrecv.at[k], p) for k, p in enumerate(by_y + [twin])]

    @pl.when(inner)
    def _():
        for copy in gone_z:
            copy.wait_recv()
        for k in range(4):
            rg[g, k] = rz[k, 0]
        thirds = []
        for k in range(2):
            pair = (rz[2 * k, 1].astype(F32) + rz[2 * k + 1, 1].astype(F32)).astype(BF)
            rg[g, 4 + k] = pair
            thirds.append(nn(pair, uuv[8 + 2 * k : 10 + 2 * k].reshape(128, RANK)))
        third = jnp.concatenate(thirds, axis=1).astype(BF)
        rg[g, 6] = third
        top = nn(third, uuv[12:14].reshape(128, RANK))
        rg[g, 7] = jnp.concatenate([top, zero], axis=1).astype(BF)
        for copy in gone_y:
            copy.start()

    for k in range(4, 8):
        get_nb[k].wait()
        batched(4, OWN, lambda i: near_own(4 * k + i), lambda i, got: keep_own(4 * k + i, got))

    get_rb.wait()

    def reach(i):
        pair = path[i]
        return nn(pair[:, :64], rbv[2 * i]).astype(BF), nn(pair[:, 64:], rbv[2 * i + 1]).astype(BF)

    def keep_reach(i, got):
        qv[:, lanes(512 * i, 256)] = got[0]
        qv[:, lanes(512 * i + 256, 256)] = got[1]

    batched(16, REACH, reach, keep_reach)
    for copy in get_ud:
        copy.wait()
    down1 = udv[0]
    down2 = nn(down1, udv[1]).astype(BF)
    down3 = nn(down2, udv[2]).astype(BF)

    for copies in moved:
        arrive(copies)

    def turn(i):
        pair = mv[i]
        return jnp.concatenate([pair[:, 64:], pair[:, :64]], axis=1)

    def keep_turn(i, got):
        mv[128 + i] = got

    batched(96, TURN, turn, keep_turn)
    get_far.wait()
    for copy in get_cp:
        copy.wait()

    def couple(t):
        total = None
        for q in range(2):
            moments = jnp.concatenate(
                [
                    jnp.where(low, mv[far_at[4 * q + 2 * j, t]], mv[far_at[4 * q + 2 * j + 1, t]])
                    for j in range(2)
                ],
                axis=1,
            )
            blocks = jnp.concatenate([cpv[t, 4 * q + j] for j in range(4)], axis=1)
            term = nt(moments, blocks)
            total = term if total is None else total + term
        return total

    def couple_two(j):
        return jnp.concatenate([couple(2 * j), couple(2 * j + 1)], axis=1)

    def keep_couple(j, got):
        far[j] = got

    batched(32, FAR, couple_two, keep_couple)

    dloc[31] = far[31].astype(BF)
    for height in range(LEVELS - 1, -1, -1):
        amount = LEAVES >> height
        base, parent = row_of(height), row_of(height + 1)

        def below(above, j):
            pair = dnv[pl.ds(base + 2 * j, 2)].reshape(128, RANK)
            return (far[base // 2 + j] + nt(above, pair)).astype(BF)

        if amount == 2:
            dloc[base // 2] = below(dloc[31][:, :64], 0)
        else:

            def descend(j):
                above = dloc[parent // 2 + j]
                return below(above[:, :64], 2 * j), below(above[:, 64:], 2 * j + 1)

            def keep_descend(j, got):
                dloc[base // 2 + 2 * j] = got[0]
                dloc[base // 2 + 2 * j + 1] = got[1]

            batched(amount // 4, 4, descend, keep_descend)

    def local(i):
        pair = dloc[i]
        return [
            acc[:, lanes(512 * i + 256 * k, 256)] + nn(pair[:, 64 * k : 64 * (k + 1)], rbv[2 * i + k])
            for k in range(2)
        ]

    def keep_rest(i, got):
        for k in range(2):
            acc[:, lanes(512 * i + 256 * k, 256)] = got[k]

    batched(16, 8, local, keep_rest)

    get_at[2].wait()
    for copies, (start, size) in zip(sent, XPARTS):
        arrive(copies)

        def window(i):
            part = lanes(start + LEAF * i, LEAF)
            return xin[0, :, part], xin[1, :, part]

        def keep_window(i, got):
            xw[start // LEAF + i] = got[0]
            xw[2 * LEAVES + start // LEAF + i] = got[1]

        batched(size // LEAF, 4, window, keep_window)

    def rest(i):
        totals = []
        for k in range(2):
            leaf = 2 * i + k
            total = acc[:, lanes(256 * leaf, 256)]
            for n in (1, 2):
                q = (near_at[n, leaf] - (d - 1) * LEAVES) & 127
                total = total + nt(xw[q], nbv[leaf, n])
            totals.append(total)
        return totals

    batched(16, REST, rest, keep_rest)

    get_at[1].wait()
    for copy in get_uc:
        copy.wait()
    passed = []
    for k in range(3):
        from_y = ((y + 3 - k) % 4) * 2 + core
        passed.append(remote(rg.at[from_y], rg.at[from_y], rgsend.at[4 + k], rgrecv.at[4 + k], twin))
    gone_p = remote(pv, pv, psend, precv, helped)

    @pl.when(inner)
    def _():
        for k in (0, 2, 1):
            gone_y[k].wait_recv()
            passed[k].start()
        gone_y[3].wait_recv()
        for copy in passed:
            copy.wait_recv()
        terms = []
        for k in range(1, 5):
            amount = 16 >> k
            row = 16 - 2 * amount + s // 2**k

            def pick(f):
                p = ufar_at[f, row]
                group, j = p >> (4 - k), p & (amount - 1)
                pair = rg[group, (0, 4, 6, 7)[k - 1] + (j >> 1)]
                pair = pair.astype(F32)
                turned = jnp.concatenate([pair[:, 64:], pair[:, :64]], axis=1)
                keep = (1 - ((j + f) & 1)).astype(F32)
                return pair * keep + turned * (1.0 - keep)

            total = None
            for q in range(2):
                moments = jnp.concatenate(
                    [jnp.where(low, pick(4 * q + 2 * j), pick(4 * q + 2 * j + 1)) for j in range(2)], axis=1
                ).astype(BF)
                blocks = jnp.concatenate([ucv[k - 1, 4 * q + j] for j in range(4)], axis=1)
                term = nt(moments, blocks)
                total = term if total is None else total + term
            terms.append(total)
        parent = (
            terms[0]
            + nt(terms[1].astype(BF), down1)
            + nt(terms[2].astype(BF), down2)
            + nt(terms[3].astype(BF), down3)
        ).astype(BF)
        pv[...] = jnp.concatenate([parent, parent], axis=1)
        gone_p.start()

    pl.when(outer)(gone_p.wait_recv)
    parent = pv[...][:, :64]

    def finish(i):
        part = lanes(512 * i, 512)
        return (acc[:, part] + nn(parent, qv[:, part])).astype(BF)

    def keep_finish(i, got):
        out[:, lanes(512 * i, 512)] = got

    batched(16, FINISH, finish, keep_finish)

    for copies in sent:
        leave(copies)
    for copies in moved:
        leave(copies)

    @pl.when(inner)
    def _():
        for copy in [gone_x[0]] + gone_z + gone_y + passed + [gone_p]:
            copy.wait_send()

    @pl.when(outer)
    def _():
        gone_x[1].wait_send()
        gone_x[2].wait_send()


def on_device(
    charges,
    column_basis,
    row_basis,
    local_up,
    local_down,
    local_far,
    local_coupling,
    upper_up,
    upper_down,
    upper_far,
    upper_coupling,
    near_source,
    near_block,
):
    dma = pltpu.SemaphoreType.DMA
    vmem = pltpu.VMEM
    anywhere = pl.BlockSpec(memory_space=pl.ANY)
    return pl.pallas_call(
        kernel,
        out_shape=pltpu.VMEM((RHS, COLS), BF),
        in_specs=[anywhere] * 13,
        out_specs=pl.BlockSpec(memory_space=vmem),
        scratch_shapes=[
            vmem((RHS, COLS), BF),
            vmem((2, RHS, COLS), BF),
            vmem((4 * LEAVES, RHS, LEAF), BF),
            vmem((LEAVES, RANK, LEAF), BF),
            vmem((LEAVES, RANK, LEAF), BF),
            vmem((63, RANK, RANK), BF),
            vmem((63, RANK, RANK), BF),
            vmem((64, 8, RANK, RANK), BF),
            vmem((14, RANK, RANK), BF),
            vmem((3, RANK, RANK), BF),
            vmem((4, 8, RANK, RANK), BF),
            vmem((LEAVES, 3, LEAF, LEAF), BF),
            vmem((256, RHS, 128), BF),
            vmem((4, RHS, 128), BF),
            vmem((4, 2, RHS, 128), BF),
            vmem((8, 8, RHS, 128), BF),
            vmem((RHS, 128), BF),
            vmem((RHS, COLS), F32),
            vmem((32, RHS, 128), F32),
            vmem((32, RHS, 128), BF),
            vmem((32, RANK, 128), BF),
            vmem((RANK, COLS), BF),
            vmem((8, 63), jnp.int32),
            vmem((8, 64), jnp.int32),
            pltpu.SMEM((8, 64), jnp.int32),
            pltpu.SMEM((8, 15), jnp.int32),
            pltpu.SMEM((3, LEAVES), jnp.int32),
            dma((40,)),
            dma((len(XPARTS), 2)),
            dma((len(XPARTS), 2)),
            dma((2, 2)),
            dma((2, 2)),
            dma((3,)),
            dma((3,)),
            dma((3,)),
            dma((3,)),
            dma((7,)),
            dma((7,)),
            dma,
            dma,
        ],
        compiler_params=pltpu.CompilerParams(
            collective_id=0, has_side_effects=True, vmem_limit_bytes=60 * 2**20
        ),
        name="h2_product",
    )(
        charges,
        column_basis,
        row_basis,
        local_up,
        local_down,
        local_far.T,
        local_coupling,
        upper_up,
        upper_down,
        upper_far.T,
        upper_coupling,
        near_source.T,
        near_block,
    )


def solution(mesh):
    both = ("grp", "sub")
    in_specs = (
        P(None, both),
        P(both, None, None),
        P(both, None, None),
        P(both, None, None),
        P(both, None, None),
        P(both, None),
        P(both, None, None, None),
        P("grp", None, None),
        P("grp", None, None),
        P("grp", None),
        P("grp", None, None, None),
        P(both, None),
        P(both, None, None, None),
    )
    return jax.shard_map(
        on_device, mesh=mesh, in_specs=in_specs, out_specs=P(None, both), check_vma=False
    )
```

```python
import functools

import jax
import jax.numpy as jnp
from jax import lax
from jax.experimental import pallas as pl
from jax.experimental.pallas import tpu as pltpu
from jax.sharding import PartitionSpec as P

MESH = pl.DeviceIdType.MESH
BF = jnp.bfloat16
F32 = jnp.float32
RHS = 32
LEAVES = 32
LEAF = 256
RANK = 64
LEVELS = 5
COLS = LEAVES * LEAF
XPARTS = ((0, 1024), (1024, 1024), (2048, 2048), (4096, 2048), (6144, 2048))
XFIRST = 2
OWN, REACH, TURN, FAR, REST, FINISH = 4, 16, 96, 16, 16, 16


def nt(a, b):
    return lax.dot_general(a, b, (((1,), (1,)), ((), ())), preferred_element_type=F32)


def nn(a, b):
    return lax.dot_general(a, b, (((1,), (0,)), ((), ())), preferred_element_type=F32)


def lanes(start, size):
    return pl.ds(pl.multiple_of(start, 128), size)


def loop(count, body, unroll):
    def step(i, carry):
        body(i)
        return carry

    lax.fori_loop(0, count, step, 0, unroll=min(unroll, count))


def batched(count, width, compute, store):
    width = min(width, count)

    def body(b):
        got = [compute(width * b + j) for j in range(width)]
        for j in range(width):
            store(width * b + j, got[j])

    loop(count // width, body, 1)


def row_of(height):
    return 64 - 2 * (LEAVES >> height)


def kernel(
    charges,
    column_basis,
    row_basis,
    local_up,
    local_down,
    local_far,
    local_coupling,
    upper_up,
    upper_down,
    upper_far,
    upper_coupling,
    near_source,
    near_block,
    out,
    cx,
    xin,
    xw,
    cbv,
    rbv,
    upv,
    dnv,
    cpv,
    uuv,
    udv,
    ucv,
    nbv,
    mv,
    rx,
    rz,
    rg,
    pv,
    acc,
    far,
    dloc,
    path,
    qv,
    far_raw,
    far_row,
    far_at,
    ufar_at,
    near_at,
    lsem,
    xsend,
    xrecv,
    msend,
    mrecv,
    rxsend,
    rxrecv,
    rzsend,
    rzrecv,
    rgsend,
    rgrecv,
    psend,
    precv,
):
    g = lax.axis_index("grp")
    s = lax.axis_index("sub")
    d = g * 16 + s
    z = s // 4
    x = s % 4

    def place(e):
        return (e // 16, e % 16)

    sides = ((d < 127, place((d + 1) % 128)), (d > 0, place((d + 127) % 128)))
    inner = (x == 1) | (x == 2)
    outer = jnp.logical_not(inner)
    y, core = g // 2, g % 2
    middle = [(g, z * 4 + 1), (g, z * 4 + 2)]
    other = (g, z * 4 + 3 - x)
    helped = (g, z * 4 + 3 * (x // 2))
    by_z = [(g, ((z + k) % 4) * 4 + x) for k in range(1, 4)]
    by_y = [(((y + k) % 4) * 2 + core, s) for k in range(1, 4)]
    twin = (2 * y + 1 - core, s)

    barrier = pltpu.get_barrier_semaphore()

    def greet(peer):
        pl.semaphore_signal(barrier, inc=1, device_id=peer, device_id_type=MESH)

    for there, peer in sides:
        pl.when(there)(functools.partial(greet, peer))

    @pl.when(inner)
    def _():
        for peer in [other, (g, z * 4), (g, z * 4 + 3)] + by_z + by_y + [twin]:
            greet(peer)

    @pl.when(outer)
    def _():
        for peer in middle:
            greet(peer)

    loads = []

    def load(src, dst):
        copy = pltpu.make_async_copy(src, dst, lsem.at[len(loads)])
        copy.start()
        loads.append(copy)
        return copy

    get_x = [load(charges.at[:, pl.ds(4096 * k, 4096)], cx.at[:, pl.ds(4096 * k, 4096)]) for k in range(2)]
    get_cb = [load(column_basis.at[pl.ds(8 * k, 8)], cbv.at[pl.ds(8 * k, 8)]) for k in range(4)]
    get_up = load(local_up, upv)
    get_uu = load(upper_up, uuv)
    get_at = [load(local_far, far_raw), load(upper_far, ufar_at), load(near_source, near_at)]

    @pl.when(outer)
    def _():
        pl.semaphore_wait(barrier, 2 + (d < 127).astype(jnp.int32) + (d > 0).astype(jnp.int32))

    def remote(src, dst, ssem, rsem, peer):
        return pltpu.make_async_remote_copy(
            src_ref=src, dst_ref=dst, send_sem=ssem, recv_sem=rsem, device_id=peer, device_id_type=MESH
        )

    def send(src, dst, ssem, rsem, peer):
        copy = remote(src, dst, ssem, rsem, peer)
        copy.start()
        return copy

    def beside(src, dst, ssem, rsem):
        return [remote(src, dst(2 * k), ssem.at[k], rsem.at[k], peer) for k, (_, peer) in enumerate(sides)]

    def start(batches):
        for k, (there, _) in enumerate(sides):

            @pl.when(there)
            def _():
                for copies in batches:
                    copies[k].start()

    def arrive(copies):
        for (there, _), copy in zip((sides[1], sides[0]), copies):
            pl.when(there)(copy.wait_recv)

    def leave(copies):
        for (there, _), copy in zip(sides, copies):
            pl.when(there)(copy.wait_send)

    def charges_part(k):
        start, size = XPARTS[k]
        part = pl.ds(start, size)
        return beside(
            charges.at[:, part],
            lambda side: xin.at[side // 2, :, part],
            xsend.at[k],
            xrecv.at[k],
        )

    sent = [charges_part(k) for k in range(len(XPARTS))]
    pl.when(outer)(lambda: start(sent[:XFIRST]))

    get_ud = [
        load(upper_down.at[16 - (32 >> k) + s // 2**k], udv.at[k - 1]) for k in range(1, 4)
    ]
    get_uc = [
        load(upper_coupling.at[16 - (32 >> k) + s // 2**k], ucv.at[k - 1]) for k in range(1, 5)
    ]

    low = lax.broadcasted_iota(jnp.int32, (RHS, 128), 1) < 64

    for k in range(4):
        if k % 2 == 0:
            get_x[k // 2].wait()
        get_cb[k].wait()

        def leaf_moments(i):
            at = 4 * k + i
            one, two = cx[:, lanes(512 * at, 256)], cx[:, lanes(512 * at + 256, 256)]
            both = nt(jnp.concatenate([one, two], axis=0), cbv[pl.ds(2 * at, 2)].reshape(128, LEAF))
            return one, two, jnp.where(low, both[:RHS], both[RHS:]).astype(BF)

        def keep_moments(i, got):
            at = 4 * k + i
            xw[LEAVES + 2 * at] = got[0]
            xw[LEAVES + 2 * at + 1] = got[1]
            mv[32 + at] = got[2]

        batched(4, 4, leaf_moments, keep_moments)

    @pl.when(inner)
    def _():
        pl.semaphore_wait(barrier, 12)
        start(sent[:1])

    get_up.wait()
    zero = jnp.zeros((RHS, RANK), F32)
    for height in range(1, LEVELS + 1):
        amount = LEAVES >> height
        base, child = row_of(height), row_of(height - 1)

        def lift(j):
            return nn(mv[32 + child // 2 + j], upv[pl.ds(child + 2 * j, 2)].reshape(128, RANK))

        def lift_two(j):
            return jnp.concatenate([lift(2 * j), lift(2 * j + 1)], axis=1).astype(BF)

        def keep_two(j, got):
            mv[32 + base // 2 + j] = got

        if amount == 1:
            root = lift(0)
            mv[63] = jnp.concatenate([root, zero], axis=1).astype(BF)
        else:
            batched(amount // 2, 4, lift_two, keep_two)

    get_dn = load(local_down, dnv)
    get_nb = [load(near_block.at[pl.ds(4 * k, 4)], nbv.at[pl.ds(4 * k, 4)]) for k in range(8)]
    get_cp = [load(local_coupling.at[pl.ds(9 * k, 9)], cpv.at[pl.ds(9 * k, 9)]) for k in range(7)]
    get_rb = load(row_basis, rbv)

    lifted = nn(root.astype(BF), upv[62])
    rx[x] = jnp.where(low == (x < 2), jnp.concatenate([lifted, lifted], axis=1), 0.0).astype(BF)

    gone_x = [remote(rx.at[x], rx.at[x], rxsend.at[0], rxrecv.at[0], other)] + [
        remote(rx.at[x], rx.at[x], rxsend.at[1 + k], rxrecv.at[1 + x // 3], p) for k, p in enumerate(middle)
    ]

    @pl.when(inner)
    def _():
        gone_x[0].start()

    @pl.when(outer)
    def _():
        gone_x[1].start()
        gone_x[2].start()

    moved = [
        beside(
            mv.at[pl.ds(32 + 16 * k, 16)],
            lambda side: mv.at[pl.ds(32 * side + 16 * k, 16)],
            msend.at[k],
            mrecv.at[k],
        )
        for k in range(2)
    ]
    start(moved)
    pl.when(inner)(lambda: start(sent[1:XFIRST]))
    start(sent[XFIRST:])

    get_at[0].wait()
    t = lax.broadcasted_iota(jnp.int32, (8, 63), 1)
    f = lax.broadcasted_iota(jnp.int32, (8, 63), 0)
    amount = jnp.full((8, 63), LEAVES, jnp.int32)
    for height in range(1, LEVELS + 1):
        amount = jnp.where(t < row_of(height), amount, LEAVES >> height)
    q = far_raw[...] - (d - 1) * amount
    window = (q >= amount).astype(jnp.int32) + (q >= 2 * amount).astype(jnp.int32)
    row = 64 - 2 * amount + (q & (amount - 1))
    far_row[...] = jnp.zeros((8, 64), jnp.int32)
    far_row[:, 0:63] = ((row + f) & 1) * 128 + window * 32 + (row >> 1)
    get_far = pltpu.make_async_copy(far_row, far_at, lsem.at[len(loads)])
    get_far.start()

    get_dn.wait()

    def extend_level(height):
        amount = LEAVES >> height
        base, parent = row_of(height), row_of(height + 1)

        def below(above, j):
            return nt(above, dnv[pl.ds(base + 2 * j, 2)].reshape(128, RANK)).astype(BF)

        if amount == 2:
            path[base // 2] = below(dnv[62].T, 0)
        else:

            def extend(j):
                above = path[parent // 2 + j]
                return below(above[:, :64], 2 * j), below(above[:, 64:], 2 * j + 1)

            def keep(j, got):
                path[base // 2 + 2 * j] = got[0]
                path[base // 2 + 2 * j + 1] = got[1]

            batched(amount // 4, 4, extend, keep)

    for height in range(LEVELS - 1, -1, -1):
        extend_level(height)

    get_uu.wait()
    gone_z = [remote(rz.at[z], rz.at[z], rzsend.at[k], rzrecv.at[k], p) for k, p in enumerate(by_z)]

    @pl.when(inner)
    def _():
        for k in range(3):
            remote(rx.at[k], rx.at[k], rxsend.at[k], rxrecv.at[k], other).wait_recv()
        first = (
            (rx[0].astype(F32) + rx[1].astype(F32)) + (rx[2].astype(F32) + rx[3].astype(F32))
        ).astype(BF)
        rz[z, 0] = first
        second = nn(first, uuv[pl.ds(2 * z, 2)].reshape(128, RANK))
        rz[z, 1] = jnp.where(low == (z % 2 == 0), jnp.concatenate([second, second], axis=1), 0.0).astype(BF)
        for copy in gone_z:
            copy.start()

    def near_own(i):
        return nt(xw[LEAVES + i], nbv[i, 0])

    def keep_own(i, got):
        acc[:, lanes(256 * i, 256)] = got

    for k in range(4):
        get_nb[k].wait()
        batched(4, OWN, lambda i: near_own(4 * k + i), lambda i, got: keep_own(4 * k + i, got))

    gone_y = [remote(rg.at[g], rg.at[g], rgsend.at[k], rgrecv.at[k], p) for k, p in enumerate(by_y + [twin])]

    @pl.when(inner)
    def _():
        for copy in gone_z:
            copy.wait_recv()
        for k in range(4):
            rg[g, k] = rz[k, 0]
        thirds = []
        for k in range(2):
            pair = (rz[2 * k, 1].astype(F32) + rz[2 * k + 1, 1].astype(F32)).astype(BF)
            rg[g, 4 + k] = pair
            thirds.append(nn(pair, uuv[8 + 2 * k : 10 + 2 * k].reshape(128, RANK)))
        third = jnp.concatenate(thirds, axis=1).astype(BF)
        rg[g, 6] = third
        top = nn(third, uuv[12:14].reshape(128, RANK))
        rg[g, 7] = jnp.concatenate([top, zero], axis=1).astype(BF)
        for copy in gone_y:
            copy.start()

    for k in range(4, 8):
        get_nb[k].wait()
        batched(4, OWN, lambda i: near_own(4 * k + i), lambda i, got: keep_own(4 * k + i, got))

    get_rb.wait()

    def reach(i):
        pair = path[i]
        return nn(pair[:, :64], rbv[2 * i]).astype(BF), nn(pair[:, 64:], rbv[2 * i + 1]).astype(BF)

    def keep_reach(i, got):
        qv[:, lanes(512 * i, 256)] = got[0]
        qv[:, lanes(512 * i + 256, 256)] = got[1]

    batched(16, REACH, reach, keep_reach)
    for copy in get_ud:
        copy.wait()
    down1 = udv[0]
    down2 = nn(down1, udv[1]).astype(BF)
    down3 = nn(down2, udv[2]).astype(BF)

    for copies in moved:
        arrive(copies)

    def turn(i):
        pair = mv[i]
        return jnp.concatenate([pair[:, 64:], pair[:, :64]], axis=1)

    def keep_turn(i, got):
        mv[128 + i] = got

    batched(96, TURN, turn, keep_turn)
    get_far.wait()
    for copy in get_cp:
        copy.wait()

    def couple(t):
        total = None
        for q in range(2):
            moments = jnp.concatenate(
                [
                    jnp.where(low, mv[far_at[4 * q + 2 * j, t]], mv[far_at[4 * q + 2 * j + 1, t]])
                    for j in range(2)
                ],
                axis=1,
            )
            blocks = jnp.concatenate([cpv[t, 4 * q + j] for j in range(4)], axis=1)
            term = nt(moments, blocks)
            total = term if total is None else total + term
        return total

    def couple_two(j):
        return jnp.concatenate([couple(2 * j), couple(2 * j + 1)], axis=1)

    def keep_couple(j, got):
        far[j] = got

    batched(32, FAR, couple_two, keep_couple)

    dloc[31] = far[31].astype(BF)
    for height in range(LEVELS - 1, -1, -1):
        amount = LEAVES >> height
        base, parent = row_of(height), row_of(height + 1)

        def below(above, j):
            pair = dnv[pl.ds(base + 2 * j, 2)].reshape(128, RANK)
            return (far[base // 2 + j] + nt(above, pair)).astype(BF)

        if amount == 2:
            dloc[base // 2] = below(dloc[31][:, :64], 0)
        else:

            def descend(j):
                above = dloc[parent // 2 + j]
                return below(above[:, :64], 2 * j), below(above[:, 64:], 2 * j + 1)

            def keep_descend(j, got):
                dloc[base // 2 + 2 * j] = got[0]
                dloc[base // 2 + 2 * j + 1] = got[1]

            batched(amount // 4, 4, descend, keep_descend)

    def local(i):
        pair = dloc[i]
        return [
            acc[:, lanes(512 * i + 256 * k, 256)] + nn(pair[:, 64 * k : 64 * (k + 1)], rbv[2 * i + k])
            for k in range(2)
        ]

    def keep_rest(i, got):
        for k in range(2):
            acc[:, lanes(512 * i + 256 * k, 256)] = got[k]

    batched(16, 8, local, keep_rest)

    get_at[1].wait()
    for copy in get_uc:
        copy.wait()
    passed = []
    for k in range(3):
        from_y = ((y + 3 - k) % 4) * 2 + core
        passed.append(remote(rg.at[from_y], rg.at[from_y], rgsend.at[4 + k], rgrecv.at[4 + k], twin))
    gone_p = remote(pv, pv, psend, precv, helped)

    @pl.when(inner)
    def _():
        for k in (0, 2, 1):
            gone_y[k].wait_recv()
            passed[k].start()
        gone_y[3].wait_recv()
        for copy in passed:
            copy.wait_recv()
        terms = []
        for k in range(1, 5):
            amount = 16 >> k
            row = 16 - 2 * amount + s // 2**k

            def pick(f):
                p = ufar_at[f, row]
                group, j = p >> (4 - k), p & (amount - 1)
                pair = rg[group, (0, 4, 6, 7)[k - 1] + (j >> 1)]
                pair = pair.astype(F32)
                turned = jnp.concatenate([pair[:, 64:], pair[:, :64]], axis=1)
                keep = (1 - ((j + f) & 1)).astype(F32)
                return pair * keep + turned * (1.0 - keep)

            total = None
            for q in range(2):
                moments = jnp.concatenate(
                    [jnp.where(low, pick(4 * q + 2 * j), pick(4 * q + 2 * j + 1)) for j in range(2)], axis=1
                ).astype(BF)
                blocks = jnp.concatenate([ucv[k - 1, 4 * q + j] for j in range(4)], axis=1)
                term = nt(moments, blocks)
                total = term if total is None else total + term
            terms.append(total)
        parent = (
            terms[0]
            + nt(terms[1].astype(BF), down1)
            + nt(terms[2].astype(BF), down2)
            + nt(terms[3].astype(BF), down3)
        ).astype(BF)
        pv[...] = jnp.concatenate([parent, parent], axis=1)
        gone_p.start()

    pl.when(outer)(gone_p.wait_recv)
    parent = pv[...][:, :64]

    get_at[2].wait()
    for copies, (start, size) in zip(sent, XPARTS):
        arrive(copies)

        def window(i):
            part = lanes(start + LEAF * i, LEAF)
            return xin[0, :, part], xin[1, :, part]

        def keep_window(i, got):
            xw[start // LEAF + i] = got[0]
            xw[2 * LEAVES + start // LEAF + i] = got[1]

        batched(size // LEAF, 4, window, keep_window)

    def rest(i):
        totals = []
        above = nn(parent, qv[:, lanes(512 * i, 512)])
        for k in range(2):
            leaf = 2 * i + k
            total = acc[:, lanes(256 * leaf, 256)] + above[:, 256 * k : 256 * (k + 1)]
            for n in (1, 2):
                q = (near_at[n, leaf] - (d - 1) * LEAVES) & 127
                total = total + nt(xw[q], nbv[leaf, n])
            totals.append(total.astype(BF))
        return totals

    def keep_out(i, got):
        for k in range(2):
            out[:, lanes(512 * i + 256 * k, 256)] = got[k]

    batched(16, REST, rest, keep_out)

    for copies in sent:
        leave(copies)
    for copies in moved:
        leave(copies)

    @pl.when(inner)
    def _():
        for copy in [gone_x[0]] + gone_z + gone_y + passed + [gone_p]:
            copy.wait_send()

    @pl.when(outer)
    def _():
        gone_x[1].wait_send()
        gone_x[2].wait_send()


def on_device(
    charges,
    column_basis,
    row_basis,
    local_up,
    local_down,
    local_far,
    local_coupling,
    upper_up,
    upper_down,
    upper_far,
    upper_coupling,
    near_source,
    near_block,
):
    dma = pltpu.SemaphoreType.DMA
    vmem = pltpu.VMEM
    anywhere = pl.BlockSpec(memory_space=pl.ANY)
    return pl.pallas_call(
        kernel,
        out_shape=pltpu.VMEM((RHS, COLS), BF),
        in_specs=[anywhere] * 13,
        out_specs=pl.BlockSpec(memory_space=vmem),
        scratch_shapes=[
            vmem((RHS, COLS), BF),
            vmem((2, RHS, COLS), BF),
            vmem((4 * LEAVES, RHS, LEAF), BF),
            vmem((LEAVES, RANK, LEAF), BF),
            vmem((LEAVES, RANK, LEAF), BF),
            vmem((63, RANK, RANK), BF),
            vmem((63, RANK, RANK), BF),
            vmem((64, 8, RANK, RANK), BF),
            vmem((14, RANK, RANK), BF),
            vmem((3, RANK, RANK), BF),
            vmem((4, 8, RANK, RANK), BF),
            vmem((LEAVES, 3, LEAF, LEAF), BF),
            vmem((256, RHS, 128), BF),
            vmem((4, RHS, 128), BF),
            vmem((4, 2, RHS, 128), BF),
            vmem((8, 8, RHS, 128), BF),
            vmem((RHS, 128), BF),
            vmem((RHS, COLS), F32),
            vmem((32, RHS, 128), F32),
            vmem((32, RHS, 128), BF),
            vmem((32, RANK, 128), BF),
            vmem((RANK, COLS), BF),
            vmem((8, 63), jnp.int32),
            vmem((8, 64), jnp.int32),
            pltpu.SMEM((8, 64), jnp.int32),
            pltpu.SMEM((8, 15), jnp.int32),
            pltpu.SMEM((3, LEAVES), jnp.int32),
            dma((40,)),
            dma((len(XPARTS), 2)),
            dma((len(XPARTS), 2)),
            dma((2, 2)),
            dma((2, 2)),
            dma((3,)),
            dma((3,)),
            dma((3,)),
            dma((3,)),
            dma((7,)),
            dma((7,)),
            dma,
            dma,
        ],
        compiler_params=pltpu.CompilerParams(
            collective_id=0, has_side_effects=True, vmem_limit_bytes=60 * 2**20
        ),
        name="h2_product",
    )(
        charges,
        column_basis,
        row_basis,
        local_up,
        local_down,
        local_far.T,
        local_coupling,
        upper_up,
        upper_down,
        upper_far.T,
        upper_coupling,
        near_source.T,
        near_block,
    )


def solution(mesh):
    both = ("grp", "sub")
    in_specs = (
        P(None, both),
        P(both, None, None),
        P(both, None, None),
        P(both, None, None),
        P(both, None, None),
        P(both, None),
        P(both, None, None, None),
        P("grp", None, None),
        P("grp", None, None),
        P("grp", None),
        P("grp", None, None, None),
        P(both, None),
        P(both, None, None, None),
    )
    return jax.shard_map(
        on_device, mesh=mesh, in_specs=in_specs, out_specs=P(None, both), check_vma=False
    )
```

```python
import functools

import jax
import jax.numpy as jnp
from jax import lax
from jax.experimental import pallas as pl
from jax.experimental.pallas import tpu as pltpu
from jax.sharding import PartitionSpec as P

MESH = pl.DeviceIdType.MESH
BF = jnp.bfloat16
F32 = jnp.float32
RHS = 32
LEAVES = 32
LEAF = 256
RANK = 64
LEVELS = 5
COLS = LEAVES * LEAF
XPARTS = ((0, 1024), (1024, 1024), (2048, 2048), (4096, 3072), (7168, 1024))
XFIRST = 2
OWN, REACH, TURN, FAR, REST, FINISH = 4, 16, 96, 16, 16, 16


def nt(a, b):
    return lax.dot_general(a, b, (((1,), (1,)), ((), ())), preferred_element_type=F32)


def nn(a, b):
    return lax.dot_general(a, b, (((1,), (0,)), ((), ())), preferred_element_type=F32)


def lanes(start, size):
    return pl.ds(pl.multiple_of(start, 128), size)


def loop(count, body, unroll):
    def step(i, carry):
        body(i)
        return carry

    lax.fori_loop(0, count, step, 0, unroll=min(unroll, count))


def batched(count, width, compute, store):
    width = min(width, count)

    def body(b):
        got = [compute(width * b + j) for j in range(width)]
        for j in range(width):
            store(width * b + j, got[j])

    loop(count // width, body, 1)


def row_of(height):
    return 64 - 2 * (LEAVES >> height)


def kernel(
    charges,
    column_basis,
    row_basis,
    local_up,
    local_down,
    local_far,
    local_coupling,
    upper_up,
    upper_down,
    upper_far,
    upper_coupling,
    near_source,
    near_block,
    out,
    cx,
    xin,
    xw,
    cbv,
    rbv,
    upv,
    dnv,
    cpv,
    uuv,
    udv,
    ucv,
    nbv,
    mv,
    rx,
    rz,
    rg,
    pv,
    acc,
    far,
    dloc,
    path,
    qv,
    far_raw,
    far_row,
    far_at,
    ufar_at,
    near_at,
    lsem,
    xsend,
    xrecv,
    msend,
    mrecv,
    rxsend,
    rxrecv,
    rzsend,
    rzrecv,
    rgsend,
    rgrecv,
    psend,
    precv,
    hello,
    hop,
    hsend,
    hrecv,
):
    g = lax.axis_index("grp")
    s = lax.axis_index("sub")
    d = g * 16 + s
    z = s // 4
    x = s % 4

    def place(e):
        return (e // 16, e % 16)

    sides = ((d < 127, place((d + 1) % 128)), (d > 0, place((d + 127) % 128)))
    inner = (x == 1) | (x == 2)
    outer = jnp.logical_not(inner)
    y, core = g // 2, g % 2
    middle = [(g, z * 4 + 1), (g, z * 4 + 2)]
    other = (g, z * 4 + 3 - x)
    helped = (g, z * 4 + 3 * (x // 2))
    by_z = [(g, ((z + k) % 4) * 4 + x) for k in range(1, 4)]
    by_y = [(((y + k) % 4) * 2 + core, s) for k in range(1, 4)]
    twin = (2 * y + 1 - core, s)

    first0 = (s == 0) & (g > 0)
    last15 = (s == 15) & (g < 7)
    relay3 = (s == 3) & (g < 7)

    barrier = pltpu.get_barrier_semaphore()

    def greet(peer):
        pl.semaphore_signal(barrier, inc=1, device_id=peer, device_id_type=MESH)

    pl.when((d < 127) & jnp.logical_not(last15))(functools.partial(greet, sides[0][1]))
    pl.when(d > 0)(functools.partial(greet, sides[1][1]))
    pl.when(first0)(functools.partial(greet, (g - 1, s + 3)))
    pl.when(relay3)(functools.partial(greet, (g, s + 12)))

    @pl.when(inner)
    def _():
        for peer in [other, (g, z * 4), (g, z * 4 + 3)] + by_z + by_y + [twin]:
            greet(peer)

    @pl.when(outer)
    def _():
        for peer in middle:
            greet(peer)

    loads = []

    def load(src, dst):
        copy = pltpu.make_async_copy(src, dst, lsem.at[len(loads)])
        copy.start()
        loads.append(copy)
        return copy

    get_x = [load(charges.at[:, pl.ds(4096 * k, 4096)], cx.at[:, pl.ds(4096 * k, 4096)]) for k in range(2)]
    get_cb = [load(column_basis.at[pl.ds(8 * k, 8)], cbv.at[pl.ds(8 * k, 8)]) for k in range(4)]
    get_up = load(local_up, upv)
    get_uu = load(upper_up, uuv)
    get_at = [load(local_far, far_raw), load(upper_far, ufar_at), load(near_source, near_at)]

    @pl.when(outer)
    def _():
        count = 2 + (d < 127).astype(jnp.int32) + ((d > 0) & (s > 0)).astype(jnp.int32)
        pl.semaphore_wait(barrier, count + (last15 | relay3).astype(jnp.int32))
        pl.when(last15)(lambda: pl.semaphore_signal(hello, inc=1, device_id=sides[0][1], device_id_type=MESH))

    def remote(src, dst, ssem, rsem, peer):
        return pltpu.make_async_remote_copy(
            src_ref=src, dst_ref=dst, send_sem=ssem, recv_sem=rsem, device_id=peer, device_id_type=MESH
        )

    def send(src, dst, ssem, rsem, peer):
        copy = remote(src, dst, ssem, rsem, peer)
        copy.start()
        return copy

    def beside(src, dst, ssem, rsem):
        return [remote(src, dst(2 * k), ssem.at[k], rsem.at[k], peer) for k, (_, peer) in enumerate(sides)]

    def start(batches, late=False):
        for k, (there, _) in enumerate(sides):
            if late:
                go = first0 if k else False
            else:
                go = there & jnp.logical_not(first0) if k else there

            if go is not False:

                @pl.when(go)
                def _():
                    for copies in batches:
                        copies[k].start()

    def arrive(copies):
        for (there, _), copy in zip((sides[1], sides[0]), copies):
            pl.when(there)(copy.wait_recv)

    def leave(copies):
        for (there, _), copy in zip(sides, copies):
            pl.when(there)(copy.wait_send)

    def charges_part(k):
        start, size = XPARTS[k]
        part = pl.ds(start, size)
        return beside(
            charges.at[:, part],
            lambda side: xin.at[side // 2, :, part],
            xsend.at[k],
            xrecv.at[k],
        )

    sent = [charges_part(k) for k in range(len(XPARTS))]
    part = pl.ds(*XPARTS[-1])
    to_relay = remote(charges.at[:, part], hop, hsend.at[0], hrecv, (g, z * 4 - 9))
    from_relay = remote(hop, xin.at[0, :, part], hsend.at[1], xrecv.at[len(XPARTS) - 1, 0], (g + 1, s - 3))
    pl.when(last15)(to_relay.start)
    pl.when(outer)(lambda: start(sent[:XFIRST]))

    get_ud = [
        load(upper_down.at[16 - (32 >> k) + s // 2**k], udv.at[k - 1]) for k in range(1, 4)
    ]
    get_uc = [
        load(upper_coupling.at[16 - (32 >> k) + s // 2**k], ucv.at[k - 1]) for k in range(1, 5)
    ]

    low = lax.broadcasted_iota(jnp.int32, (RHS, 128), 1) < 64

    for k in range(4):
        if k % 2 == 0:
            get_x[k // 2].wait()
        get_cb[k].wait()

        def leaf_moments(i):
            at = 4 * k + i
            one, two = cx[:, lanes(512 * at, 256)], cx[:, lanes(512 * at + 256, 256)]
            both = nt(jnp.concatenate([one, two], axis=0), cbv[pl.ds(2 * at, 2)].reshape(128, LEAF))
            return one, two, jnp.where(low, both[:RHS], both[RHS:]).astype(BF)

        def keep_moments(i, got):
            at = 4 * k + i
            xw[LEAVES + 2 * at] = got[0]
            xw[LEAVES + 2 * at + 1] = got[1]
            mv[32 + at] = got[2]

        batched(4, 4, leaf_moments, keep_moments)

    @pl.when(inner)
    def _():
        pl.semaphore_wait(barrier, 12)
        start(sent[:1])

    get_up.wait()
    zero = jnp.zeros((RHS, RANK), F32)
    for height in range(1, LEVELS + 1):
        amount = LEAVES >> height
        base, child = row_of(height), row_of(height - 1)

        def lift(j):
            return nn(mv[32 + child // 2 + j], upv[pl.ds(child + 2 * j, 2)].reshape(128, RANK))

        def lift_two(j):
            return jnp.concatenate([lift(2 * j), lift(2 * j + 1)], axis=1).astype(BF)

        def keep_two(j, got):
            mv[32 + base // 2 + j] = got

        if amount == 1:
            root = lift(0)
            mv[63] = jnp.concatenate([root, zero], axis=1).astype(BF)
        else:
            batched(amount // 2, 4, lift_two, keep_two)

    get_dn = load(local_down, dnv)
    get_nb = [load(near_block.at[pl.ds(4 * k, 4)], nbv.at[pl.ds(4 * k, 4)]) for k in range(8)]
    get_cp = [load(local_coupling.at[pl.ds(9 * k, 9)], cpv.at[pl.ds(9 * k, 9)]) for k in range(7)]
    get_rb = load(row_basis, rbv)

    lifted = nn(root.astype(BF), upv[62])
    rx[x] = jnp.where(low == (x < 2), jnp.concatenate([lifted, lifted], axis=1), 0.0).astype(BF)

    gone_x = [remote(rx.at[x], rx.at[x], rxsend.at[0], rxrecv.at[0], other)] + [
        remote(rx.at[x], rx.at[x], rxsend.at[1 + k], rxrecv.at[1 + x // 3], p) for k, p in enumerate(middle)
    ]

    @pl.when(inner)
    def _():
        gone_x[0].start()

    @pl.when(outer)
    def _():
        gone_x[1].start()
        gone_x[2].start()

    moved = [
        beside(
            mv.at[pl.ds(32 + 16 * k, 16)],
            lambda side: mv.at[pl.ds(32 * side + 16 * k, 16)],
            msend.at[k],
            mrecv.at[k],
        )
        for k in range(2)
    ]
    start(moved)
    pl.when(inner)(lambda: start(sent[1:XFIRST]))
    start(sent[XFIRST:-2])
    pl.when((d < 127) & jnp.logical_not(relay3))(sent[-2][0].start)
    pl.when((d < 127) & jnp.logical_not(relay3 | last15))(sent[-1][0].start)
    for copies in sent[-2:]:
        pl.when((d > 0) & jnp.logical_not(first0))(copies[1].start)

    @pl.when(first0)
    def _():
        pl.semaphore_wait(hello, 1)
        start(sent[:XFIRST] + moved + sent[XFIRST:], late=True)


    get_at[0].wait()
    t = lax.broadcasted_iota(jnp.int32, (8, 63), 1)
    f = lax.broadcasted_iota(jnp.int32, (8, 63), 0)
    amount = jnp.full((8, 63), LEAVES, jnp.int32)
    for height in range(1, LEVELS + 1):
        amount = jnp.where(t < row_of(height), amount, LEAVES >> height)
    q = far_raw[...] - (d - 1) * amount
    window = (q >= amount).astype(jnp.int32) + (q >= 2 * amount).astype(jnp.int32)
    row = 64 - 2 * amount + (q & (amount - 1))
    far_row[...] = jnp.zeros((8, 64), jnp.int32)
    far_row[:, 0:63] = ((row + f) & 1) * 128 + window * 32 + (row >> 1)
    get_far = pltpu.make_async_copy(far_row, far_at, lsem.at[len(loads)])
    get_far.start()

    get_dn.wait()

    def extend_level(height):
        amount = LEAVES >> height
        base, parent = row_of(height), row_of(height + 1)

        def below(above, j):
            return nt(above, dnv[pl.ds(base + 2 * j, 2)].reshape(128, RANK)).astype(BF)

        if amount == 2:
            path[base // 2] = below(dnv[62].T, 0)
        else:

            def extend(j):
                above = path[parent // 2 + j]
                return below(above[:, :64], 2 * j), below(above[:, 64:], 2 * j + 1)

            def keep(j, got):
                path[base // 2 + 2 * j] = got[0]
                path[base // 2 + 2 * j + 1] = got[1]

            batched(amount // 4, 4, extend, keep)

    for height in range(LEVELS - 1, -1, -1):
        extend_level(height)

    get_uu.wait()
    gone_z = [remote(rz.at[z], rz.at[z], rzsend.at[k], rzrecv.at[k], p) for k, p in enumerate(by_z)]

    @pl.when(inner)
    def _():
        for k in range(3):
            remote(rx.at[k], rx.at[k], rxsend.at[k], rxrecv.at[k], other).wait_recv()
        first = (
            (rx[0].astype(F32) + rx[1].astype(F32)) + (rx[2].astype(F32) + rx[3].astype(F32))
        ).astype(BF)
        rz[z, 0] = first
        second = nn(first, uuv[pl.ds(2 * z, 2)].reshape(128, RANK))
        rz[z, 1] = jnp.where(low == (z % 2 == 0), jnp.concatenate([second, second], axis=1), 0.0).astype(BF)
        for copy in gone_z:
            copy.start()

    def near_own(i):
        return nt(xw[LEAVES + i], nbv[i, 0])

    def keep_own(i, got):
        acc[:, lanes(256 * i, 256)] = got

    for k in range(4):
        get_nb[k].wait()
        batched(4, OWN, lambda i: near_own(4 * k + i), lambda i, got: keep_own(4 * k + i, got))

    gone_y = [remote(rg.at[g], rg.at[g], rgsend.at[k], rgrecv.at[k], p) for k, p in enumerate(by_y + [twin])]

    @pl.when(inner)
    def _():
        for copy in gone_z:
            copy.wait_recv()
        for k in range(4):
            rg[g, k] = rz[k, 0]
        thirds = []
        for k in range(2):
            pair = (rz[2 * k, 1].astype(F32) + rz[2 * k + 1, 1].astype(F32)).astype(BF)
            rg[g, 4 + k] = pair
            thirds.append(nn(pair, uuv[8 + 2 * k : 10 + 2 * k].reshape(128, RANK)))
        third = jnp.concatenate(thirds, axis=1).astype(BF)
        rg[g, 6] = third
        top = nn(third, uuv[12:14].reshape(128, RANK))
        rg[g, 7] = jnp.concatenate([top, zero], axis=1).astype(BF)
        for copy in gone_y:
            copy.start()

    for k in range(4, 8):
        get_nb[k].wait()
        batched(4, OWN, lambda i: near_own(4 * k + i), lambda i, got: keep_own(4 * k + i, got))

    get_rb.wait()

    def reach(i):
        pair = path[i]
        return nn(pair[:, :64], rbv[2 * i]).astype(BF), nn(pair[:, 64:], rbv[2 * i + 1]).astype(BF)

    def keep_reach(i, got):
        qv[:, lanes(512 * i, 256)] = got[0]
        qv[:, lanes(512 * i + 256, 256)] = got[1]

    batched(16, REACH, reach, keep_reach)

    @pl.when(relay3)
    def _():
        to_relay.wait_recv()
        from_relay.start()
        sent[-2][0].start()
        sent[-1][0].start()

    for copy in get_ud:
        copy.wait()
    down1 = udv[0]
    down2 = nn(down1, udv[1]).astype(BF)
    down3 = nn(down2, udv[2]).astype(BF)

    for copies in moved:
        arrive(copies)

    def turn(i):
        pair = mv[i]
        return jnp.concatenate([pair[:, 64:], pair[:, :64]], axis=1)

    def keep_turn(i, got):
        mv[128 + i] = got

    batched(96, TURN, turn, keep_turn)
    get_far.wait()
    for copy in get_cp:
        copy.wait()

    def couple(t):
        total = None
        for q in range(2):
            moments = jnp.concatenate(
                [
                    jnp.where(low, mv[far_at[4 * q + 2 * j, t]], mv[far_at[4 * q + 2 * j + 1, t]])
                    for j in range(2)
                ],
                axis=1,
            )
            blocks = jnp.concatenate([cpv[t, 4 * q + j] for j in range(4)], axis=1)
            term = nt(moments, blocks)
            total = term if total is None else total + term
        return total

    def couple_two(j):
        return jnp.concatenate([couple(2 * j), couple(2 * j + 1)], axis=1)

    def keep_couple(j, got):
        far[j] = got

    batched(32, FAR, couple_two, keep_couple)

    dloc[31] = far[31].astype(BF)
    for height in range(LEVELS - 1, -1, -1):
        amount = LEAVES >> height
        base, parent = row_of(height), row_of(height + 1)

        def below(above, j):
            pair = dnv[pl.ds(base + 2 * j, 2)].reshape(128, RANK)
            return (far[base // 2 + j] + nt(above, pair)).astype(BF)

        if amount == 2:
            dloc[base // 2] = below(dloc[31][:, :64], 0)
        else:

            def descend(j):
                above = dloc[parent // 2 + j]
                return below(above[:, :64], 2 * j), below(above[:, 64:], 2 * j + 1)

            def keep_descend(j, got):
                dloc[base // 2 + 2 * j] = got[0]
                dloc[base // 2 + 2 * j + 1] = got[1]

            batched(amount // 4, 4, descend, keep_descend)

    def local(i):
        pair = dloc[i]
        return [
            acc[:, lanes(512 * i + 256 * k, 256)] + nn(pair[:, 64 * k : 64 * (k + 1)], rbv[2 * i + k])
            for k in range(2)
        ]

    def keep_rest(i, got):
        for k in range(2):
            acc[:, lanes(512 * i + 256 * k, 256)] = got[k]

    batched(16, 8, local, keep_rest)

    get_at[1].wait()
    for copy in get_uc:
        copy.wait()
    passed = []
    for k in range(3):
        from_y = ((y + 3 - k) % 4) * 2 + core
        passed.append(remote(rg.at[from_y], rg.at[from_y], rgsend.at[4 + k], rgrecv.at[4 + k], twin))
    gone_p = remote(pv, pv, psend, precv, helped)

    @pl.when(inner)
    def _():
        for k in (0, 2, 1):
            gone_y[k].wait_recv()
            passed[k].start()
        gone_y[3].wait_recv()
        for copy in passed:
            copy.wait_recv()
        terms = []
        for k in range(1, 5):
            amount = 16 >> k
            row = 16 - 2 * amount + s // 2**k

            def pick(f):
                p = ufar_at[f, row]
                group, j = p >> (4 - k), p & (amount - 1)
                pair = rg[group, (0, 4, 6, 7)[k - 1] + (j >> 1)]
                pair = pair.astype(F32)
                turned = jnp.concatenate([pair[:, 64:], pair[:, :64]], axis=1)
                keep = (1 - ((j + f) & 1)).astype(F32)
                return pair * keep + turned * (1.0 - keep)

            total = None
            for q in range(2):
                moments = jnp.concatenate(
                    [jnp.where(low, pick(4 * q + 2 * j), pick(4 * q + 2 * j + 1)) for j in range(2)], axis=1
                ).astype(BF)
                blocks = jnp.concatenate([ucv[k - 1, 4 * q + j] for j in range(4)], axis=1)
                term = nt(moments, blocks)
                total = term if total is None else total + term
            terms.append(total)
        parent = (
            terms[0]
            + nt(terms[1].astype(BF), down1)
            + nt(terms[2].astype(BF), down2)
            + nt(terms[3].astype(BF), down3)
        ).astype(BF)
        pv[...] = jnp.concatenate([parent, parent], axis=1)
        gone_p.start()

    get_at[2].wait()
    for copies, (start, size) in zip(sent, XPARTS):
        arrive(copies)

        def window(i):
            part = lanes(start + LEAF * i, LEAF)
            return xin[0, :, part], xin[1, :, part]

        def keep_window(i, got):
            xw[start // LEAF + i] = got[0]
            xw[2 * LEAVES + start // LEAF + i] = got[1]

        batched(size // LEAF, 4, window, keep_window)

    def add_near(i, k, total):
        leaf = 2 * i + k
        for n in (1, 2):
            q = (near_at[n, leaf] - (d - 1) * LEAVES) & 127
            total = total + nt(xw[q], nbv[leaf, n])
        return total

    upper_first = inner

    @pl.when(upper_first)
    def _():
        parent = pv[...][:, :64]

        def rest(i):
            above = nn(parent, qv[:, lanes(512 * i, 512)])
            return [
                add_near(
                    i, k, acc[:, lanes(512 * i + 256 * k, 256)] + above[:, 256 * k : 256 * (k + 1)]
                ).astype(BF)
                for k in range(2)
            ]

        def keep_out(i, got):
            for k in range(2):
                out[:, lanes(512 * i + 256 * k, 256)] = got[k]

        batched(16, REST, rest, keep_out)

    @pl.when(jnp.logical_not(upper_first))
    def _():
        def rest(i):
            return [add_near(i, k, acc[:, lanes(512 * i + 256 * k, 256)]) for k in range(2)]

        batched(16, REST, rest, keep_rest)
        gone_p.wait_recv()
        parent = pv[...][:, :64]

        def finish(i):
            part = lanes(512 * i, 512)
            return (acc[:, part] + nn(parent, qv[:, part])).astype(BF)

        def keep_finish(i, got):
            out[:, lanes(512 * i, 512)] = got

        batched(16, FINISH, finish, keep_finish)

    for copies in sent[:-1]:
        leave(copies)
    pl.when((d < 127) & jnp.logical_not(last15))(sent[-1][0].wait_send)
    pl.when(d > 0)(sent[-1][1].wait_send)
    pl.when(last15)(to_relay.wait_send)
    pl.when(relay3)(from_relay.wait_send)
    for copies in moved:
        leave(copies)

    @pl.when(inner)
    def _():
        for copy in [gone_x[0]] + gone_z + gone_y + passed + [gone_p]:
            copy.wait_send()

    @pl.when(outer)
    def _():
        gone_x[1].wait_send()
        gone_x[2].wait_send()


def on_device(
    charges,
    column_basis,
    row_basis,
    local_up,
    local_down,
    local_far,
    local_coupling,
    upper_up,
    upper_down,
    upper_far,
    upper_coupling,
    near_source,
    near_block,
):
    dma = pltpu.SemaphoreType.DMA
    vmem = pltpu.VMEM
    anywhere = pl.BlockSpec(memory_space=pl.ANY)
    return pl.pallas_call(
        kernel,
        out_shape=pltpu.VMEM((RHS, COLS), BF),
        in_specs=[anywhere] * 13,
        out_specs=pl.BlockSpec(memory_space=vmem),
        scratch_shapes=[
            vmem((RHS, COLS), BF),
            vmem((2, RHS, COLS), BF),
            vmem((4 * LEAVES, RHS, LEAF), BF),
            vmem((LEAVES, RANK, LEAF), BF),
            vmem((LEAVES, RANK, LEAF), BF),
            vmem((63, RANK, RANK), BF),
            vmem((63, RANK, RANK), BF),
            vmem((64, 8, RANK, RANK), BF),
            vmem((14, RANK, RANK), BF),
            vmem((3, RANK, RANK), BF),
            vmem((4, 8, RANK, RANK), BF),
            vmem((LEAVES, 3, LEAF, LEAF), BF),
            vmem((256, RHS, 128), BF),
            vmem((4, RHS, 128), BF),
            vmem((4, 2, RHS, 128), BF),
            vmem((8, 8, RHS, 128), BF),
            vmem((RHS, 128), BF),
            vmem((RHS, COLS), F32),
            vmem((32, RHS, 128), F32),
            vmem((32, RHS, 128), BF),
            vmem((32, RANK, 128), BF),
            vmem((RANK, COLS), BF),
            vmem((8, 63), jnp.int32),
            vmem((8, 64), jnp.int32),
            pltpu.SMEM((8, 64), jnp.int32),
            pltpu.SMEM((8, 15), jnp.int32),
            pltpu.SMEM((3, LEAVES), jnp.int32),
            dma((40,)),
            dma((len(XPARTS), 2)),
            dma((len(XPARTS), 2)),
            dma((2, 2)),
            dma((2, 2)),
            dma((3,)),
            dma((3,)),
            dma((3,)),
            dma((3,)),
            dma((7,)),
            dma((7,)),
            dma,
            dma,
            pltpu.SemaphoreType.REGULAR,
            vmem((RHS, XPARTS[-1][1]), BF),
            dma((2,)),
            dma,
        ],
        compiler_params=pltpu.CompilerParams(
            collective_id=0, has_side_effects=True, vmem_limit_bytes=60 * 2**20
        ),
        name="h2_product",
    )(
        charges,
        column_basis,
        row_basis,
        local_up,
        local_down,
        local_far.T,
        local_coupling,
        upper_up,
        upper_down,
        upper_far.T,
        upper_coupling,
        near_source.T,
        near_block,
    )


def solution(mesh):
    both = ("grp", "sub")
    in_specs = (
        P(None, both),
        P(both, None, None),
        P(both, None, None),
        P(both, None, None),
        P(both, None, None),
        P(both, None),
        P(both, None, None, None),
        P("grp", None, None),
        P("grp", None, None),
        P("grp", None),
        P("grp", None, None, None),
        P(both, None),
        P(both, None, None, None),
    )
    return jax.shard_map(
        on_device, mesh=mesh, in_specs=in_specs, out_specs=P(None, both), check_vma=False
    )
```

```python
import functools

import jax
import jax.numpy as jnp
from jax import lax
from jax.experimental import pallas as pl
from jax.experimental.pallas import tpu as pltpu
from jax.sharding import PartitionSpec as P

MESH = pl.DeviceIdType.MESH
BF = jnp.bfloat16
F32 = jnp.float32
RHS = 32
LEAVES = 32
LEAF = 256
RANK = 64
LEVELS = 5
COLS = LEAVES * LEAF
XPARTS = ((0, 1024), (1024, 1024), (2048, 2048), (4096, 3072), (7168, 1024))
XFIRST = 2
OWN, REACH, TURN, FAR, REST, FINISH = 4, 16, 96, 16, 16, 16


def nt(a, b):
    return lax.dot_general(a, b, (((1,), (1,)), ((), ())), preferred_element_type=F32)


def nn(a, b):
    return lax.dot_general(a, b, (((1,), (0,)), ((), ())), preferred_element_type=F32)


def lanes(start, size):
    return pl.ds(pl.multiple_of(start, 128), size)


def loop(count, body, unroll):
    def step(i, carry):
        body(i)
        return carry

    lax.fori_loop(0, count, step, 0, unroll=min(unroll, count))


def batched(count, width, compute, store):
    width = min(width, count)

    def body(b):
        got = [compute(width * b + j) for j in range(width)]
        for j in range(width):
            store(width * b + j, got[j])

    loop(count // width, body, 1)


def row_of(height):
    return 64 - 2 * (LEAVES >> height)


def kernel(
    charges,
    column_basis,
    row_basis,
    local_up,
    local_down,
    local_far,
    local_coupling,
    upper_up,
    upper_down,
    upper_far,
    upper_coupling,
    near_source,
    near_block,
    out,
    cx,
    xin,
    xw,
    cbv,
    rbv,
    upv,
    dnv,
    cpv,
    uuv,
    udv,
    ucv,
    nbv,
    mv,
    rx,
    rz,
    rg,
    pv,
    acc,
    far,
    dloc,
    path,
    qv,
    far_raw,
    far_row,
    far_at,
    ufar_at,
    near_at,
    lsem,
    xsend,
    xrecv,
    msend,
    mrecv,
    rxsend,
    rxrecv,
    rzsend,
    rzrecv,
    rgsend,
    rgrecv,
    psend,
    precv,
    hello,
    hop,
    hsend,
    hrecv,
):
    g = lax.axis_index("grp")
    s = lax.axis_index("sub")
    d = g * 16 + s
    z = s // 4
    x = s % 4

    def place(e):
        return (e // 16, e % 16)

    sides = ((d < 127, place((d + 1) % 128)), (d > 0, place((d + 127) % 128)))
    inner = (x == 1) | (x == 2)
    outer = jnp.logical_not(inner)
    y, core = g // 2, g % 2
    middle = [(g, z * 4 + 1), (g, z * 4 + 2)]
    other = (g, z * 4 + 3 - x)
    helped = (g, z * 4 + 3 * (x // 2))
    by_z = [(g, ((z + k) % 4) * 4 + x) for k in range(1, 4)]
    by_y = [(((y + k) % 4) * 2 + core, s) for k in range(1, 4)]
    twin = (2 * y + 1 - core, s)

    first0 = (s == 0) & (g > 0)
    last15 = (s == 15) & (g < 7)
    relay3 = (s == 3) & (g < 7)
    before15 = (z == 3) & (g < 7) & inner
    later = first0 | last15

    barrier = pltpu.get_barrier_semaphore()

    def greet(peer):
        pl.semaphore_signal(barrier, inc=1, device_id=peer, device_id_type=MESH)

    pl.when((d < 127) & jnp.logical_not(last15 | before15 & (x == 2)))(functools.partial(greet, sides[0][1]))
    pl.when(d > 0)(functools.partial(greet, sides[1][1]))
    pl.when(first0)(functools.partial(greet, (g - 1, s + 3)))
    pl.when(relay3)(functools.partial(greet, (g, s + 12)))

    @pl.when(inner)
    def _():
        for peer in [other, (g, z * 4)] + by_z + by_y + [twin]:
            greet(peer)
        pl.when(jnp.logical_not(before15))(functools.partial(greet, (g, z * 4 + 3)))

    @pl.when(outer)
    def _():
        for peer in middle:
            greet(peer)

    loads = []

    def load(src, dst):
        copy = pltpu.make_async_copy(src, dst, lsem.at[len(loads)])
        copy.start()
        loads.append(copy)
        return copy

    get_x = [load(charges.at[:, pl.ds(4096 * k, 4096)], cx.at[:, pl.ds(4096 * k, 4096)]) for k in range(2)]
    get_cb = [load(column_basis.at[pl.ds(8 * k, 8)], cbv.at[pl.ds(8 * k, 8)]) for k in range(4)]
    get_up = load(local_up, upv)
    get_uu = load(upper_up, uuv)
    get_at = [load(local_far, far_raw), load(upper_far, ufar_at), load(near_source, near_at)]

    @pl.when(outer)
    def _():
        count = 2 + (d < 127).astype(jnp.int32) + ((d > 0) & (s > 0)).astype(jnp.int32)
        pl.semaphore_wait(barrier, jnp.where(last15, 2, count + relay3.astype(jnp.int32)))
        pl.when(last15)(lambda: pl.semaphore_signal(hello, inc=1, device_id=sides[0][1], device_id_type=MESH))

    def remote(src, dst, ssem, rsem, peer):
        return pltpu.make_async_remote_copy(
            src_ref=src, dst_ref=dst, send_sem=ssem, recv_sem=rsem, device_id=peer, device_id_type=MESH
        )

    def send(src, dst, ssem, rsem, peer):
        copy = remote(src, dst, ssem, rsem, peer)
        copy.start()
        return copy

    def beside(src, dst, ssem, rsem):
        return [remote(src, dst(2 * k), ssem.at[k], rsem.at[k], peer) for k, (_, peer) in enumerate(sides)]

    def start(batches, late=False):
        for k, (there, _) in enumerate(sides):
            if late:
                go = later if k else False
            else:
                go = there & jnp.logical_not(later) if k else there

            if go is not False:

                @pl.when(go)
                def _():
                    for copies in batches:
                        copies[k].start()

    def arrive(copies):
        for (there, _), copy in zip((sides[1], sides[0]), copies):
            pl.when(there)(copy.wait_recv)

    def leave(copies):
        for (there, _), copy in zip(sides, copies):
            pl.when(there)(copy.wait_send)

    def charges_part(k):
        start, size = XPARTS[k]
        part = pl.ds(start, size)
        return beside(
            charges.at[:, part],
            lambda side: xin.at[side // 2, :, part],
            xsend.at[k],
            xrecv.at[k],
        )

    sent = [charges_part(k) for k in range(len(XPARTS))]
    part = pl.ds(*XPARTS[-1])
    to_relay = remote(charges.at[:, part], hop, hsend.at[0], hrecv, (g, z * 4 - 9))
    from_relay = remote(hop, xin.at[0, :, part], hsend.at[1], xrecv.at[len(XPARTS) - 1, 0], (g + 1, s - 3))
    pl.when(last15)(to_relay.start)
    pl.when(outer)(lambda: start(sent[:XFIRST]))

    get_ud = [
        load(upper_down.at[16 - (32 >> k) + s // 2**k], udv.at[k - 1]) for k in range(1, 4)
    ]
    get_uc = [
        load(upper_coupling.at[16 - (32 >> k) + s // 2**k], ucv.at[k - 1]) for k in range(1, 5)
    ]

    low = lax.broadcasted_iota(jnp.int32, (RHS, 128), 1) < 64

    for k in range(4):
        if k % 2 == 0:
            get_x[k // 2].wait()
        get_cb[k].wait()

        def leaf_moments(i):
            at = 4 * k + i
            one, two = cx[:, lanes(512 * at, 256)], cx[:, lanes(512 * at + 256, 256)]
            both = nt(jnp.concatenate([one, two], axis=0), cbv[pl.ds(2 * at, 2)].reshape(128, LEAF))
            return one, two, jnp.where(low, both[:RHS], both[RHS:]).astype(BF)

        def keep_moments(i, got):
            at = 4 * k + i
            xw[LEAVES + 2 * at] = got[0]
            xw[LEAVES + 2 * at + 1] = got[1]
            mv[32 + at] = got[2]

        batched(4, 4, leaf_moments, keep_moments)

    @pl.when(inner)
    def _():
        pl.semaphore_wait(barrier, 12)
        pl.when(before15)(lambda: pl.semaphore_signal(hello, inc=1, device_id=(g, 15), device_id_type=MESH))
        start(sent[:1])

    get_up.wait()
    zero = jnp.zeros((RHS, RANK), F32)
    for height in range(1, LEVELS + 1):
        amount = LEAVES >> height
        base, child = row_of(height), row_of(height - 1)

        def lift(j):
            return nn(mv[32 + child // 2 + j], upv[pl.ds(child + 2 * j, 2)].reshape(128, RANK))

        def lift_two(j):
            return jnp.concatenate([lift(2 * j), lift(2 * j + 1)], axis=1).astype(BF)

        def keep_two(j, got):
            mv[32 + base // 2 + j] = got

        if amount == 1:
            root = lift(0)
            mv[63] = jnp.concatenate([root, zero], axis=1).astype(BF)
        else:
            batched(amount // 2, 4, lift_two, keep_two)

    get_dn = load(local_down, dnv)
    get_nb = [load(near_block.at[pl.ds(4 * k, 4)], nbv.at[pl.ds(4 * k, 4)]) for k in range(8)]
    get_cp = [load(local_coupling.at[pl.ds(9 * k, 9)], cpv.at[pl.ds(9 * k, 9)]) for k in range(7)]
    get_rb = load(row_basis, rbv)

    lifted = nn(root.astype(BF), upv[62])
    rx[x] = jnp.where(low == (x < 2), jnp.concatenate([lifted, lifted], axis=1), 0.0).astype(BF)

    gone_x = [remote(rx.at[x], rx.at[x], rxsend.at[0], rxrecv.at[0], other)] + [
        remote(rx.at[x], rx.at[x], rxsend.at[1 + k], rxrecv.at[1 + x // 3], p) for k, p in enumerate(middle)
    ]

    @pl.when(inner)
    def _():
        gone_x[0].start()

    @pl.when(outer)
    def _():
        pl.when(last15)(lambda: pl.semaphore_wait(hello, 2))
        gone_x[1].start()
        gone_x[2].start()

    moved = [
        beside(
            mv.at[pl.ds(32 + 16 * k, 16)],
            lambda side: mv.at[pl.ds(32 * side + 16 * k, 16)],
            msend.at[k],
            mrecv.at[k],
        )
        for k in range(2)
    ]
    start(moved)
    pl.when(inner)(lambda: start(sent[1:XFIRST]))
    start(sent[XFIRST:-2])
    pl.when((d < 127) & jnp.logical_not(relay3))(sent[-2][0].start)
    pl.when((d < 127) & jnp.logical_not(relay3 | last15))(sent[-1][0].start)
    for copies in sent[-2:]:
        pl.when((d > 0) & jnp.logical_not(later))(copies[1].start)

    pl.when(first0)(lambda: pl.semaphore_wait(hello, 1))
    start(sent[:XFIRST] + moved + sent[XFIRST:], late=True)


    get_at[0].wait()
    t = lax.broadcasted_iota(jnp.int32, (8, 63), 1)
    f = lax.broadcasted_iota(jnp.int32, (8, 63), 0)
    amount = jnp.full((8, 63), LEAVES, jnp.int32)
    for height in range(1, LEVELS + 1):
        amount = jnp.where(t < row_of(height), amount, LEAVES >> height)
    q = far_raw[...] - (d - 1) * amount
    window = (q >= amount).astype(jnp.int32) + (q >= 2 * amount).astype(jnp.int32)
    row = 64 - 2 * amount + (q & (amount - 1))
    far_row[...] = jnp.zeros((8, 64), jnp.int32)
    far_row[:, 0:63] = ((row + f) & 1) * 128 + window * 32 + (row >> 1)
    get_far = pltpu.make_async_copy(far_row, far_at, lsem.at[len(loads)])
    get_far.start()

    get_dn.wait()

    def extend_level(height):
        amount = LEAVES >> height
        base, parent = row_of(height), row_of(height + 1)

        def below(above, j):
            return nt(above, dnv[pl.ds(base + 2 * j, 2)].reshape(128, RANK)).astype(BF)

        if amount == 2:
            path[base // 2] = below(dnv[62].T, 0)
        else:

            def extend(j):
                above = path[parent // 2 + j]
                return below(above[:, :64], 2 * j), below(above[:, 64:], 2 * j + 1)

            def keep(j, got):
                path[base // 2 + 2 * j] = got[0]
                path[base // 2 + 2 * j + 1] = got[1]

            batched(amount // 4, 4, extend, keep)

    for height in range(LEVELS - 1, -1, -1):
        extend_level(height)

    get_uu.wait()
    gone_z = [remote(rz.at[z], rz.at[z], rzsend.at[k], rzrecv.at[k], p) for k, p in enumerate(by_z)]

    @pl.when(inner)
    def _():
        for k in range(3):
            remote(rx.at[k], rx.at[k], rxsend.at[k], rxrecv.at[k], other).wait_recv()
        first = (
            (rx[0].astype(F32) + rx[1].astype(F32)) + (rx[2].astype(F32) + rx[3].astype(F32))
        ).astype(BF)
        rz[z, 0] = first
        second = nn(first, uuv[pl.ds(2 * z, 2)].reshape(128, RANK))
        rz[z, 1] = jnp.where(low == (z % 2 == 0), jnp.concatenate([second, second], axis=1), 0.0).astype(BF)
        for copy in gone_z:
            copy.start()

    def near_own(i):
        return nt(xw[LEAVES + i], nbv[i, 0])

    def keep_own(i, got):
        acc[:, lanes(256 * i, 256)] = got

    for k in range(4):
        get_nb[k].wait()
        batched(4, OWN, lambda i: near_own(4 * k + i), lambda i, got: keep_own(4 * k + i, got))

    gone_y = [remote(rg.at[g], rg.at[g], rgsend.at[k], rgrecv.at[k], p) for k, p in enumerate(by_y + [twin])]

    @pl.when(inner)
    def _():
        for copy in gone_z:
            copy.wait_recv()
        for k in range(4):
            rg[g, k] = rz[k, 0]
        thirds = []
        for k in range(2):
            pair = (rz[2 * k, 1].astype(F32) + rz[2 * k + 1, 1].astype(F32)).astype(BF)
            rg[g, 4 + k] = pair
            thirds.append(nn(pair, uuv[8 + 2 * k : 10 + 2 * k].reshape(128, RANK)))
        third = jnp.concatenate(thirds, axis=1).astype(BF)
        rg[g, 6] = third
        top = nn(third, uuv[12:14].reshape(128, RANK))
        rg[g, 7] = jnp.concatenate([top, zero], axis=1).astype(BF)
        for copy in gone_y:
            copy.start()

    for k in range(4, 8):
        get_nb[k].wait()
        batched(4, OWN, lambda i: near_own(4 * k + i), lambda i, got: keep_own(4 * k + i, got))

    get_rb.wait()

    def reach(i):
        pair = path[i]
        return nn(pair[:, :64], rbv[2 * i]).astype(BF), nn(pair[:, 64:], rbv[2 * i + 1]).astype(BF)

    def keep_reach(i, got):
        qv[:, lanes(512 * i, 256)] = got[0]
        qv[:, lanes(512 * i + 256, 256)] = got[1]

    batched(16, REACH, reach, keep_reach)

    @pl.when(relay3)
    def _():
        to_relay.wait_recv()
        from_relay.start()
        sent[-2][0].start()
        sent[-1][0].start()

    for copy in get_ud:
        copy.wait()
    down1 = udv[0]
    down2 = nn(down1, udv[1]).astype(BF)
    down3 = nn(down2, udv[2]).astype(BF)

    for copies in moved:
        arrive(copies)

    def turn(i):
        pair = mv[i]
        return jnp.concatenate([pair[:, 64:], pair[:, :64]], axis=1)

    def keep_turn(i, got):
        mv[128 + i] = got

    batched(96, TURN, turn, keep_turn)
    get_far.wait()
    for copy in get_cp:
        copy.wait()

    def couple(t):
        total = None
        for q in range(2):
            moments = jnp.concatenate(
                [
                    jnp.where(low, mv[far_at[4 * q + 2 * j, t]], mv[far_at[4 * q + 2 * j + 1, t]])
                    for j in range(2)
                ],
                axis=1,
            )
            blocks = jnp.concatenate([cpv[t, 4 * q + j] for j in range(4)], axis=1)
            term = nt(moments, blocks)
            total = term if total is None else total + term
        return total

    def couple_two(j):
        return jnp.concatenate([couple(2 * j), couple(2 * j + 1)], axis=1)

    def keep_couple(j, got):
        far[j] = got

    batched(32, FAR, couple_two, keep_couple)

    dloc[31] = far[31].astype(BF)
    for height in range(LEVELS - 1, -1, -1):
        amount = LEAVES >> height
        base, parent = row_of(height), row_of(height + 1)

        def below(above, j):
            pair = dnv[pl.ds(base + 2 * j, 2)].reshape(128, RANK)
            return (far[base // 2 + j] + nt(above, pair)).astype(BF)

        if amount == 2:
            dloc[base // 2] = below(dloc[31][:, :64], 0)
        else:

            def descend(j):
                above = dloc[parent // 2 + j]
                return below(above[:, :64], 2 * j), below(above[:, 64:], 2 * j + 1)

            def keep_descend(j, got):
                dloc[base // 2 + 2 * j] = got[0]
                dloc[base // 2 + 2 * j + 1] = got[1]

            batched(amount // 4, 4, descend, keep_descend)

    def local(i):
        pair = dloc[i]
        return [
            acc[:, lanes(512 * i + 256 * k, 256)] + nn(pair[:, 64 * k : 64 * (k + 1)], rbv[2 * i + k])
            for k in range(2)
        ]

    def keep_rest(i, got):
        for k in range(2):
            acc[:, lanes(512 * i + 256 * k, 256)] = got[k]

    batched(16, 8, local, keep_rest)

    get_at[1].wait()
    for copy in get_uc:
        copy.wait()
    passed = []
    for k in range(3):
        from_y = ((y + 3 - k) % 4) * 2 + core
        passed.append(remote(rg.at[from_y], rg.at[from_y], rgsend.at[4 + k], rgrecv.at[4 + k], twin))
    gone_p = remote(pv, pv, psend, precv, helped)

    @pl.when(inner)
    def _():
        for k in (0, 2, 1):
            gone_y[k].wait_recv()
            passed[k].start()
        gone_y[3].wait_recv()
        for copy in passed:
            copy.wait_recv()
        terms = []
        for k in range(1, 5):
            amount = 16 >> k
            row = 16 - 2 * amount + s // 2**k

            def pick(f):
                p = ufar_at[f, row]
                group, j = p >> (4 - k), p & (amount - 1)
                pair = rg[group, (0, 4, 6, 7)[k - 1] + (j >> 1)]
                pair = pair.astype(F32)
                turned = jnp.concatenate([pair[:, 64:], pair[:, :64]], axis=1)
                keep = (1 - ((j + f) & 1)).astype(F32)
                return pair * keep + turned * (1.0 - keep)

            total = None
            for q in range(2):
                moments = jnp.concatenate(
                    [jnp.where(low, pick(4 * q + 2 * j), pick(4 * q + 2 * j + 1)) for j in range(2)], axis=1
                ).astype(BF)
                blocks = jnp.concatenate([ucv[k - 1, 4 * q + j] for j in range(4)], axis=1)
                term = nt(moments, blocks)
                total = term if total is None else total + term
            terms.append(total)
        parent = (
            terms[0]
            + nt(terms[1].astype(BF), down1)
            + nt(terms[2].astype(BF), down2)
            + nt(terms[3].astype(BF), down3)
        ).astype(BF)
        pv[...] = jnp.concatenate([parent, parent], axis=1)
        gone_p.start()

    get_at[2].wait()
    for copies, (start, size) in zip(sent, XPARTS):
        arrive(copies)

        def window(i):
            part = lanes(start + LEAF * i, LEAF)
            return xin[0, :, part], xin[1, :, part]

        def keep_window(i, got):
            xw[start // LEAF + i] = got[0]
            xw[2 * LEAVES + start // LEAF + i] = got[1]

        batched(size // LEAF, 4, window, keep_window)

    def add_near(i, k, total):
        leaf = 2 * i + k
        for n in (1, 2):
            q = (near_at[n, leaf] - (d - 1) * LEAVES) & 127
            total = total + nt(xw[q], nbv[leaf, n])
        return total

    upper_first = inner

    @pl.when(upper_first)
    def _():
        parent = pv[...][:, :64]

        def rest(i):
            above = nn(parent, qv[:, lanes(512 * i, 512)])
            return [
                add_near(
                    i, k, acc[:, lanes(512 * i + 256 * k, 256)] + above[:, 256 * k : 256 * (k + 1)]
                ).astype(BF)
                for k in range(2)
            ]

        def keep_out(i, got):
            for k in range(2):
                out[:, lanes(512 * i + 256 * k, 256)] = got[k]

        batched(16, REST, rest, keep_out)

    @pl.when(jnp.logical_not(upper_first))
    def _():
        def rest(i):
            return [add_near(i, k, acc[:, lanes(512 * i + 256 * k, 256)]) for k in range(2)]

        batched(16, REST, rest, keep_rest)
        gone_p.wait_recv()
        parent = pv[...][:, :64]

        def finish(i):
            part = lanes(512 * i, 512)
            return (acc[:, part] + nn(parent, qv[:, part])).astype(BF)

        def keep_finish(i, got):
            out[:, lanes(512 * i, 512)] = got

        batched(16, FINISH, finish, keep_finish)

    for copies in sent[:-1]:
        leave(copies)
    pl.when((d < 127) & jnp.logical_not(last15))(sent[-1][0].wait_send)
    pl.when(d > 0)(sent[-1][1].wait_send)
    pl.when(last15)(to_relay.wait_send)
    pl.when(relay3)(from_relay.wait_send)
    for copies in moved:
        leave(copies)

    @pl.when(inner)
    def _():
        for copy in [gone_x[0]] + gone_z + gone_y + passed + [gone_p]:
            copy.wait_send()

    @pl.when(outer)
    def _():
        gone_x[1].wait_send()
        gone_x[2].wait_send()


def on_device(
    charges,
    column_basis,
    row_basis,
    local_up,
    local_down,
    local_far,
    local_coupling,
    upper_up,
    upper_down,
    upper_far,
    upper_coupling,
    near_source,
    near_block,
):
    dma = pltpu.SemaphoreType.DMA
    vmem = pltpu.VMEM
    anywhere = pl.BlockSpec(memory_space=pl.ANY)
    return pl.pallas_call(
        kernel,
        out_shape=pltpu.VMEM((RHS, COLS), BF),
        in_specs=[anywhere] * 13,
        out_specs=pl.BlockSpec(memory_space=vmem),
        scratch_shapes=[
            vmem((RHS, COLS), BF),
            vmem((2, RHS, COLS), BF),
            vmem((4 * LEAVES, RHS, LEAF), BF),
            vmem((LEAVES, RANK, LEAF), BF),
            vmem((LEAVES, RANK, LEAF), BF),
            vmem((63, RANK, RANK), BF),
            vmem((63, RANK, RANK), BF),
            vmem((64, 8, RANK, RANK), BF),
            vmem((14, RANK, RANK), BF),
            vmem((3, RANK, RANK), BF),
            vmem((4, 8, RANK, RANK), BF),
            vmem((LEAVES, 3, LEAF, LEAF), BF),
            vmem((256, RHS, 128), BF),
            vmem((4, RHS, 128), BF),
            vmem((4, 2, RHS, 128), BF),
            vmem((8, 8, RHS, 128), BF),
            vmem((RHS, 128), BF),
            vmem((RHS, COLS), F32),
            vmem((32, RHS, 128), F32),
            vmem((32, RHS, 128), BF),
            vmem((32, RANK, 128), BF),
            vmem((RANK, COLS), BF),
            vmem((8, 63), jnp.int32),
            vmem((8, 64), jnp.int32),
            pltpu.SMEM((8, 64), jnp.int32),
            pltpu.SMEM((8, 15), jnp.int32),
            pltpu.SMEM((3, LEAVES), jnp.int32),
            dma((40,)),
            dma((len(XPARTS), 2)),
            dma((len(XPARTS), 2)),
            dma((2, 2)),
            dma((2, 2)),
            dma((3,)),
            dma((3,)),
            dma((3,)),
            dma((3,)),
            dma((7,)),
            dma((7,)),
            dma,
            dma,
            pltpu.SemaphoreType.REGULAR,
            vmem((RHS, XPARTS[-1][1]), BF),
            dma((2,)),
            dma,
        ],
        compiler_params=pltpu.CompilerParams(
            collective_id=0, has_side_effects=True, vmem_limit_bytes=60 * 2**20
        ),
        name="h2_product",
    )(
        charges,
        column_basis,
        row_basis,
        local_up,
        local_down,
        local_far.T,
        local_coupling,
        upper_up,
        upper_down,
        upper_far.T,
        upper_coupling,
        near_source.T,
        near_block,
    )


def solution(mesh):
    both = ("grp", "sub")
    in_specs = (
        P(None, both),
        P(both, None, None),
        P(both, None, None),
        P(both, None, None),
        P(both, None, None),
        P(both, None),
        P(both, None, None, None),
        P("grp", None, None),
        P("grp", None, None),
        P("grp", None),
        P("grp", None, None, None),
        P(both, None),
        P(both, None, None, None),
    )
    return jax.shard_map(
        on_device, mesh=mesh, in_specs=in_specs, out_specs=P(None, both), check_vma=False
    )
```

```python
import functools

import jax
import jax.numpy as jnp
from jax import lax
from jax.experimental import pallas as pl
from jax.experimental.pallas import tpu as pltpu
from jax.sharding import PartitionSpec as P

MESH = pl.DeviceIdType.MESH
BF = jnp.bfloat16
F32 = jnp.float32
RHS = 32
LEAVES = 32
LEAF = 256
RANK = 64
LEVELS = 5
COLS = LEAVES * LEAF
XPARTS = ((0, 1024), (1024, 1024), (2048, 2048), (4096, 2560), (6656, 1536))
XFIRST = 2
OWN, REACH, TURN, FAR, REST, FINISH = 4, 16, 96, 16, 16, 16


def nt(a, b):
    return lax.dot_general(a, b, (((1,), (1,)), ((), ())), preferred_element_type=F32)


def nn(a, b):
    return lax.dot_general(a, b, (((1,), (0,)), ((), ())), preferred_element_type=F32)


def lanes(start, size):
    return pl.ds(pl.multiple_of(start, 128), size)


def loop(count, body, unroll):
    def step(i, carry):
        body(i)
        return carry

    lax.fori_loop(0, count, step, 0, unroll=min(unroll, count))


def batched(count, width, compute, store):
    width = min(width, count)

    def body(b):
        got = [compute(width * b + j) for j in range(width)]
        for j in range(width):
            store(width * b + j, got[j])

    loop(count // width, body, 1)


def row_of(height):
    return 64 - 2 * (LEAVES >> height)


def kernel(
    charges,
    column_basis,
    row_basis,
    local_up,
    local_down,
    local_far,
    local_coupling,
    upper_up,
    upper_down,
    upper_far,
    upper_coupling,
    near_source,
    near_block,
    out,
    cx,
    xin,
    xw,
    cbv,
    rbv,
    upv,
    dnv,
    cpv,
    uuv,
    udv,
    ucv,
    nbv,
    mv,
    rx,
    rz,
    rg,
    pv,
    acc,
    far,
    dloc,
    path,
    qv,
    far_raw,
    far_row,
    far_at,
    ufar_at,
    near_at,
    lsem,
    xsend,
    xrecv,
    msend,
    mrecv,
    rxsend,
    rxrecv,
    rzsend,
    rzrecv,
    rgsend,
    rgrecv,
    psend,
    precv,
    hello,
    hop,
    hsend,
    hrecv,
):
    g = lax.axis_index("grp")
    s = lax.axis_index("sub")
    d = g * 16 + s
    z = s // 4
    x = s % 4

    def place(e):
        return (e // 16, e % 16)

    sides = ((d < 127, place((d + 1) % 128)), (d > 0, place((d + 127) % 128)))
    inner = (x == 1) | (x == 2)
    outer = jnp.logical_not(inner)
    y, core = g // 2, g % 2
    middle = [(g, z * 4 + 1), (g, z * 4 + 2)]
    other = (g, z * 4 + 3 - x)
    helped = (g, z * 4 + 3 * (x // 2))
    by_z = [(g, ((z + k) % 4) * 4 + x) for k in range(1, 4)]
    by_y = [(((y + k) % 4) * 2 + core, s) for k in range(1, 4)]
    twin = (2 * y + 1 - core, s)

    first0 = (s == 0) & (g > 0)
    last15 = (s == 15) & (g < 7)
    relay3 = (s == 3) & (g < 7)
    before15 = (z == 3) & (g < 7) & inner
    later = first0 | last15

    barrier = pltpu.get_barrier_semaphore()

    def greet(peer):
        pl.semaphore_signal(barrier, inc=1, device_id=peer, device_id_type=MESH)

    pl.when((d < 127) & jnp.logical_not(last15 | before15 & (x == 2)))(functools.partial(greet, sides[0][1]))
    pl.when(d > 0)(functools.partial(greet, sides[1][1]))
    pl.when(first0)(functools.partial(greet, (g - 1, s + 3)))
    pl.when(relay3)(functools.partial(greet, (g, s + 12)))

    @pl.when(inner)
    def _():
        for peer in [other, (g, z * 4)] + by_z + by_y + [twin]:
            greet(peer)
        pl.when(jnp.logical_not(before15))(functools.partial(greet, (g, z * 4 + 3)))

    @pl.when(outer)
    def _():
        for peer in middle:
            greet(peer)

    loads = []

    def load(src, dst):
        copy = pltpu.make_async_copy(src, dst, lsem.at[len(loads)])
        copy.start()
        loads.append(copy)
        return copy

    get_x = [load(charges.at[:, pl.ds(4096 * k, 4096)], cx.at[:, pl.ds(4096 * k, 4096)]) for k in range(2)]
    get_cb = [load(column_basis.at[pl.ds(8 * k, 8)], cbv.at[pl.ds(8 * k, 8)]) for k in range(4)]
    get_up = load(local_up, upv)
    get_uu = load(upper_up, uuv)
    get_at = [load(local_far, far_raw), load(upper_far, ufar_at), load(near_source, near_at)]

    @pl.when(outer)
    def _():
        count = 2 + (d < 127).astype(jnp.int32) + ((d > 0) & (s > 0)).astype(jnp.int32)
        pl.semaphore_wait(barrier, jnp.where(last15, 2, count + relay3.astype(jnp.int32)))
        pl.when(last15)(lambda: pl.semaphore_signal(hello, inc=1, device_id=sides[0][1], device_id_type=MESH))

    def remote(src, dst, ssem, rsem, peer):
        return pltpu.make_async_remote_copy(
            src_ref=src, dst_ref=dst, send_sem=ssem, recv_sem=rsem, device_id=peer, device_id_type=MESH
        )

    def send(src, dst, ssem, rsem, peer):
        copy = remote(src, dst, ssem, rsem, peer)
        copy.start()
        return copy

    def beside(src, dst, ssem, rsem):
        return [remote(src, dst(2 * k), ssem.at[k], rsem.at[k], peer) for k, (_, peer) in enumerate(sides)]

    def start(batches, late=False):
        for k, (there, _) in enumerate(sides):
            if late:
                go = later if k else False
            else:
                go = there & jnp.logical_not(later) if k else there

            if go is not False:

                @pl.when(go)
                def _():
                    for copies in batches:
                        copies[k].start()

    def arrive(copies):
        for (there, _), copy in zip((sides[1], sides[0]), copies):
            pl.when(there)(copy.wait_recv)

    def leave(copies):
        for (there, _), copy in zip(sides, copies):
            pl.when(there)(copy.wait_send)

    def charges_part(k):
        start, size = XPARTS[k]
        part = pl.ds(start, size)
        return beside(
            charges.at[:, part],
            lambda side: xin.at[side // 2, :, part],
            xsend.at[k],
            xrecv.at[k],
        )

    sent = [charges_part(k) for k in range(len(XPARTS))]
    part = pl.ds(*XPARTS[-1])
    to_relay = remote(charges.at[:, part], hop, hsend.at[0], hrecv, (g, z * 4 - 9))
    from_relay = remote(hop, xin.at[0, :, part], hsend.at[1], xrecv.at[len(XPARTS) - 1, 0], (g + 1, s - 3))
    pl.when(last15)(to_relay.start)
    pl.when(outer)(lambda: start(sent[:XFIRST]))

    get_ud = [
        load(upper_down.at[16 - (32 >> k) + s // 2**k], udv.at[k - 1]) for k in range(1, 4)
    ]
    get_uc = [
        load(upper_coupling.at[16 - (32 >> k) + s // 2**k], ucv.at[k - 1]) for k in range(1, 5)
    ]

    low = lax.broadcasted_iota(jnp.int32, (RHS, 128), 1) < 64

    for k in range(4):
        if k % 2 == 0:
            get_x[k // 2].wait()
        get_cb[k].wait()

        def leaf_moments(i):
            at = 4 * k + i
            one, two = cx[:, lanes(512 * at, 256)], cx[:, lanes(512 * at + 256, 256)]
            both = nt(jnp.concatenate([one, two], axis=0), cbv[pl.ds(2 * at, 2)].reshape(128, LEAF))
            return one, two, jnp.where(low, both[:RHS], both[RHS:]).astype(BF)

        def keep_moments(i, got):
            at = 4 * k + i
            xw[LEAVES + 2 * at] = got[0]
            xw[LEAVES + 2 * at + 1] = got[1]
            mv[32 + at] = got[2]

        batched(4, 4, leaf_moments, keep_moments)

    @pl.when(inner)
    def _():
        pl.semaphore_wait(barrier, 12)
        pl.when(before15)(lambda: pl.semaphore_signal(hello, inc=1, device_id=(g, 15), device_id_type=MESH))
        start(sent[:1])

    get_up.wait()
    zero = jnp.zeros((RHS, RANK), F32)
    for height in range(1, LEVELS + 1):
        amount = LEAVES >> height
        base, child = row_of(height), row_of(height - 1)

        def lift(j):
            return nn(mv[32 + child // 2 + j], upv[pl.ds(child + 2 * j, 2)].reshape(128, RANK))

        def lift_two(j):
            return jnp.concatenate([lift(2 * j), lift(2 * j + 1)], axis=1).astype(BF)

        def keep_two(j, got):
            mv[32 + base // 2 + j] = got

        if amount == 1:
            root = lift(0)
            mv[63] = jnp.concatenate([root, zero], axis=1).astype(BF)
        else:
            batched(amount // 2, 4, lift_two, keep_two)

    get_dn = load(local_down, dnv)
    get_nb = [load(near_block.at[pl.ds(4 * k, 4)], nbv.at[pl.ds(4 * k, 4)]) for k in range(8)]
    get_cp = [load(local_coupling.at[pl.ds(9 * k, 9)], cpv.at[pl.ds(9 * k, 9)]) for k in range(7)]
    get_rb = load(row_basis, rbv)

    lifted = nn(root.astype(BF), upv[62])
    rx[x] = jnp.where(low == (x < 2), jnp.concatenate([lifted, lifted], axis=1), 0.0).astype(BF)

    gone_x = [remote(rx.at[x], rx.at[x], rxsend.at[0], rxrecv.at[0], other)] + [
        remote(rx.at[x], rx.at[x], rxsend.at[1 + k], rxrecv.at[1 + x // 3], p) for k, p in enumerate(middle)
    ]

    @pl.when(inner)
    def _():
        gone_x[0].start()

    @pl.when(outer)
    def _():
        pl.when(last15)(lambda: pl.semaphore_wait(hello, 2))
        gone_x[1].start()
        gone_x[2].start()

    moved = [
        beside(
            mv.at[pl.ds(32 + 16 * k, 16)],
            lambda side: mv.at[pl.ds(32 * side + 16 * k, 16)],
            msend.at[k],
            mrecv.at[k],
        )
        for k in range(2)
    ]
    start(moved)
    pl.when(inner)(lambda: start(sent[1:XFIRST]))
    start(sent[XFIRST:-2])
    pl.when((d < 127) & jnp.logical_not(relay3))(sent[-2][0].start)
    pl.when((d < 127) & jnp.logical_not(relay3 | last15))(sent[-1][0].start)
    for copies in sent[-2:]:
        pl.when((d > 0) & jnp.logical_not(later))(copies[1].start)

    pl.when(first0)(lambda: pl.semaphore_wait(hello, 1))
    start(sent[:XFIRST] + moved + sent[XFIRST:], late=True)


    get_at[0].wait()
    t = lax.broadcasted_iota(jnp.int32, (8, 63), 1)
    f = lax.broadcasted_iota(jnp.int32, (8, 63), 0)
    amount = jnp.full((8, 63), LEAVES, jnp.int32)
    for height in range(1, LEVELS + 1):
        amount = jnp.where(t < row_of(height), amount, LEAVES >> height)
    q = far_raw[...] - (d - 1) * amount
    window = (q >= amount).astype(jnp.int32) + (q >= 2 * amount).astype(jnp.int32)
    row = 64 - 2 * amount + (q & (amount - 1))
    far_row[...] = jnp.zeros((8, 64), jnp.int32)
    far_row[:, 0:63] = ((row + f) & 1) * 128 + window * 32 + (row >> 1)
    get_far = pltpu.make_async_copy(far_row, far_at, lsem.at[len(loads)])
    get_far.start()

    get_dn.wait()

    def extend_level(height):
        amount = LEAVES >> height
        base, parent = row_of(height), row_of(height + 1)

        def below(above, j):
            return nt(above, dnv[pl.ds(base + 2 * j, 2)].reshape(128, RANK)).astype(BF)

        if amount == 2:
            path[base // 2] = below(dnv[62].T, 0)
        else:

            def extend(j):
                above = path[parent // 2 + j]
                return below(above[:, :64], 2 * j), below(above[:, 64:], 2 * j + 1)

            def keep(j, got):
                path[base // 2 + 2 * j] = got[0]
                path[base // 2 + 2 * j + 1] = got[1]

            batched(amount // 4, 4, extend, keep)

    for height in range(LEVELS - 1, -1, -1):
        extend_level(height)

    get_uu.wait()
    gone_z = [remote(rz.at[z], rz.at[z], rzsend.at[k], rzrecv.at[k], p) for k, p in enumerate(by_z)]

    @pl.when(inner)
    def _():
        for k in range(3):
            remote(rx.at[k], rx.at[k], rxsend.at[k], rxrecv.at[k], other).wait_recv()
        first = (
            (rx[0].astype(F32) + rx[1].astype(F32)) + (rx[2].astype(F32) + rx[3].astype(F32))
        ).astype(BF)
        rz[z, 0] = first
        second = nn(first, uuv[pl.ds(2 * z, 2)].reshape(128, RANK))
        rz[z, 1] = jnp.where(low == (z % 2 == 0), jnp.concatenate([second, second], axis=1), 0.0).astype(BF)
        for copy in gone_z:
            copy.start()

    def near_own(i):
        return nt(xw[LEAVES + i], nbv[i, 0])

    def keep_own(i, got):
        acc[:, lanes(256 * i, 256)] = got

    for k in range(4):
        get_nb[k].wait()
        batched(4, OWN, lambda i: near_own(4 * k + i), lambda i, got: keep_own(4 * k + i, got))

    gone_y = [remote(rg.at[g], rg.at[g], rgsend.at[k], rgrecv.at[k], p) for k, p in enumerate(by_y + [twin])]

    @pl.when(inner)
    def _():
        for copy in gone_z:
            copy.wait_recv()
        for k in range(4):
            rg[g, k] = rz[k, 0]
        thirds = []
        for k in range(2):
            pair = (rz[2 * k, 1].astype(F32) + rz[2 * k + 1, 1].astype(F32)).astype(BF)
            rg[g, 4 + k] = pair
            thirds.append(nn(pair, uuv[8 + 2 * k : 10 + 2 * k].reshape(128, RANK)))
        third = jnp.concatenate(thirds, axis=1).astype(BF)
        rg[g, 6] = third
        top = nn(third, uuv[12:14].reshape(128, RANK))
        rg[g, 7] = jnp.concatenate([top, zero], axis=1).astype(BF)
        for copy in gone_y:
            copy.start()

    for k in range(4, 8):
        get_nb[k].wait()
        batched(4, OWN, lambda i: near_own(4 * k + i), lambda i, got: keep_own(4 * k + i, got))

    get_rb.wait()

    def reach(i):
        pair = path[i]
        return nn(pair[:, :64], rbv[2 * i]).astype(BF), nn(pair[:, 64:], rbv[2 * i + 1]).astype(BF)

    def keep_reach(i, got):
        qv[:, lanes(512 * i, 256)] = got[0]
        qv[:, lanes(512 * i + 256, 256)] = got[1]

    batched(16, REACH, reach, keep_reach)

    @pl.when(relay3)
    def _():
        to_relay.wait_recv()
        from_relay.start()
        sent[-2][0].start()
        sent[-1][0].start()

    for copy in get_ud:
        copy.wait()
    down1 = udv[0]
    down2 = nn(down1, udv[1]).astype(BF)
    down3 = nn(down2, udv[2]).astype(BF)

    for copies in moved:
        arrive(copies)

    def turn(i):
        pair = mv[i]
        return jnp.concatenate([pair[:, 64:], pair[:, :64]], axis=1)

    def keep_turn(i, got):
        mv[128 + i] = got

    batched(96, TURN, turn, keep_turn)
    get_far.wait()
    for copy in get_cp:
        copy.wait()

    def couple(t):
        total = None
        for q in range(2):
            moments = jnp.concatenate(
                [
                    jnp.where(low, mv[far_at[4 * q + 2 * j, t]], mv[far_at[4 * q + 2 * j + 1, t]])
                    for j in range(2)
                ],
                axis=1,
            )
            blocks = jnp.concatenate([cpv[t, 4 * q + j] for j in range(4)], axis=1)
            term = nt(moments, blocks)
            total = term if total is None else total + term
        return total

    def couple_two(j):
        return jnp.concatenate([couple(2 * j), couple(2 * j + 1)], axis=1)

    def keep_couple(j, got):
        far[j] = got

    batched(32, FAR, couple_two, keep_couple)

    dloc[31] = far[31].astype(BF)
    for height in range(LEVELS - 1, -1, -1):
        amount = LEAVES >> height
        base, parent = row_of(height), row_of(height + 1)

        def below(above, j):
            pair = dnv[pl.ds(base + 2 * j, 2)].reshape(128, RANK)
            return (far[base // 2 + j] + nt(above, pair)).astype(BF)

        if amount == 2:
            dloc[base // 2] = below(dloc[31][:, :64], 0)
        else:

            def descend(j):
                above = dloc[parent // 2 + j]
                return below(above[:, :64], 2 * j), below(above[:, 64:], 2 * j + 1)

            def keep_descend(j, got):
                dloc[base // 2 + 2 * j] = got[0]
                dloc[base // 2 + 2 * j + 1] = got[1]

            batched(amount // 4, 4, descend, keep_descend)

    def local(i):
        pair = dloc[i]
        return [
            acc[:, lanes(512 * i + 256 * k, 256)] + nn(pair[:, 64 * k : 64 * (k + 1)], rbv[2 * i + k])
            for k in range(2)
        ]

    def keep_rest(i, got):
        for k in range(2):
            acc[:, lanes(512 * i + 256 * k, 256)] = got[k]

    batched(16, 8, local, keep_rest)

    get_at[1].wait()
    for copy in get_uc:
        copy.wait()
    passed = []
    for k in range(3):
        from_y = ((y + 3 - k) % 4) * 2 + core
        passed.append(remote(rg.at[from_y], rg.at[from_y], rgsend.at[4 + k], rgrecv.at[4 + k], twin))
    gone_p = remote(pv, pv, psend, precv, helped)

    @pl.when(inner)
    def _():
        for k in (0, 2, 1):
            gone_y[k].wait_recv()
            passed[k].start()
        gone_y[3].wait_recv()
        for copy in passed:
            copy.wait_recv()
        terms = []
        for k in range(1, 5):
            amount = 16 >> k
            row = 16 - 2 * amount + s // 2**k

            def pick(f):
                p = ufar_at[f, row]
                group, j = p >> (4 - k), p & (amount - 1)
                pair = rg[group, (0, 4, 6, 7)[k - 1] + (j >> 1)]
                pair = pair.astype(F32)
                turned = jnp.concatenate([pair[:, 64:], pair[:, :64]], axis=1)
                keep = (1 - ((j + f) & 1)).astype(F32)
                return pair * keep + turned * (1.0 - keep)

            total = None
            for q in range(2):
                moments = jnp.concatenate(
                    [jnp.where(low, pick(4 * q + 2 * j), pick(4 * q + 2 * j + 1)) for j in range(2)], axis=1
                ).astype(BF)
                blocks = jnp.concatenate([ucv[k - 1, 4 * q + j] for j in range(4)], axis=1)
                term = nt(moments, blocks)
                total = term if total is None else total + term
            terms.append(total)
        parent = (
            terms[0]
            + nt(terms[1].astype(BF), down1)
            + nt(terms[2].astype(BF), down2)
            + nt(terms[3].astype(BF), down3)
        ).astype(BF)
        pv[...] = jnp.concatenate([parent, parent], axis=1)
        gone_p.start()

    get_at[2].wait()
    for copies, (start, size) in zip(sent, XPARTS):
        arrive(copies)

        def window(i):
            part = lanes(start + LEAF * i, LEAF)
            return xin[0, :, part], xin[1, :, part]

        def keep_window(i, got):
            xw[start // LEAF + i] = got[0]
            xw[2 * LEAVES + start // LEAF + i] = got[1]

        batched(size // LEAF, 2, window, keep_window)

    def add_near(i, k, total):
        leaf = 2 * i + k
        for n in (1, 2):
            q = (near_at[n, leaf] - (d - 1) * LEAVES) & 127
            total = total + nt(xw[q], nbv[leaf, n])
        return total

    upper_first = inner | last15
    pl.when(last15)(gone_p.wait_recv)

    @pl.when(upper_first)
    def _():
        parent = pv[...][:, :64]

        def rest(i):
            above = nn(parent, qv[:, lanes(512 * i, 512)])
            return [
                add_near(
                    i, k, acc[:, lanes(512 * i + 256 * k, 256)] + above[:, 256 * k : 256 * (k + 1)]
                ).astype(BF)
                for k in range(2)
            ]

        def keep_out(i, got):
            for k in range(2):
                out[:, lanes(512 * i + 256 * k, 256)] = got[k]

        batched(16, REST, rest, keep_out)

    @pl.when(jnp.logical_not(upper_first))
    def _():
        def rest(i):
            return [add_near(i, k, acc[:, lanes(512 * i + 256 * k, 256)]) for k in range(2)]

        batched(16, REST, rest, keep_rest)
        gone_p.wait_recv()
        parent = pv[...][:, :64]

        def finish(i):
            part = lanes(512 * i, 512)
            return (acc[:, part] + nn(parent, qv[:, part])).astype(BF)

        def keep_finish(i, got):
            out[:, lanes(512 * i, 512)] = got

        batched(16, FINISH, finish, keep_finish)

    for copies in sent[:-1]:
        leave(copies)
    pl.when((d < 127) & jnp.logical_not(last15))(sent[-1][0].wait_send)
    pl.when(d > 0)(sent[-1][1].wait_send)
    pl.when(last15)(to_relay.wait_send)
    pl.when(relay3)(from_relay.wait_send)
    for copies in moved:
        leave(copies)

    @pl.when(inner)
    def _():
        for copy in [gone_x[0]] + gone_z + gone_y + passed + [gone_p]:
            copy.wait_send()

    @pl.when(outer)
    def _():
        gone_x[1].wait_send()
        gone_x[2].wait_send()


def on_device(
    charges,
    column_basis,
    row_basis,
    local_up,
    local_down,
    local_far,
    local_coupling,
    upper_up,
    upper_down,
    upper_far,
    upper_coupling,
    near_source,
    near_block,
):
    dma = pltpu.SemaphoreType.DMA
    vmem = pltpu.VMEM
    anywhere = pl.BlockSpec(memory_space=pl.ANY)
    return pl.pallas_call(
        kernel,
        out_shape=pltpu.VMEM((RHS, COLS), BF),
        in_specs=[anywhere] * 13,
        out_specs=pl.BlockSpec(memory_space=vmem),
        scratch_shapes=[
            vmem((RHS, COLS), BF),
            vmem((2, RHS, COLS), BF),
            vmem((4 * LEAVES, RHS, LEAF), BF),
            vmem((LEAVES, RANK, LEAF), BF),
            vmem((LEAVES, RANK, LEAF), BF),
            vmem((63, RANK, RANK), BF),
            vmem((63, RANK, RANK), BF),
            vmem((64, 8, RANK, RANK), BF),
            vmem((14, RANK, RANK), BF),
            vmem((3, RANK, RANK), BF),
            vmem((4, 8, RANK, RANK), BF),
            vmem((LEAVES, 3, LEAF, LEAF), BF),
            vmem((256, RHS, 128), BF),
            vmem((4, RHS, 128), BF),
            vmem((4, 2, RHS, 128), BF),
            vmem((8, 8, RHS, 128), BF),
            vmem((RHS, 128), BF),
            vmem((RHS, COLS), F32),
            vmem((32, RHS, 128), F32),
            vmem((32, RHS, 128), BF),
            vmem((32, RANK, 128), BF),
            vmem((RANK, COLS), BF),
            vmem((8, 63), jnp.int32),
            vmem((8, 64), jnp.int32),
            pltpu.SMEM((8, 64), jnp.int32),
            pltpu.SMEM((8, 15), jnp.int32),
            pltpu.SMEM((3, LEAVES), jnp.int32),
            dma((40,)),
            dma((len(XPARTS), 2)),
            dma((len(XPARTS), 2)),
            dma((2, 2)),
            dma((2, 2)),
            dma((3,)),
            dma((3,)),
            dma((3,)),
            dma((3,)),
            dma((7,)),
            dma((7,)),
            dma,
            dma,
            pltpu.SemaphoreType.REGULAR,
            vmem((RHS, XPARTS[-1][1]), BF),
            dma((2,)),
            dma,
        ],
        compiler_params=pltpu.CompilerParams(
            collective_id=0, has_side_effects=True, vmem_limit_bytes=60 * 2**20
        ),
        name="h2_product",
    )(
        charges,
        column_basis,
        row_basis,
        local_up,
        local_down,
        local_far.T,
        local_coupling,
        upper_up,
        upper_down,
        upper_far.T,
        upper_coupling,
        near_source.T,
        near_block,
    )


def solution(mesh):
    both = ("grp", "sub")
    in_specs = (
        P(None, both),
        P(both, None, None),
        P(both, None, None),
        P(both, None, None),
        P(both, None, None),
        P(both, None),
        P(both, None, None, None),
        P("grp", None, None),
        P("grp", None, None),
        P("grp", None),
        P("grp", None, None, None),
        P(both, None),
        P(both, None, None, None),
    )
    return jax.shard_map(
        on_device, mesh=mesh, in_specs=in_specs, out_specs=P(None, both), check_vma=False
    )
```

```python
import functools

import jax
import jax.numpy as jnp
from jax import lax
from jax.experimental import pallas as pl
from jax.experimental.pallas import tpu as pltpu
from jax.sharding import PartitionSpec as P

MESH = pl.DeviceIdType.MESH
BF = jnp.bfloat16
F32 = jnp.float32
RHS = 32
LEAVES = 32
LEAF = 256
RANK = 64
LEVELS = 5
COLS = LEAVES * LEAF
XPARTS = ((0, 1024), (1024, 1024), (2048, 2048), (4096, 2560), (6656, 1536))
XFIRST = 2
OWN, REACH, TURN, FAR, REST, FINISH = 4, 16, 96, 16, 16, 16


def nt(a, b):
    return lax.dot_general(a, b, (((1,), (1,)), ((), ())), preferred_element_type=F32)


def nn(a, b):
    return lax.dot_general(a, b, (((1,), (0,)), ((), ())), preferred_element_type=F32)


def lanes(start, size):
    return pl.ds(pl.multiple_of(start, 128), size)


def loop(count, body, unroll):
    def step(i, carry):
        body(i)
        return carry

    lax.fori_loop(0, count, step, 0, unroll=min(unroll, count))


def batched(count, width, compute, store):
    width = min(width, count)

    def body(b):
        got = [compute(width * b + j) for j in range(width)]
        for j in range(width):
            store(width * b + j, got[j])

    loop(count // width, body, 1)


def row_of(height):
    return 64 - 2 * (LEAVES >> height)


def kernel(
    charges,
    column_basis,
    row_basis,
    local_up,
    local_down,
    local_far,
    local_coupling,
    upper_up,
    upper_down,
    upper_far,
    upper_coupling,
    near_source,
    near_block,
    out,
    cx,
    xin,
    xw,
    cbv,
    rbv,
    upv,
    dnv,
    cpv,
    uuv,
    udv,
    ucv,
    nbv,
    mv,
    rx,
    rz,
    rg,
    pv,
    acc,
    far,
    dloc,
    path,
    qv,
    far_raw,
    far_row,
    far_at,
    ufar_at,
    near_at,
    lsem,
    xsend,
    xrecv,
    msend,
    mrecv,
    rxsend,
    rxrecv,
    rzsend,
    rzrecv,
    rgsend,
    rgrecv,
    psend,
    precv,
    hello,
    hop,
    hsend,
    hrecv,
):
    g = lax.axis_index("grp")
    s = lax.axis_index("sub")
    d = g * 16 + s
    z = s // 4
    x = s % 4

    def place(e):
        return (e // 16, e % 16)

    sides = ((d < 127, place((d + 1) % 128)), (d > 0, place((d + 127) % 128)))
    inner = (x == 1) | (x == 2)
    outer = jnp.logical_not(inner)
    y, core = g // 2, g % 2
    middle = [(g, z * 4 + 1), (g, z * 4 + 2)]
    other = (g, z * 4 + 3 - x)
    helped = (g, z * 4 + 3 * (x // 2))
    by_z = [(g, ((z + k) % 4) * 4 + x) for k in range(1, 4)]
    by_y = [(((y + k) % 4) * 2 + core, s) for k in range(1, 4)]
    twin = (2 * y + 1 - core, s)

    first0 = (s == 0) & (g > 0)
    last15 = (s == 15) & (g < 7)
    relay3 = (s == 3) & (g < 7)
    before15 = (z == 3) & (g < 7) & inner
    later = first0 | last15

    barrier = pltpu.get_barrier_semaphore()

    def greet(peer):
        pl.semaphore_signal(barrier, inc=1, device_id=peer, device_id_type=MESH)

    pl.when((d < 127) & jnp.logical_not(last15 | before15 & (x == 2)))(functools.partial(greet, sides[0][1]))
    pl.when(d > 0)(functools.partial(greet, sides[1][1]))
    pl.when(first0)(functools.partial(greet, ((g + 7) % 8, 3)))
    pl.when(relay3)(functools.partial(greet, (g, 15)))

    @pl.when(inner)
    def _():
        for peer in [other, (g, z * 4)] + by_z + by_y + [twin]:
            greet(peer)
        pl.when(jnp.logical_not(before15))(functools.partial(greet, (g, z * 4 + 3)))

    @pl.when(outer)
    def _():
        for peer in middle:
            greet(peer)

    loads = []

    def load(src, dst):
        copy = pltpu.make_async_copy(src, dst, lsem.at[len(loads)])
        copy.start()
        loads.append(copy)
        return copy

    get_x = [load(charges.at[:, pl.ds(4096 * k, 4096)], cx.at[:, pl.ds(4096 * k, 4096)]) for k in range(2)]
    get_cb = [load(column_basis.at[pl.ds(8 * k, 8)], cbv.at[pl.ds(8 * k, 8)]) for k in range(4)]
    get_up = load(local_up, upv)
    get_uu = load(upper_up, uuv)
    get_at = [load(local_far, far_raw), load(upper_far, ufar_at), load(near_source, near_at)]

    @pl.when(outer)
    def _():
        count = 2 + (d < 127).astype(jnp.int32) + ((d > 0) & (s > 0)).astype(jnp.int32)
        pl.semaphore_wait(barrier, jnp.where(last15, 2, count + relay3.astype(jnp.int32)))
        pl.when(last15)(lambda: pl.semaphore_signal(hello, inc=1, device_id=sides[0][1], device_id_type=MESH))

    def remote(src, dst, ssem, rsem, peer):
        return pltpu.make_async_remote_copy(
            src_ref=src, dst_ref=dst, send_sem=ssem, recv_sem=rsem, device_id=peer, device_id_type=MESH
        )

    def send(src, dst, ssem, rsem, peer):
        copy = remote(src, dst, ssem, rsem, peer)
        copy.start()
        return copy

    def beside(src, dst, ssem, rsem):
        return [remote(src, dst(2 * k), ssem.at[k], rsem.at[k], peer) for k, (_, peer) in enumerate(sides)]

    def start(batches, late=False):
        for k, (there, _) in enumerate(sides):
            if late:
                go = later if k else False
            else:
                go = there & jnp.logical_not(later) if k else there

            if go is not False:

                @pl.when(go)
                def _():
                    for copies in batches:
                        copies[k].start()

    def arrive(copies):
        for (there, _), copy in zip((sides[1], sides[0]), copies):
            pl.when(there)(copy.wait_recv)

    def leave(copies):
        for (there, _), copy in zip(sides, copies):
            pl.when(there)(copy.wait_send)

    def charges_part(k):
        start, size = XPARTS[k]
        part = pl.ds(start, size)
        return beside(
            charges.at[:, part],
            lambda side: xin.at[side // 2, :, part],
            xsend.at[k],
            xrecv.at[k],
        )

    sent = [charges_part(k) for k in range(len(XPARTS))]
    part = pl.ds(*XPARTS[-1])
    to_relay = remote(charges.at[:, part], hop, hsend.at[0], hrecv, (g, 3))
    from_relay = remote(hop, xin.at[0, :, part], hsend.at[1], xrecv.at[len(XPARTS) - 1, 0], ((g + 1) % 8, 0))
    pl.when(last15)(to_relay.start)
    pl.when(outer)(lambda: start(sent[:XFIRST]))

    get_ud = [
        load(upper_down.at[16 - (32 >> k) + s // 2**k], udv.at[k - 1]) for k in range(1, 4)
    ]
    get_uc = [
        load(upper_coupling.at[16 - (32 >> k) + s // 2**k], ucv.at[k - 1]) for k in range(1, 5)
    ]

    low = lax.broadcasted_iota(jnp.int32, (RHS, 128), 1) < 64

    for k in range(4):
        if k % 2 == 0:
            get_x[k // 2].wait()
        get_cb[k].wait()

        def leaf_moments(i):
            at = 4 * k + i
            one, two = cx[:, lanes(512 * at, 256)], cx[:, lanes(512 * at + 256, 256)]
            both = nt(jnp.concatenate([one, two], axis=0), cbv[pl.ds(2 * at, 2)].reshape(128, LEAF))
            return one, two, jnp.where(low, both[:RHS], both[RHS:]).astype(BF)

        def keep_moments(i, got):
            at = 4 * k + i
            xw[LEAVES + 2 * at] = got[0]
            xw[LEAVES + 2 * at + 1] = got[1]
            mv[32 + at] = got[2]

        batched(4, 4, leaf_moments, keep_moments)

    @pl.when(inner)
    def _():
        pl.semaphore_wait(barrier, 12)
        pl.when(before15)(lambda: pl.semaphore_signal(hello, inc=1, device_id=(g, 15), device_id_type=MESH))
        start(sent[:1])

    get_up.wait()
    zero = jnp.zeros((RHS, RANK), F32)
    for height in range(1, LEVELS + 1):
        amount = LEAVES >> height
        base, child = row_of(height), row_of(height - 1)

        def lift(j):
            return nn(mv[32 + child // 2 + j], upv[pl.ds(child + 2 * j, 2)].reshape(128, RANK))

        def lift_two(j):
            return jnp.concatenate([lift(2 * j), lift(2 * j + 1)], axis=1).astype(BF)

        def keep_two(j, got):
            mv[32 + base // 2 + j] = got

        if amount == 1:
            root = lift(0)
            mv[63] = jnp.concatenate([root, zero], axis=1).astype(BF)
        else:
            batched(amount // 2, 4, lift_two, keep_two)

    get_dn = load(local_down, dnv)
    get_nb = [load(near_block.at[pl.ds(4 * k, 4)], nbv.at[pl.ds(4 * k, 4)]) for k in range(8)]
    get_cp = [load(local_coupling.at[pl.ds(9 * k, 9)], cpv.at[pl.ds(9 * k, 9)]) for k in range(7)]
    get_rb = load(row_basis, rbv)

    lifted = nn(root.astype(BF), upv[62])
    rx[x] = jnp.where(low == (x < 2), jnp.concatenate([lifted, lifted], axis=1), 0.0).astype(BF)

    gone_x = [remote(rx.at[x], rx.at[x], rxsend.at[0], rxrecv.at[0], other)] + [
        remote(rx.at[x], rx.at[x], rxsend.at[1 + k], rxrecv.at[1 + x // 3], p) for k, p in enumerate(middle)
    ]

    @pl.when(inner)
    def _():
        gone_x[0].start()

    @pl.when(outer)
    def _():
        pl.when(last15)(lambda: pl.semaphore_wait(hello, 2))
        gone_x[1].start()
        gone_x[2].start()

    moved = [
        beside(
            mv.at[pl.ds(32 + 16 * k, 16)],
            lambda side: mv.at[pl.ds(32 * side + 16 * k, 16)],
            msend.at[k],
            mrecv.at[k],
        )
        for k in range(2)
    ]
    start(moved)
    pl.when(inner)(lambda: start(sent[1:XFIRST]))
    start(sent[XFIRST:-2])
    pl.when((d < 127) & jnp.logical_not(relay3))(sent[-2][0].start)
    pl.when((d < 127) & jnp.logical_not(relay3 | last15))(sent[-1][0].start)
    for copies in sent[-2:]:
        pl.when((d > 0) & jnp.logical_not(later))(copies[1].start)

    pl.when(first0)(lambda: pl.semaphore_wait(hello, 1))
    start(sent[:XFIRST] + moved + sent[XFIRST:], late=True)


    get_at[0].wait()
    t = lax.broadcasted_iota(jnp.int32, (8, 63), 1)
    f = lax.broadcasted_iota(jnp.int32, (8, 63), 0)
    amount = jnp.full((8, 63), LEAVES, jnp.int32)
    for height in range(1, LEVELS + 1):
        amount = jnp.where(t < row_of(height), amount, LEAVES >> height)
    q = far_raw[...] - (d - 1) * amount
    window = (q >= amount).astype(jnp.int32) + (q >= 2 * amount).astype(jnp.int32)
    row = 64 - 2 * amount + (q & (amount - 1))
    far_row[...] = jnp.zeros((8, 64), jnp.int32)
    far_row[:, 0:63] = ((row + f) & 1) * 128 + window * 32 + (row >> 1)
    get_far = pltpu.make_async_copy(far_row, far_at, lsem.at[len(loads)])
    get_far.start()

    get_dn.wait()

    def extend_level(height):
        amount = LEAVES >> height
        base, parent = row_of(height), row_of(height + 1)

        def below(above, j):
            return nt(above, dnv[pl.ds(base + 2 * j, 2)].reshape(128, RANK)).astype(BF)

        if amount == 2:
            path[base // 2] = below(dnv[62].T, 0)
        else:

            def extend(j):
                above = path[parent // 2 + j]
                return below(above[:, :64], 2 * j), below(above[:, 64:], 2 * j + 1)

            def keep(j, got):
                path[base // 2 + 2 * j] = got[0]
                path[base // 2 + 2 * j + 1] = got[1]

            batched(amount // 4, 4, extend, keep)

    for height in range(LEVELS - 1, -1, -1):
        extend_level(height)

    get_uu.wait()
    gone_z = [remote(rz.at[z], rz.at[z], rzsend.at[k], rzrecv.at[k], p) for k, p in enumerate(by_z)]

    @pl.when(inner)
    def _():
        for k in range(3):
            remote(rx.at[k], rx.at[k], rxsend.at[k], rxrecv.at[k], other).wait_recv()
        first = (
            (rx[0].astype(F32) + rx[1].astype(F32)) + (rx[2].astype(F32) + rx[3].astype(F32))
        ).astype(BF)
        rz[z, 0] = first
        second = nn(first, uuv[pl.ds(2 * z, 2)].reshape(128, RANK))
        rz[z, 1] = jnp.where(low == (z % 2 == 0), jnp.concatenate([second, second], axis=1), 0.0).astype(BF)
        for copy in gone_z:
            copy.start()

    def near_own(i):
        return nt(xw[LEAVES + i], nbv[i, 0])

    def keep_own(i, got):
        acc[:, lanes(256 * i, 256)] = got

    for k in range(4):
        get_nb[k].wait()
        batched(4, OWN, lambda i: near_own(4 * k + i), lambda i, got: keep_own(4 * k + i, got))

    gone_y = [remote(rg.at[g], rg.at[g], rgsend.at[k], rgrecv.at[k], p) for k, p in enumerate(by_y + [twin])]

    @pl.when(inner)
    def _():
        for copy in gone_z:
            copy.wait_recv()
        for k in range(4):
            rg[g, k] = rz[k, 0]
        thirds = []
        for k in range(2):
            pair = (rz[2 * k, 1].astype(F32) + rz[2 * k + 1, 1].astype(F32)).astype(BF)
            rg[g, 4 + k] = pair
            thirds.append(nn(pair, uuv[8 + 2 * k : 10 + 2 * k].reshape(128, RANK)))
        third = jnp.concatenate(thirds, axis=1).astype(BF)
        rg[g, 6] = third
        top = nn(third, uuv[12:14].reshape(128, RANK))
        rg[g, 7] = jnp.concatenate([top, zero], axis=1).astype(BF)
        for copy in gone_y:
            copy.start()

    for k in range(4, 8):
        get_nb[k].wait()
        batched(4, OWN, lambda i: near_own(4 * k + i), lambda i, got: keep_own(4 * k + i, got))

    get_rb.wait()

    def reach(i):
        pair = path[i]
        return nn(pair[:, :64], rbv[2 * i]).astype(BF), nn(pair[:, 64:], rbv[2 * i + 1]).astype(BF)

    def keep_reach(i, got):
        qv[:, lanes(512 * i, 256)] = got[0]
        qv[:, lanes(512 * i + 256, 256)] = got[1]

    batched(16, REACH, reach, keep_reach)

    @pl.when(relay3)
    def _():
        to_relay.wait_recv()
        from_relay.start()
        sent[-2][0].start()
        sent[-1][0].start()

    for copy in get_ud:
        copy.wait()
    down1 = udv[0]
    down2 = nn(down1, udv[1]).astype(BF)
    down3 = nn(down2, udv[2]).astype(BF)

    for copies in moved:
        arrive(copies)

    def turn(i):
        pair = mv[i]
        return jnp.concatenate([pair[:, 64:], pair[:, :64]], axis=1)

    def keep_turn(i, got):
        mv[128 + i] = got

    batched(96, TURN, turn, keep_turn)
    get_far.wait()
    for copy in get_cp:
        copy.wait()

    def couple(t):
        total = None
        for q in range(2):
            moments = jnp.concatenate(
                [
                    jnp.where(low, mv[far_at[4 * q + 2 * j, t]], mv[far_at[4 * q + 2 * j + 1, t]])
                    for j in range(2)
                ],
                axis=1,
            )
            blocks = jnp.concatenate([cpv[t, 4 * q + j] for j in range(4)], axis=1)
            term = nt(moments, blocks)
            total = term if total is None else total + term
        return total

    def couple_two(j):
        return jnp.concatenate([couple(2 * j), couple(2 * j + 1)], axis=1)

    def keep_couple(j, got):
        far[j] = got

    batched(32, FAR, couple_two, keep_couple)

    dloc[31] = far[31].astype(BF)
    for height in range(LEVELS - 1, -1, -1):
        amount = LEAVES >> height
        base, parent = row_of(height), row_of(height + 1)

        def below(above, j):
            pair = dnv[pl.ds(base + 2 * j, 2)].reshape(128, RANK)
            return (far[base // 2 + j] + nt(above, pair)).astype(BF)

        if amount == 2:
            dloc[base // 2] = below(dloc[31][:, :64], 0)
        else:

            def descend(j):
                above = dloc[parent // 2 + j]
                return below(above[:, :64], 2 * j), below(above[:, 64:], 2 * j + 1)

            def keep_descend(j, got):
                dloc[base // 2 + 2 * j] = got[0]
                dloc[base // 2 + 2 * j + 1] = got[1]

            batched(amount // 4, 4, descend, keep_descend)

    def local(i):
        pair = dloc[i]
        return [
            acc[:, lanes(512 * i + 256 * k, 256)] + nn(pair[:, 64 * k : 64 * (k + 1)], rbv[2 * i + k])
            for k in range(2)
        ]

    def keep_rest(i, got):
        for k in range(2):
            acc[:, lanes(512 * i + 256 * k, 256)] = got[k]

    batched(16, 8, local, keep_rest)

    get_at[1].wait()
    for copy in get_uc:
        copy.wait()
    passed = []
    for k in range(3):
        from_y = ((y + 3 - k) % 4) * 2 + core
        passed.append(remote(rg.at[from_y], rg.at[from_y], rgsend.at[4 + k], rgrecv.at[4 + k], twin))
    gone_p = remote(pv, pv, psend, precv, helped)

    @pl.when(inner)
    def _():
        for k in (0, 2, 1):
            gone_y[k].wait_recv()
            passed[k].start()
        gone_y[3].wait_recv()
        for copy in passed:
            copy.wait_recv()
        terms = []
        for k in range(1, 5):
            amount = 16 >> k
            row = 16 - 2 * amount + s // 2**k

            def pick(f):
                p = ufar_at[f, row]
                group, j = p >> (4 - k), p & (amount - 1)
                pair = rg[group, (0, 4, 6, 7)[k - 1] + (j >> 1)]
                pair = pair.astype(F32)
                turned = jnp.concatenate([pair[:, 64:], pair[:, :64]], axis=1)
                keep = (1 - ((j + f) & 1)).astype(F32)
                return pair * keep + turned * (1.0 - keep)

            total = None
            for q in range(2):
                moments = jnp.concatenate(
                    [jnp.where(low, pick(4 * q + 2 * j), pick(4 * q + 2 * j + 1)) for j in range(2)], axis=1
                ).astype(BF)
                blocks = jnp.concatenate([ucv[k - 1, 4 * q + j] for j in range(4)], axis=1)
                term = nt(moments, blocks)
                total = term if total is None else total + term
            terms.append(total)
        parent = (
            terms[0]
            + nt(terms[1].astype(BF), down1)
            + nt(terms[2].astype(BF), down2)
            + nt(terms[3].astype(BF), down3)
        ).astype(BF)
        pv[...] = jnp.concatenate([parent, parent], axis=1)
        gone_p.start()

    get_at[2].wait()
    for copies, (start, size) in zip(sent, XPARTS):
        arrive(copies)

        def window(i):
            part = lanes(start + LEAF * i, LEAF)
            return xin[0, :, part], xin[1, :, part]

        def keep_window(i, got):
            xw[start // LEAF + i] = got[0]
            xw[2 * LEAVES + start // LEAF + i] = got[1]

        batched(size // LEAF, 2, window, keep_window)

    def add_near(i, k, total):
        leaf = 2 * i + k
        for n in (1, 2):
            q = (near_at[n, leaf] - (d - 1) * LEAVES) & 127
            total = total + nt(xw[q], nbv[leaf, n])
        return total

    upper_first = inner | last15
    pl.when(last15)(gone_p.wait_recv)

    @pl.when(upper_first)
    def _():
        parent = pv[...][:, :64]

        def rest(i):
            above = nn(parent, qv[:, lanes(512 * i, 512)])
            return [
                add_near(
                    i, k, acc[:, lanes(512 * i + 256 * k, 256)] + above[:, 256 * k : 256 * (k + 1)]
                ).astype(BF)
                for k in range(2)
            ]

        def keep_out(i, got):
            for k in range(2):
                out[:, lanes(512 * i + 256 * k, 256)] = got[k]

        batched(16, REST, rest, keep_out)

    @pl.when(jnp.logical_not(upper_first))
    def _():
        def rest(i):
            return [add_near(i, k, acc[:, lanes(512 * i + 256 * k, 256)]) for k in range(2)]

        batched(16, REST, rest, keep_rest)
        gone_p.wait_recv()
        parent = pv[...][:, :64]

        def finish(i):
            part = lanes(512 * i, 512)
            return (acc[:, part] + nn(parent, qv[:, part])).astype(BF)

        def keep_finish(i, got):
            out[:, lanes(512 * i, 512)] = got

        batched(16, FINISH, finish, keep_finish)

    for copies in sent[:-1]:
        leave(copies)
    pl.when((d < 127) & jnp.logical_not(last15))(sent[-1][0].wait_send)
    pl.when(d > 0)(sent[-1][1].wait_send)
    pl.when(last15)(to_relay.wait_send)
    pl.when(relay3)(from_relay.wait_send)
    for copies in moved:
        leave(copies)

    @pl.when(inner)
    def _():
        for copy in [gone_x[0]] + gone_z + gone_y + passed + [gone_p]:
            copy.wait_send()

    @pl.when(outer)
    def _():
        gone_x[1].wait_send()
        gone_x[2].wait_send()


def on_device(
    charges,
    column_basis,
    row_basis,
    local_up,
    local_down,
    local_far,
    local_coupling,
    upper_up,
    upper_down,
    upper_far,
    upper_coupling,
    near_source,
    near_block,
):
    dma = pltpu.SemaphoreType.DMA
    vmem = pltpu.VMEM
    anywhere = pl.BlockSpec(memory_space=pl.ANY)
    return pl.pallas_call(
        kernel,
        out_shape=pltpu.VMEM((RHS, COLS), BF),
        in_specs=[anywhere] * 13,
        out_specs=pl.BlockSpec(memory_space=vmem),
        scratch_shapes=[
            vmem((RHS, COLS), BF),
            vmem((2, RHS, COLS), BF),
            vmem((4 * LEAVES, RHS, LEAF), BF),
            vmem((LEAVES, RANK, LEAF), BF),
            vmem((LEAVES, RANK, LEAF), BF),
            vmem((63, RANK, RANK), BF),
            vmem((63, RANK, RANK), BF),
            vmem((64, 8, RANK, RANK), BF),
            vmem((14, RANK, RANK), BF),
            vmem((3, RANK, RANK), BF),
            vmem((4, 8, RANK, RANK), BF),
            vmem((LEAVES, 3, LEAF, LEAF), BF),
            vmem((256, RHS, 128), BF),
            vmem((4, RHS, 128), BF),
            vmem((4, 2, RHS, 128), BF),
            vmem((8, 8, RHS, 128), BF),
            vmem((RHS, 128), BF),
            vmem((RHS, COLS), F32),
            vmem((32, RHS, 128), F32),
            vmem((32, RHS, 128), BF),
            vmem((32, RANK, 128), BF),
            vmem((RANK, COLS), BF),
            vmem((8, 63), jnp.int32),
            vmem((8, 64), jnp.int32),
            pltpu.SMEM((8, 64), jnp.int32),
            pltpu.SMEM((8, 15), jnp.int32),
            pltpu.SMEM((3, LEAVES), jnp.int32),
            dma((40,)),
            dma((len(XPARTS), 2)),
            dma((len(XPARTS), 2)),
            dma((2, 2)),
            dma((2, 2)),
            dma((3,)),
            dma((3,)),
            dma((3,)),
            dma((3,)),
            dma((7,)),
            dma((7,)),
            dma,
            dma,
            pltpu.SemaphoreType.REGULAR,
            vmem((RHS, XPARTS[-1][1]), BF),
            dma((2,)),
            dma,
        ],
        compiler_params=pltpu.CompilerParams(
            collective_id=0, has_side_effects=True, vmem_limit_bytes=60 * 2**20
        ),
        name="h2_product",
    )(
        charges,
        column_basis,
        row_basis,
        local_up,
        local_down,
        local_far.T,
        local_coupling,
        upper_up,
        upper_down,
        upper_far.T,
        upper_coupling,
        near_source.T,
        near_block,
    )


def solution(mesh):
    both = ("grp", "sub")
    in_specs = (
        P(None, both),
        P(both, None, None),
        P(both, None, None),
        P(both, None, None),
        P(both, None, None),
        P(both, None),
        P(both, None, None, None),
        P("grp", None, None),
        P("grp", None, None),
        P("grp", None),
        P("grp", None, None, None),
        P(both, None),
        P(both, None, None, None),
    )
    return jax.shard_map(
        on_device, mesh=mesh, in_specs=in_specs, out_specs=P(None, both), check_vma=False
    )
```

```python
import functools

import jax
import jax.numpy as jnp
from jax import lax
from jax.experimental import pallas as pl
from jax.experimental.pallas import tpu as pltpu
from jax.sharding import PartitionSpec as P

MESH = pl.DeviceIdType.MESH
BF = jnp.bfloat16
F32 = jnp.float32
RHS = 32
LEAVES = 32
LEAF = 256
RANK = 64
LEVELS = 5
COLS = LEAVES * LEAF
XPARTS = ((0, 1024), (1024, 1024), (2048, 2048), (4096, 2560), (6656, 1536))
XFIRST = 2
OWN, REACH, TURN, FAR, REST, FINISH = 4, 16, 96, 16, 16, 16


def nt(a, b):
    return lax.dot_general(a, b, (((1,), (1,)), ((), ())), preferred_element_type=F32)


def nn(a, b):
    return lax.dot_general(a, b, (((1,), (0,)), ((), ())), preferred_element_type=F32)


def lanes(start, size):
    return pl.ds(pl.multiple_of(start, 128), size)


def loop(count, body, unroll):
    def step(i, carry):
        body(i)
        return carry

    lax.fori_loop(0, count, step, 0, unroll=min(unroll, count))


def batched(count, width, compute, store):
    width = min(width, count)

    def body(b):
        got = [compute(width * b + j) for j in range(width)]
        for j in range(width):
            store(width * b + j, got[j])

    loop(count // width, body, 1)


def row_of(height):
    return 64 - 2 * (LEAVES >> height)


def kernel(
    charges,
    column_basis,
    row_basis,
    local_up,
    local_down,
    local_far,
    local_coupling,
    upper_up,
    upper_down,
    upper_far,
    upper_coupling,
    near_source,
    near_block,
    out,
    cx,
    xin,
    xw,
    cbv,
    rbv,
    upv,
    dnv,
    cpv,
    uuv,
    udv,
    ucv,
    nbv,
    mv,
    rx,
    rz,
    rg,
    pv,
    acc,
    far,
    dloc,
    path,
    qv,
    far_raw,
    far_row,
    far_at,
    ufar_at,
    near_at,
    lsem,
    xsend,
    xrecv,
    msend,
    mrecv,
    rxsend,
    rxrecv,
    rzsend,
    rzrecv,
    rgsend,
    rgrecv,
    psend,
    precv,
    hello,
    hop,
    hsend,
    hrecv,
):
    g = lax.axis_index("grp")
    s = lax.axis_index("sub")
    d = g * 16 + s
    z = s // 4
    x = s % 4

    def place(e):
        return (e // 16, e % 16)

    sides = ((d < 127, place((d + 1) % 128)), (d > 0, place((d + 127) % 128)))
    inner = (x == 1) | (x == 2)
    outer = jnp.logical_not(inner)
    y, core = g // 2, g % 2
    middle = [(g, z * 4 + 1), (g, z * 4 + 2)]
    other = (g, z * 4 + 3 - x)
    helped = (g, z * 4 + 3 * (x // 2))
    by_z = [(g, ((z + k) % 4) * 4 + x) for k in range(1, 4)]
    by_y = [(((y + k) % 4) * 2 + core, s) for k in range(1, 4)]
    twin = (2 * y + 1 - core, s)

    first0 = (s == 0) & (g > 0)
    last15 = (s == 15) & (g < 7)
    relay3 = (s == 3) & (g < 7)
    before15 = (z == 3) & (g < 7) & inner
    later = first0 | last15

    barrier = pltpu.get_barrier_semaphore()

    def greet(peer):
        pl.semaphore_signal(barrier, inc=1, device_id=peer, device_id_type=MESH)

    pl.when((d < 127) & jnp.logical_not(last15 | before15 & (x == 2)))(functools.partial(greet, sides[0][1]))
    pl.when(d > 0)(functools.partial(greet, sides[1][1]))
    pl.when(first0)(functools.partial(greet, ((g + 7) % 8, 3)))
    pl.when(relay3)(functools.partial(greet, (g, 15)))

    @pl.when(inner)
    def _():
        for peer in [other, (g, z * 4)] + by_z + by_y + [twin]:
            greet(peer)
        pl.when(jnp.logical_not(before15))(functools.partial(greet, (g, z * 4 + 3)))

    @pl.when(outer)
    def _():
        for peer in middle:
            greet(peer)

    loads = []

    def load(src, dst):
        copy = pltpu.make_async_copy(src, dst, lsem.at[len(loads)])
        copy.start()
        loads.append(copy)
        return copy

    get_x = [load(charges.at[:, pl.ds(4096 * k, 4096)], cx.at[:, pl.ds(4096 * k, 4096)]) for k in range(2)]
    get_cb = [load(column_basis.at[pl.ds(16 * k, 16)], cbv.at[pl.ds(16 * k, 16)]) for k in range(2)]
    get_up = load(local_up, upv)
    get_uu = load(upper_up, uuv)
    get_at = [load(local_far, far_raw), load(upper_far, ufar_at), load(near_source, near_at)]

    @pl.when(outer)
    def _():
        count = 2 + (d < 127).astype(jnp.int32) + ((d > 0) & (s > 0)).astype(jnp.int32)
        pl.semaphore_wait(barrier, jnp.where(last15, 2, count + relay3.astype(jnp.int32)))
        pl.when(last15)(lambda: pl.semaphore_signal(hello, inc=1, device_id=sides[0][1], device_id_type=MESH))

    def remote(src, dst, ssem, rsem, peer):
        return pltpu.make_async_remote_copy(
            src_ref=src, dst_ref=dst, send_sem=ssem, recv_sem=rsem, device_id=peer, device_id_type=MESH
        )

    def send(src, dst, ssem, rsem, peer):
        copy = remote(src, dst, ssem, rsem, peer)
        copy.start()
        return copy

    def beside(src, dst, ssem, rsem):
        return [remote(src, dst(2 * k), ssem.at[k], rsem.at[k], peer) for k, (_, peer) in enumerate(sides)]

    def start(batches, late=False):
        for k, (there, _) in enumerate(sides):
            if late:
                go = later if k else False
            else:
                go = there & jnp.logical_not(later) if k else there

            if go is not False:

                @pl.when(go)
                def _():
                    for copies in batches:
                        copies[k].start()

    def arrive(copies):
        for (there, _), copy in zip((sides[1], sides[0]), copies):
            pl.when(there)(copy.wait_recv)

    def leave(copies):
        for (there, _), copy in zip(sides, copies):
            pl.when(there)(copy.wait_send)

    def charges_part(k):
        start, size = XPARTS[k]
        part = pl.ds(start, size)
        return beside(
            charges.at[:, part],
            lambda side: xin.at[side // 2, :, part],
            xsend.at[k],
            xrecv.at[k],
        )

    sent = [charges_part(k) for k in range(len(XPARTS))]
    part = pl.ds(*XPARTS[-1])
    to_relay = remote(charges.at[:, part], hop, hsend.at[0], hrecv, (g, 3))
    from_relay = remote(hop, xin.at[0, :, part], hsend.at[1], xrecv.at[len(XPARTS) - 1, 0], ((g + 1) % 8, 0))
    pl.when(last15)(to_relay.start)
    pl.when(outer)(lambda: start(sent[:XFIRST]))

    get_ud = [
        load(upper_down.at[16 - (32 >> k) + s // 2**k], udv.at[k - 1]) for k in range(1, 4)
    ]
    get_uc = [
        load(upper_coupling.at[16 - (32 >> k) + s // 2**k], ucv.at[k - 1]) for k in range(1, 5)
    ]

    low = lax.broadcasted_iota(jnp.int32, (RHS, 128), 1) < 64

    for k in range(2):
        get_x[k].wait()
        get_cb[k].wait()

        def leaf_moments(i):
            at = 8 * k + i
            one, two = cx[:, lanes(512 * at, 256)], cx[:, lanes(512 * at + 256, 256)]
            both = nt(jnp.concatenate([one, two], axis=0), cbv[pl.ds(2 * at, 2)].reshape(128, LEAF))
            return one, two, jnp.where(low, both[:RHS], both[RHS:]).astype(BF)

        def keep_moments(i, got):
            at = 8 * k + i
            xw[LEAVES + 2 * at] = got[0]
            xw[LEAVES + 2 * at + 1] = got[1]
            mv[32 + at] = got[2]

        batched(8, 8, leaf_moments, keep_moments)

    @pl.when(inner)
    def _():
        pl.semaphore_wait(barrier, 12)
        pl.when(before15)(lambda: pl.semaphore_signal(hello, inc=1, device_id=(g, 15), device_id_type=MESH))
        start(sent[:1])

    get_up.wait()
    zero = jnp.zeros((RHS, RANK), F32)
    for height in range(1, LEVELS + 1):
        amount = LEAVES >> height
        base, child = row_of(height), row_of(height - 1)

        def lift(j):
            return nn(mv[32 + child // 2 + j], upv[pl.ds(child + 2 * j, 2)].reshape(128, RANK))

        def lift_two(j):
            return jnp.concatenate([lift(2 * j), lift(2 * j + 1)], axis=1).astype(BF)

        def keep_two(j, got):
            mv[32 + base // 2 + j] = got

        if amount == 1:
            root = lift(0)
            mv[63] = jnp.concatenate([root, zero], axis=1).astype(BF)
        else:
            batched(amount // 2, 4, lift_two, keep_two)

    get_dn = load(local_down, dnv)
    get_nb = [load(near_block.at[pl.ds(4 * k, 4)], nbv.at[pl.ds(4 * k, 4)]) for k in range(8)]
    get_cp = [load(local_coupling.at[pl.ds(9 * k, 9)], cpv.at[pl.ds(9 * k, 9)]) for k in range(7)]
    get_rb = load(row_basis, rbv)

    lifted = nn(root.astype(BF), upv[62])
    rx[x] = jnp.where(low == (x < 2), jnp.concatenate([lifted, lifted], axis=1), 0.0).astype(BF)

    gone_x = [remote(rx.at[x], rx.at[x], rxsend.at[0], rxrecv.at[0], other)] + [
        remote(rx.at[x], rx.at[x], rxsend.at[1 + k], rxrecv.at[1 + x // 3], p) for k, p in enumerate(middle)
    ]

    @pl.when(inner)
    def _():
        gone_x[0].start()

    @pl.when(outer)
    def _():
        pl.when(last15)(lambda: pl.semaphore_wait(hello, 2))
        gone_x[1].start()
        gone_x[2].start()

    moved = [
        beside(
            mv.at[pl.ds(32 + 16 * k, 16)],
            lambda side: mv.at[pl.ds(32 * side + 16 * k, 16)],
            msend.at[k],
            mrecv.at[k],
        )
        for k in range(2)
    ]
    start(moved)
    pl.when(inner)(lambda: start(sent[1:XFIRST]))
    start(sent[XFIRST:-2])
    pl.when((d < 127) & jnp.logical_not(relay3))(sent[-2][0].start)
    pl.when((d < 127) & jnp.logical_not(relay3 | last15))(sent[-1][0].start)
    for copies in sent[-2:]:
        pl.when((d > 0) & jnp.logical_not(later))(copies[1].start)

    pl.when(first0)(lambda: pl.semaphore_wait(hello, 1))
    start(sent[:XFIRST] + moved + sent[XFIRST:], late=True)


    get_at[0].wait()
    t = lax.broadcasted_iota(jnp.int32, (8, 63), 1)
    f = lax.broadcasted_iota(jnp.int32, (8, 63), 0)
    amount = jnp.full((8, 63), LEAVES, jnp.int32)
    for height in range(1, LEVELS + 1):
        amount = jnp.where(t < row_of(height), amount, LEAVES >> height)
    q = far_raw[...] - (d - 1) * amount
    window = (q >= amount).astype(jnp.int32) + (q >= 2 * amount).astype(jnp.int32)
    row = 64 - 2 * amount + (q & (amount - 1))
    far_row[...] = jnp.zeros((8, 64), jnp.int32)
    far_row[:, 0:63] = ((row + f) & 1) * 128 + window * 32 + (row >> 1)
    get_far = pltpu.make_async_copy(far_row, far_at, lsem.at[len(loads)])
    get_far.start()

    get_dn.wait()

    def extend_level(height):
        amount = LEAVES >> height
        base, parent = row_of(height), row_of(height + 1)

        def below(above, j):
            return nt(above, dnv[pl.ds(base + 2 * j, 2)].reshape(128, RANK)).astype(BF)

        if amount == 2:
            path[base // 2] = below(dnv[62].T, 0)
        else:

            def extend(j):
                above = path[parent // 2 + j]
                return below(above[:, :64], 2 * j), below(above[:, 64:], 2 * j + 1)

            def keep(j, got):
                path[base // 2 + 2 * j] = got[0]
                path[base // 2 + 2 * j + 1] = got[1]

            batched(amount // 4, 4, extend, keep)

    for height in range(LEVELS - 1, -1, -1):
        extend_level(height)

    get_uu.wait()
    gone_z = [remote(rz.at[z], rz.at[z], rzsend.at[k], rzrecv.at[k], p) for k, p in enumerate(by_z)]

    @pl.when(inner)
    def _():
        for k in range(3):
            remote(rx.at[k], rx.at[k], rxsend.at[k], rxrecv.at[k], other).wait_recv()
        first = (
            (rx[0].astype(F32) + rx[1].astype(F32)) + (rx[2].astype(F32) + rx[3].astype(F32))
        ).astype(BF)
        rz[z, 0] = first
        second = nn(first, uuv[pl.ds(2 * z, 2)].reshape(128, RANK))
        rz[z, 1] = jnp.where(low == (z % 2 == 0), jnp.concatenate([second, second], axis=1), 0.0).astype(BF)
        for copy in gone_z:
            copy.start()

    def near_own(i):
        return nt(xw[LEAVES + i], nbv[i, 0])

    def keep_own(i, got):
        acc[:, lanes(256 * i, 256)] = got

    for k in range(4):
        get_nb[k].wait()
        batched(4, OWN, lambda i: near_own(4 * k + i), lambda i, got: keep_own(4 * k + i, got))

    gone_y = [remote(rg.at[g], rg.at[g], rgsend.at[k], rgrecv.at[k], p) for k, p in enumerate(by_y + [twin])]

    @pl.when(inner)
    def _():
        for copy in gone_z:
            copy.wait_recv()
        for k in range(4):
            rg[g, k] = rz[k, 0]
        thirds = []
        for k in range(2):
            pair = (rz[2 * k, 1].astype(F32) + rz[2 * k + 1, 1].astype(F32)).astype(BF)
            rg[g, 4 + k] = pair
            thirds.append(nn(pair, uuv[8 + 2 * k : 10 + 2 * k].reshape(128, RANK)))
        third = jnp.concatenate(thirds, axis=1).astype(BF)
        rg[g, 6] = third
        top = nn(third, uuv[12:14].reshape(128, RANK))
        rg[g, 7] = jnp.concatenate([top, zero], axis=1).astype(BF)
        for copy in gone_y:
            copy.start()

    for k in range(4, 8):
        get_nb[k].wait()
        batched(4, OWN, lambda i: near_own(4 * k + i), lambda i, got: keep_own(4 * k + i, got))

    get_rb.wait()

    def reach(i):
        pair = path[i]
        return nn(pair[:, :64], rbv[2 * i]).astype(BF), nn(pair[:, 64:], rbv[2 * i + 1]).astype(BF)

    def keep_reach(i, got):
        qv[:, lanes(512 * i, 256)] = got[0]
        qv[:, lanes(512 * i + 256, 256)] = got[1]

    batched(16, REACH, reach, keep_reach)

    @pl.when(relay3)
    def _():
        to_relay.wait_recv()
        from_relay.start()
        sent[-2][0].start()
        sent[-1][0].start()

    for copy in get_ud:
        copy.wait()
    down1 = udv[0]
    down2 = nn(down1, udv[1]).astype(BF)
    down3 = nn(down2, udv[2]).astype(BF)

    for copies in moved:
        arrive(copies)

    def turn(i):
        pair = mv[i]
        return jnp.concatenate([pair[:, 64:], pair[:, :64]], axis=1)

    def keep_turn(i, got):
        mv[128 + i] = got

    batched(96, TURN, turn, keep_turn)
    get_far.wait()
    for copy in get_cp:
        copy.wait()

    def couple(t):
        total = None
        for q in range(2):
            moments = jnp.concatenate(
                [
                    jnp.where(low, mv[far_at[4 * q + 2 * j, t]], mv[far_at[4 * q + 2 * j + 1, t]])
                    for j in range(2)
                ],
                axis=1,
            )
            blocks = jnp.concatenate([cpv[t, 4 * q + j] for j in range(4)], axis=1)
            term = nt(moments, blocks)
            total = term if total is None else total + term
        return total

    def couple_two(j):
        return jnp.concatenate([couple(2 * j), couple(2 * j + 1)], axis=1)

    def keep_couple(j, got):
        far[j] = got

    batched(32, FAR, couple_two, keep_couple)

    dloc[31] = far[31].astype(BF)
    for height in range(LEVELS - 1, -1, -1):
        amount = LEAVES >> height
        base, parent = row_of(height), row_of(height + 1)

        def below(above, j):
            pair = dnv[pl.ds(base + 2 * j, 2)].reshape(128, RANK)
            return (far[base // 2 + j] + nt(above, pair)).astype(BF)

        if amount == 2:
            dloc[base // 2] = below(dloc[31][:, :64], 0)
        else:

            def descend(j):
                above = dloc[parent // 2 + j]
                return below(above[:, :64], 2 * j), below(above[:, 64:], 2 * j + 1)

            def keep_descend(j, got):
                dloc[base // 2 + 2 * j] = got[0]
                dloc[base // 2 + 2 * j + 1] = got[1]

            batched(amount // 4, 4, descend, keep_descend)

    def local(i):
        pair = dloc[i]
        return [
            acc[:, lanes(512 * i + 256 * k, 256)] + nn(pair[:, 64 * k : 64 * (k + 1)], rbv[2 * i + k])
            for k in range(2)
        ]

    def keep_rest(i, got):
        for k in range(2):
            acc[:, lanes(512 * i + 256 * k, 256)] = got[k]

    batched(16, 8, local, keep_rest)

    get_at[1].wait()
    for copy in get_uc:
        copy.wait()
    passed = []
    for k in range(3):
        from_y = ((y + 3 - k) % 4) * 2 + core
        passed.append(remote(rg.at[from_y], rg.at[from_y], rgsend.at[4 + k], rgrecv.at[4 + k], twin))
    gone_p = remote(pv, pv, psend, precv, helped)

    @pl.when(inner)
    def _():
        for k in (0, 2, 1):
            gone_y[k].wait_recv()
            passed[k].start()
        gone_y[3].wait_recv()
        for copy in passed:
            copy.wait_recv()
        terms = []
        for k in range(1, 5):
            amount = 16 >> k
            row = 16 - 2 * amount + s // 2**k

            def pick(f):
                p = ufar_at[f, row]
                group, j = p >> (4 - k), p & (amount - 1)
                pair = rg[group, (0, 4, 6, 7)[k - 1] + (j >> 1)]
                pair = pair.astype(F32)
                turned = jnp.concatenate([pair[:, 64:], pair[:, :64]], axis=1)
                keep = (1 - ((j + f) & 1)).astype(F32)
                return pair * keep + turned * (1.0 - keep)

            total = None
            for q in range(2):
                moments = jnp.concatenate(
                    [jnp.where(low, pick(4 * q + 2 * j), pick(4 * q + 2 * j + 1)) for j in range(2)], axis=1
                ).astype(BF)
                blocks = jnp.concatenate([ucv[k - 1, 4 * q + j] for j in range(4)], axis=1)
                term = nt(moments, blocks)
                total = term if total is None else total + term
            terms.append(total)
        parent = (
            terms[0]
            + nt(terms[1].astype(BF), down1)
            + nt(terms[2].astype(BF), down2)
            + nt(terms[3].astype(BF), down3)
        ).astype(BF)
        pv[...] = jnp.concatenate([parent, parent], axis=1)
        gone_p.start()

    get_at[2].wait()
    for copies, (start, size) in zip(sent, XPARTS):
        arrive(copies)

        def window(i):
            part = lanes(start + LEAF * i, LEAF)
            return xin[0, :, part], xin[1, :, part]

        def keep_window(i, got):
            xw[start // LEAF + i] = got[0]
            xw[2 * LEAVES + start // LEAF + i] = got[1]

        batched(size // LEAF, 2, window, keep_window)

    def add_near(i, k, total):
        leaf = 2 * i + k
        for n in (1, 2):
            q = (near_at[n, leaf] - (d - 1) * LEAVES) & 127
            total = total + nt(xw[q], nbv[leaf, n])
        return total

    upper_first = inner | last15
    pl.when(last15)(gone_p.wait_recv)

    @pl.when(upper_first)
    def _():
        parent = pv[...][:, :64]

        def rest(i):
            above = nn(parent, qv[:, lanes(512 * i, 512)])
            return [
                add_near(
                    i, k, acc[:, lanes(512 * i + 256 * k, 256)] + above[:, 256 * k : 256 * (k + 1)]
                ).astype(BF)
                for k in range(2)
            ]

        def keep_out(i, got):
            for k in range(2):
                out[:, lanes(512 * i + 256 * k, 256)] = got[k]

        batched(16, REST, rest, keep_out)

    @pl.when(jnp.logical_not(upper_first))
    def _():
        def rest(i):
            return [add_near(i, k, acc[:, lanes(512 * i + 256 * k, 256)]) for k in range(2)]

        batched(16, REST, rest, keep_rest)
        gone_p.wait_recv()
        parent = pv[...][:, :64]

        def finish(i):
            part = lanes(512 * i, 512)
            return (acc[:, part] + nn(parent, qv[:, part])).astype(BF)

        def keep_finish(i, got):
            out[:, lanes(512 * i, 512)] = got

        batched(16, FINISH, finish, keep_finish)

    for copies in sent[:-1]:
        leave(copies)
    pl.when((d < 127) & jnp.logical_not(last15))(sent[-1][0].wait_send)
    pl.when(d > 0)(sent[-1][1].wait_send)
    pl.when(last15)(to_relay.wait_send)
    pl.when(relay3)(from_relay.wait_send)
    for copies in moved:
        leave(copies)

    @pl.when(inner)
    def _():
        for copy in [gone_x[0]] + gone_z + gone_y + passed + [gone_p]:
            copy.wait_send()

    @pl.when(outer)
    def _():
        gone_x[1].wait_send()
        gone_x[2].wait_send()


def on_device(
    charges,
    column_basis,
    row_basis,
    local_up,
    local_down,
    local_far,
    local_coupling,
    upper_up,
    upper_down,
    upper_far,
    upper_coupling,
    near_source,
    near_block,
):
    dma = pltpu.SemaphoreType.DMA
    vmem = pltpu.VMEM
    anywhere = pl.BlockSpec(memory_space=pl.ANY)
    return pl.pallas_call(
        kernel,
        out_shape=pltpu.VMEM((RHS, COLS), BF),
        in_specs=[anywhere] * 13,
        out_specs=pl.BlockSpec(memory_space=vmem),
        scratch_shapes=[
            vmem((RHS, COLS), BF),
            vmem((2, RHS, COLS), BF),
            vmem((4 * LEAVES, RHS, LEAF), BF),
            vmem((LEAVES, RANK, LEAF), BF),
            vmem((LEAVES, RANK, LEAF), BF),
            vmem((63, RANK, RANK), BF),
            vmem((63, RANK, RANK), BF),
            vmem((64, 8, RANK, RANK), BF),
            vmem((14, RANK, RANK), BF),
            vmem((3, RANK, RANK), BF),
            vmem((4, 8, RANK, RANK), BF),
            vmem((LEAVES, 3, LEAF, LEAF), BF),
            vmem((256, RHS, 128), BF),
            vmem((4, RHS, 128), BF),
            vmem((4, 2, RHS, 128), BF),
            vmem((8, 8, RHS, 128), BF),
            vmem((RHS, 128), BF),
            vmem((RHS, COLS), F32),
            vmem((32, RHS, 128), F32),
            vmem((32, RHS, 128), BF),
            vmem((32, RANK, 128), BF),
            vmem((RANK, COLS), BF),
            vmem((8, 63), jnp.int32),
            vmem((8, 64), jnp.int32),
            pltpu.SMEM((8, 64), jnp.int32),
            pltpu.SMEM((8, 15), jnp.int32),
            pltpu.SMEM((3, LEAVES), jnp.int32),
            dma((40,)),
            dma((len(XPARTS), 2)),
            dma((len(XPARTS), 2)),
            dma((2, 2)),
            dma((2, 2)),
            dma((3,)),
            dma((3,)),
            dma((3,)),
            dma((3,)),
            dma((7,)),
            dma((7,)),
            dma,
            dma,
            pltpu.SemaphoreType.REGULAR,
            vmem((RHS, XPARTS[-1][1]), BF),
            dma((2,)),
            dma,
        ],
        compiler_params=pltpu.CompilerParams(
            collective_id=0, has_side_effects=True, vmem_limit_bytes=60 * 2**20
        ),
        name="h2_product",
    )(
        charges,
        column_basis,
        row_basis,
        local_up,
        local_down,
        local_far.T,
        local_coupling,
        upper_up,
        upper_down,
        upper_far.T,
        upper_coupling,
        near_source.T,
        near_block,
    )


def solution(mesh):
    both = ("grp", "sub")
    in_specs = (
        P(None, both),
        P(both, None, None),
        P(both, None, None),
        P(both, None, None),
        P(both, None, None),
        P(both, None),
        P(both, None, None, None),
        P("grp", None, None),
        P("grp", None, None),
        P("grp", None),
        P("grp", None, None, None),
        P(both, None),
        P(both, None, None, None),
    )
    return jax.shard_map(
        on_device, mesh=mesh, in_specs=in_specs, out_specs=P(None, both), check_vma=False
    )
```
